32 devices in a mesh: ka: 4 (over x, core), brick: 8 (over z, y).
Axes of the slice: x: 2, y: 2, z: 4, core: 2. Of those that a mesh axis runs over, the one named last changes fastest.
Arguments:
- spinors: bfloat16 [32, 4, 32, 36864], P('ka', None, 'brick'), may hold values from -6 to 6
- kpt_mult: int32 [32], P('ka'), may hold values from 1 to 4
- occupied: int32 [32], P('ka'), may hold values 0 or 1
- core_density: float32 [32, 36864], P('brick'), may hold values from 0.05 to 1
- local_potential: float32 [32, 36864], P('brick'), may hold values from -6 to 6
Outputs:
- applied: bfloat16 [32, 4, 32, 36864], P('ka', None, 'brick')
The draws below stay inside these ranges and needn't reach their ends.
All inputs are finite; a program needn't handle non-finite values. No bound on the sum of `occupied` on one device may be relied on, other than what follows from the above.
Results may differ from the reference program's by a relative error of at most 0.005.
Values may be sent and summed in bfloat16 or wider, within the bound.
No kernel may reach another device: no remote copies, remote signals or barrier semaphores. Data moves between devices by JAX's collectives and lax.ppermute only.
A program may use at most 128 MiB of HBM per device.

```python
import math
import jax
import jax.numpy as jnp
from jax import lax

NY = 192
CELLS = 36864
B_TOTAL = 32
NZ = 32


def plant(values, key, least, high):
    longest = values.shape.index(max(values.shape))
    spots = []
    for shift in (0, 1):
        where = [jax.random.randint(jax.random.fold_in(key, axis), (), 0, length) for axis, length in enumerate(values.shape)]
        where[longest] = (where[longest] + shift) % values.shape[longest]
        spots.append(tuple(where))
    return values.at[spots[0]].set(least).at[spots[1]].set(high)


def level_of(rng, extent, pieces, least, high):
    gain, own = 1.0, jax.random.fold_in(rng, 6)
    for position, shards_of in pieces:
        draws = jnp.exp(jax.random.uniform(jax.random.fold_in(own, position), (shards_of,), jnp.float32, least / len(pieces), high / len(pieces)))
        gain = gain * jnp.repeat(draws, extent[position] // shards_of).reshape([-1 if axis == position else 1 for axis in range(len(extent))])
    return gain


def scatter_about(own_key, dims, spread, bound, pieces=(), held_as=jnp.bfloat16):
    level = level_of(own_key, dims, pieces, -0.22, 0.18) if pieces else 1.0
    values = jax.random.normal(own_key, dims, jnp.float32) * spread * level
    return jnp.minimum(jnp.maximum(values, -bound), bound).astype(held_as)


def setup_inputs(seed: int = 0) -> dict:
    keys = jax.random.split(jax.random.key(seed), 6)
    spinors = scatter_about(keys[0], (B_TOTAL, 4, NZ, CELLS), 1.0, 6.0, ((0, 4), (2, 8)))
    kpt_mult = plant(jax.random.randint(keys[1], (B_TOTAL,), 1, 5), jax.random.fold_in(keys[1], 1), 1, 4).astype(jnp.int32)
    occupied = plant((jax.random.randint(keys[2], (B_TOTAL,), 0, 4) < 3).astype(jnp.int32), jax.random.fold_in(keys[2], 1), 0, 1)
    core_density = jnp.clip(jnp.exp(math.log(1.0) - 2.9957323 * jax.random.uniform(keys[3], (NZ, CELLS), jnp.float32) ** level_of(keys[3], (NZ, CELLS), ((0, 8),), -0.2, 0.2)), 0.05, 1.0)
    local_potential = scatter_about(keys[4], (NZ, CELLS), 1.0, 6.0, ((0, 8),), jnp.float32)
    return {"spinors": spinors, "kpt_mult": kpt_mult, "occupied": occupied, "core_density": core_density, "local_potential": local_potential}


FLOOR_FRACTION = 0.05

def density_terms(band, weight):
    values = band.astype(jnp.float32)
    up_real, up_imag, down_real, down_imag = (values[0], values[1], values[2], values[3])
    up_square = up_real * up_real + up_imag * up_imag
    down_square = down_real * down_real + down_imag * down_imag
    return weight * jnp.stack([up_square + down_square, 2.0 * (up_real * down_real + up_imag * down_imag), 2.0 * (up_real * down_imag - up_imag * down_real), up_square - down_square])

def accumulate_density(spinors, weights):
    zeros = jnp.zeros((4,) + spinors.shape[2:], jnp.float32)

    def step_band(carry, item):
        band, weight = item
        return (carry + density_terms(band, weight), None)
    result, unused = lax.scan(step_band, zeros, (spinors, weights))
    return result

def frame_potential(density, core):
    electrons = density[0] + core
    magnitude = jnp.sqrt(density[1] * density[1] + density[2] * density[2] + density[3] * density[3])
    upper = -jnp.cbrt(3.0 / math.pi * (electrons + magnitude))
    lower = -jnp.cbrt(3.0 / math.pi * (electrons - magnitude))
    factor = 0.5 * (upper - lower) / jnp.maximum(magnitude, FLOOR_FRACTION * electrons)
    return jnp.stack([0.5 * (upper + lower), factor * density[1], factor * density[2], factor * density[3]])

def plane_neighbours(center, row_length):
    column = jnp.arange(center.shape[-1], dtype=jnp.int32) % row_length
    forward = jnp.where(column == row_length - 1, jnp.roll(center, row_length - 1, -1), jnp.roll(center, -1, -1))
    backward = jnp.where(column == 0, jnp.roll(center, 1 - row_length, -1), jnp.roll(center, 1, -1))
    across = jnp.roll(center, row_length, -1) + jnp.roll(center, -row_length, -1)
    return forward + backward + across

def apply_hamiltonian(padded_band, potential):
    values = padded_band.astype(jnp.float32)
    center = values[:, 1:-1]
    neighbours = values[:, 2:] + values[:, :-2]
    neighbours = neighbours + plane_neighbours(center, NY)
    kinetic = -0.5 * (neighbours - 6.0 * center)
    diagonal_up = potential[0] + potential[3]
    diagonal_down = potential[0] - potential[3]
    field_x, field_y = (potential[1], potential[2])
    up_real, up_imag, down_real, down_imag = (center[0], center[1], center[2], center[3])
    mixed = jnp.stack([diagonal_up * up_real + field_x * down_real + field_y * down_imag, diagonal_up * up_imag + field_x * down_imag - field_y * down_real, field_x * up_real - field_y * up_imag + diagonal_down * down_real, field_x * up_imag + field_y * up_real + diagonal_down * down_imag])
    return (kinetic + mixed).astype(jnp.bfloat16)

def reference(spinors, kpt_mult, occupied, core_density, local_potential):
    weights = (kpt_mult * occupied).astype(jnp.float32) / (2.0 * B_TOTAL)
    density = accumulate_density(spinors, weights)
    potential = frame_potential(density, core_density)
    potential = jnp.concatenate([(potential[0] + local_potential)[None], potential[1:]], axis=0)

    def one_band(band):
        padded = jnp.pad(band, ((0, 0), (1, 1), (0, 0)))
        return apply_hamiltonian(padded, potential)
    return lax.map(one_band, spinors)
```

```python
import functools
import math

import jax
import jax.numpy as jnp
from jax import lax
from jax.experimental import pallas as pl
from jax.experimental.pallas import tpu as pltpu
from jax.sharding import PartitionSpec as P

NY = 192
LANES = 128
SUB = 8
FLOOR_FRACTION = 0.05
VMEM_LIMIT = 40 * 1024 * 1024


def rows_view(x):
    lead, planes, cells = x.shape[:-2], x.shape[-2], x.shape[-1]
    tiles = cells // LANES
    n = len(lead)
    x = x.reshape(lead + (planes, tiles, LANES))
    x = x.transpose(tuple(range(n)) + (n + 1, n, n + 2))
    return x.reshape(lead + (tiles * planes, LANES))


def planes_view(x, planes):
    lead, rows = x.shape[:-2], x.shape[-2]
    tiles = rows // planes
    n = len(lead)
    x = x.reshape(lead + (tiles, planes, LANES))
    x = x.transpose(tuple(range(n)) + (n + 1, n, n + 2))
    return x.reshape(lead + (planes, tiles * LANES))


def edges_body(planes, tiles, x_ref, first_ref, last_ref, wide):
    for c in range(4):
        wide[...] = x_ref[0, c].astype(jnp.float32)
        first_ref[0, c] = wide[pl.ds(0, tiles, stride=planes), :].astype(jnp.bfloat16)
        last_ref[0, c] = wide[pl.ds(planes - 1, tiles, stride=planes), :].astype(jnp.bfloat16)


def edges(x, planes, start, count):
    rows = x.shape[2]
    tiles = rows // planes
    shape = jax.ShapeDtypeStruct((count, 4, tiles, LANES), jnp.bfloat16)
    block = pl.BlockSpec((1, 4, tiles, LANES), lambda b: (b, 0, 0, 0))
    return pl.pallas_call(
        functools.partial(edges_body, planes, tiles),
        grid=(count,),
        in_specs=[pl.BlockSpec((1, 4, rows, LANES), lambda b: (start + b, 0, 0, 0))],
        out_specs=[block, block],
        out_shape=[shape, shape],
        scratch_shapes=[pltpu.VMEM((rows, LANES), jnp.float32)],
        compiler_params=pltpu.CompilerParams(vmem_limit_bytes=VMEM_LIMIT),
        cost_estimate=pl.CostEstimate(
            flops=count * 4 * rows * LANES, bytes_accessed=count * 4 * rows * LANES * 3, transcendentals=0
        ),
        name="edges",
    )(x)


def density_body(bands, rows, scale, mult_ref, occ_ref, x_ref, out_ref):
    weights = [(mult_ref[b] * occ_ref[b]).astype(jnp.float32) * scale for b in range(bands)]

    def step(i, unused):
        at = pl.ds(pl.multiple_of(i * 16, 16), 16)
        up = down = real = imag = None
        for b in range(bands):
            ur, ui, dr, di = (x_ref[b, c, at, :].astype(jnp.float32) for c in range(4))
            wur, wui = weights[b] * ur, weights[b] * ui
            wdr, wdi = weights[b] * dr, weights[b] * di
            terms = (
                wur * ur + wui * ui,
                wdr * dr + wdi * di,
                wur * dr + wui * di,
                wur * di - wui * dr,
            )
            if b == 0:
                up, down, real, imag = terms
            else:
                up, down, real, imag = up + terms[0], down + terms[1], real + terms[2], imag + terms[3]
        out_ref[0, at, :] = (up + down).astype(jnp.bfloat16)
        out_ref[1, at, :] = (2.0 * real).astype(jnp.bfloat16)
        out_ref[2, at, :] = (2.0 * imag).astype(jnp.bfloat16)
        out_ref[3, at, :] = (up - down).astype(jnp.bfloat16)
        return unused

    lax.fori_loop(0, rows // 16, step, 0)


def density_of(x, mult, occ, total):
    bands, rows = x.shape[0], x.shape[2]
    steps = 8
    part = rows // steps
    return pl.pallas_call(
        functools.partial(density_body, bands, part, 1.0 / (2.0 * total)),
        grid=(steps,),
        in_specs=[
            pl.BlockSpec(memory_space=pltpu.SMEM),
            pl.BlockSpec(memory_space=pltpu.SMEM),
            pl.BlockSpec((bands, 4, part, LANES), lambda i: (0, 0, i, 0)),
        ],
        out_specs=pl.BlockSpec((4, part, LANES), lambda i: (0, i, 0)),
        out_shape=jax.ShapeDtypeStruct((4, rows, LANES), jnp.bfloat16),
        compiler_params=pltpu.CompilerParams(vmem_limit_bytes=VMEM_LIMIT),
        cost_estimate=pl.CostEstimate(
            flops=bands * 4 * rows * LANES * 6, bytes_accessed=(bands * 2 + 2) * 4 * rows * LANES, transcendentals=0
        ),
        name="density",
    )(mult, occ, x)


def cube_root(x):
    root = jnp.exp(jnp.log(jnp.abs(x)) * (1.0 / 3.0))
    return jnp.where(x < 0.0, -root, root)


def potential_body(rows, d_ref, core_ref, local_ref, out_ref):
    def step(i, unused):
        at = pl.ds(pl.multiple_of(i * 16, 16), 16)
        d0, d1, d2, d3 = (d_ref[f, at, :].astype(jnp.float32) for f in range(4))
        electrons = d0 + core_ref[at, :]
        magnitude = jnp.sqrt(d1 * d1 + d2 * d2 + d3 * d3)
        upper = -cube_root((3.0 / math.pi) * (electrons + magnitude))
        lower = -cube_root((3.0 / math.pi) * (electrons - magnitude))
        factor = 0.5 * (upper - lower) / jnp.maximum(magnitude, FLOOR_FRACTION * electrons)
        v = 0.5 * (upper + lower) + local_ref[at, :]
        bz = factor * d3
        out_ref[0, at, :] = v + bz + 3.0
        out_ref[1, at, :] = factor * d1
        out_ref[2, at, :] = factor * d2
        out_ref[3, at, :] = v - bz + 3.0
        return unused

    lax.fori_loop(0, rows // 16, step, 0)


def potential_of(density, core, local):
    rows = density.shape[1]
    steps = 8
    part = rows // steps
    return pl.pallas_call(
        functools.partial(potential_body, part),
        grid=(steps,),
        in_specs=[
            pl.BlockSpec((4, part, LANES), lambda i: (0, i, 0)),
            pl.BlockSpec((part, LANES), lambda i: (i, 0)),
            pl.BlockSpec((part, LANES), lambda i: (i, 0)),
        ],
        out_specs=pl.BlockSpec((4, part, LANES), lambda i: (0, i, 0)),
        out_shape=jax.ShapeDtypeStruct((4, rows, LANES), jnp.float32),
        compiler_params=pltpu.CompilerParams(vmem_limit_bytes=VMEM_LIMIT),
        cost_estimate=pl.CostEstimate(
            flops=rows * LANES * 40, bytes_accessed=rows * LANES * 32, transcendentals=rows * LANES * 6
        ),
        name="potential",
    )(density, core, local)


def apply_body(planes, rows, x_ref, pot_ref, below_ref, above_ref, carry_ref, out_ref, wide, ends):
    tiles = rows // planes
    group = SUB // planes
    assert group == 2
    vregs = 3
    step_rows = vregs * SUB

    @pl.when(pl.program_id(0) == 0)
    def _():
        ends[...] = jnp.zeros_like(ends)

    for c in range(4):
        wide[c, pl.ds(SUB, rows), :] = x_ref[0, c].astype(jnp.float32)
        wide[c, pl.ds(0, SUB), :] = wide[c, pl.ds(rows, SUB), :]
        wide[c, pl.ds(rows + SUB, SUB), :] = wide[c, pl.ds(SUB, SUB), :]
        ends[c, pl.ds(0, tiles, stride=planes), :] = below_ref[0, c].astype(jnp.float32)
        ends[c, pl.ds(planes - 1, tiles, stride=planes), :] = above_ref[0, c].astype(jnp.float32)

    shape = (vregs, SUB, LANES)
    vreg = lax.broadcasted_iota(jnp.int32, shape, 0)
    row = lax.broadcasted_iota(jnp.int32, shape, 1)
    lane = lax.broadcasted_iota(jnp.int32, shape, 2)
    kind = (vreg * group + row // planes) % 3
    plane = row % planes
    half = NY // 2 - 32
    low_rows = row < planes
    low_lanes = lane < half
    plus_near = (lane == 0) & (kind != 2)
    plus_far = ((lane == half) & (kind == 1)) | ((lane == 0) & (kind == 2))
    minus_near = (lane == LANES - 1) & (kind != 0)
    minus_far = ((lane == half - 1) & (kind == 1)) | ((lane == LANES - 1) & (kind == 0))
    not_first = plane != 0
    not_last = plane != planes - 1

    def stencil(c, start):
        value = wide[c, pl.ds(start, step_rows + 2 * SUB), :].reshape(vregs + 2, SUB, LANES)
        here = value[1:-1]
        turned = pltpu.roll(value, half, 2)
        swapped = pltpu.roll(value, planes, 1)
        turned_swapped = pltpu.roll(turned, planes, 1)
        after = jnp.where(low_rows, swapped[1:-1], swapped[2:])
        before = jnp.where(low_rows, swapped[:-2], swapped[1:-1])
        turned_after = jnp.where(low_rows, turned_swapped[1:-1], turned_swapped[2:])
        turned_before = jnp.where(low_rows, turned_swapped[:-2], turned_swapped[1:-1])
        across = jnp.where(low_lanes, turned_after + turned[:-2], turned_before + turned[2:])
        plus = jnp.where(plus_far, turned_before, jnp.where(plus_near, after, here))
        minus = jnp.where(minus_far, turned_after, jnp.where(minus_near, before, here))
        along = pltpu.roll(plus, LANES - 1, 2) + pltpu.roll(minus, 1, 2)
        normal = jnp.where(not_first, pltpu.roll(here, 1, 1), 0.0) + jnp.where(
            not_last, pltpu.roll(here, SUB - 1, 1), 0.0
        )
        outside = ends[c, pl.ds(start, step_rows), :].reshape(shape)
        return here, (across + along) + (normal + outside)

    def block(start):
        parts = [stencil(c, start) for c in range(4)]
        (ur, nur), (ui, nui), (dr, ndr), (di, ndi) = parts
        at = pl.ds(start, step_rows)
        diag_up, bx, by, diag_down = (pot_ref[f, at, :].reshape(shape) for f in range(4))
        results = (
            diag_up * ur + bx * dr + by * di - 0.5 * nur,
            diag_up * ui + bx * di - by * dr - 0.5 * nui,
            bx * ur - by * ui + diag_down * dr - 0.5 * ndr,
            bx * ui + by * ur + diag_down * di - 0.5 * ndi,
        )
        return [r.reshape(step_rows, LANES) for r in results]

    def step(i, unused):
        start = pl.multiple_of(i * (2 * step_rows), 2 * SUB)
        low, high = block(start), block(start + step_rows)
        for c in range(4):
            both = jnp.concatenate([low[c], high[c]], axis=0)
            out_ref[0, c, pl.ds(start, 2 * step_rows), :] = both.astype(jnp.bfloat16)
        return unused

    lax.fori_loop(0, rows // (2 * step_rows), step, 0)


def apply_bands(x, potential, below, above, planes, start, carry):
    bands, rows = x.shape[0], x.shape[2]
    count = below.shape[0]
    tiles = rows // planes
    halo = pl.BlockSpec((1, 4, tiles, LANES), lambda b: (b, 0, 0, 0))
    body = functools.partial(apply_body, planes, rows)
    in_specs = [
        pl.BlockSpec((1, 4, rows, LANES), lambda b: (start + b, 0, 0, 0)),
        pl.BlockSpec((4, rows, LANES), lambda b: (0, 0, 0)),
        halo,
        halo,
    ]
    operands = [x, potential, below, above]
    aliases = {}
    if carry is not None:
        in_specs.append(pl.BlockSpec(memory_space=pl.ANY))
        operands.append(carry)
        aliases = {4: 0}
        call = body
    else:

        def call(x_ref, pot_ref, below_ref, above_ref, *rest):
            body(x_ref, pot_ref, below_ref, above_ref, None, *rest)

    return pl.pallas_call(
        call,
        grid=(count,),
        in_specs=in_specs,
        out_specs=pl.BlockSpec((1, 4, rows, LANES), lambda b: (start + b, 0, 0, 0)),
        out_shape=jax.ShapeDtypeStruct(x.shape, jnp.bfloat16),
        input_output_aliases=aliases,
        scratch_shapes=[
            pltpu.VMEM((4, rows + 2 * SUB, LANES), jnp.float32),
            pltpu.VMEM((4, rows, LANES), jnp.float32),
        ],
        compiler_params=pltpu.CompilerParams(vmem_limit_bytes=VMEM_LIMIT),
        cost_estimate=pl.CostEstimate(
            flops=count * 4 * rows * LANES * 30, bytes_accessed=count * 4 * rows * LANES * 5, transcendentals=0
        ),
        name="apply",
    )(*operands)


def shards(spinors, kpt_mult, occupied, core_density, local_potential):
    bands, planes = spinors.shape[0], spinors.shape[2]
    total = bands * lax.axis_size("ka")
    size = lax.axis_size("brick")
    up = [(i, i + 1) for i in range(size - 1)]
    down = [(j, i) for i, j in up]
    x = rows_view(spinors)
    core, local = rows_view(core_density), rows_view(local_potential)
    counts = [bands // 4] * 4 if bands % 4 == 0 else [bands]
    halos, start = [], 0
    for count in counts:
        first, last = edges(x, planes, start, count)
        halos.append((start, lax.ppermute(last, "brick", up), lax.ppermute(first, "brick", down)))
        start += count
    density = density_of(x, kpt_mult, occupied, total)
    potential = potential_of(lax.psum(density, "ka"), core, local)
    out = None
    for start, below, above in halos:
        out = apply_bands(x, potential, below, above, planes, start, out)
    return planes_view(out, planes)


def solution(mesh):
    placed = (P("ka", None, "brick", None), P("ka"), P("ka"), P("brick", None), P("brick", None))
    return jax.shard_map(
        shards, mesh=mesh, in_specs=placed, out_specs=P("ka", None, "brick", None), check_vma=False
    )
```

```python
import functools
import math

import jax
import jax.numpy as jnp
from jax import lax
from jax.experimental import pallas as pl
from jax.experimental.pallas import tpu as pltpu
from jax.sharding import PartitionSpec as P

NY = 192
LANES = 128
SUB = 8
FLOOR_FRACTION = 0.05
VMEM_LIMIT = 56 * 1024 * 1024


def rows_view(x):
    lead, planes, cells = x.shape[:-2], x.shape[-2], x.shape[-1]
    tiles = cells // LANES
    n = len(lead)
    x = x.reshape(lead + (planes, tiles, LANES))
    x = x.transpose(tuple(range(n)) + (n + 1, n, n + 2))
    return x.reshape(lead + (tiles * planes, LANES))


def planes_view(x, planes):
    lead, rows = x.shape[:-2], x.shape[-2]
    tiles = rows // planes
    n = len(lead)
    x = x.reshape(lead + (tiles, planes, LANES))
    x = x.transpose(tuple(range(n)) + (n + 1, n, n + 2))
    return x.reshape(lead + (planes, tiles * LANES))


def even_brick():
    return lax.axis_index("brick") % 2 == 0


def edges_body(planes, tiles, start, count, x_ref, *refs):
    near_ref, far_ref, held, wide, sems = refs[-5:]
    even = even_brick()
    copies = [pltpu.make_async_copy(x_ref.at[start + b], held.at[b], sems.at[b]) for b in range(count)]
    for copy in copies:
        copy.start()
    for b in range(count):
        copies[b].wait()
        for c in range(4):
            wide[...] = held[b, c].astype(jnp.float32)
            first = wide[pl.ds(0, tiles, stride=planes), :]
            last = wide[pl.ds(planes - 1, tiles, stride=planes), :]
            near_ref[b, c] = jnp.where(even, last, first).astype(jnp.bfloat16)
            far_ref[b, c] = jnp.where(even, first, last).astype(jnp.bfloat16)


def edges(x, planes, start, count, after):
    rows = x.shape[2]
    tiles = rows // planes
    shape = jax.ShapeDtypeStruct((count, 4, tiles, LANES), jnp.bfloat16)
    return pl.pallas_call(
        functools.partial(edges_body, planes, tiles, start, count),
        in_specs=[pl.BlockSpec(memory_space=pltpu.HBM)] + [pl.BlockSpec(memory_space=pl.ANY)] * len(after),
        out_shape=[shape, shape],
        scratch_shapes=[
            pltpu.VMEM((count, 4, rows, LANES), jnp.bfloat16),
            pltpu.VMEM((rows, LANES), jnp.float32),
            pltpu.SemaphoreType.DMA((count,)),
        ],
        compiler_params=pltpu.CompilerParams(vmem_limit_bytes=VMEM_LIMIT),
        cost_estimate=pl.CostEstimate(
            flops=count * 4 * rows * LANES, bytes_accessed=count * 4 * rows * LANES * 3, transcendentals=0
        ),
        name="edges",
    )(x, *after)


def density_body(bands, rows, scale, mult_ref, occ_ref, x_ref, after_ref, out_ref):
    weights = [(mult_ref[b] * occ_ref[b]).astype(jnp.float32) * scale for b in range(bands)]

    def step(i, unused):
        at = pl.ds(pl.multiple_of(i * 16, 16), 16)
        up = down = real = imag = None
        for b in range(bands):
            ur, ui, dr, di = (x_ref[b, c, at, :].astype(jnp.float32) for c in range(4))
            wur, wui = weights[b] * ur, weights[b] * ui
            wdr, wdi = weights[b] * dr, weights[b] * di
            terms = (
                wur * ur + wui * ui,
                wdr * dr + wdi * di,
                wur * dr + wui * di,
                wur * di - wui * dr,
            )
            if b == 0:
                up, down, real, imag = terms
            else:
                up, down, real, imag = up + terms[0], down + terms[1], real + terms[2], imag + terms[3]
        out_ref[0, at, :] = (up + down).astype(jnp.bfloat16)
        out_ref[1, at, :] = (2.0 * real).astype(jnp.bfloat16)
        out_ref[2, at, :] = (2.0 * imag).astype(jnp.bfloat16)
        out_ref[3, at, :] = (up - down).astype(jnp.bfloat16)
        return unused

    lax.fori_loop(0, rows // 16, step, 0)


def density_of(x, mult, occ, total, after):
    bands, rows = x.shape[0], x.shape[2]
    steps = 8
    part = rows // steps
    return pl.pallas_call(
        functools.partial(density_body, bands, part, 1.0 / (2.0 * total)),
        grid=(steps,),
        in_specs=[
            pl.BlockSpec(memory_space=pltpu.SMEM),
            pl.BlockSpec(memory_space=pltpu.SMEM),
            pl.BlockSpec((bands, 4, part, LANES), lambda i: (0, 0, i, 0)),
            pl.BlockSpec(memory_space=pl.ANY),
        ],
        out_specs=pl.BlockSpec((4, part, LANES), lambda i: (0, i, 0)),
        out_shape=jax.ShapeDtypeStruct((4, rows, LANES), jnp.bfloat16),
        compiler_params=pltpu.CompilerParams(vmem_limit_bytes=VMEM_LIMIT),
        cost_estimate=pl.CostEstimate(
            flops=bands * 4 * rows * LANES * 6, bytes_accessed=(bands * 2 + 2) * 4 * rows * LANES, transcendentals=0
        ),
        name="density",
    )(mult, occ, x, after)


def cube_root(x):
    root = jnp.exp(jnp.log(jnp.abs(x)) * (1.0 / 3.0))
    return jnp.where(x < 0.0, -root, root)


def potential_body(rows, d_ref, core_ref, local_ref, after_ref, out_ref):
    def step(i, unused):
        at = pl.ds(pl.multiple_of(i * 16, 16), 16)
        d0, d1, d2, d3 = (d_ref[f, at, :].astype(jnp.float32) for f in range(4))
        electrons = d0 + core_ref[at, :]
        magnitude = jnp.sqrt(d1 * d1 + d2 * d2 + d3 * d3)
        upper = -cube_root((3.0 / math.pi) * (electrons + magnitude))
        lower = -cube_root((3.0 / math.pi) * (electrons - magnitude))
        factor = 0.5 * (upper - lower) / jnp.maximum(magnitude, FLOOR_FRACTION * electrons)
        v = 0.5 * (upper + lower) + local_ref[at, :]
        bz = factor * d3
        out_ref[0, at, :] = v + bz + 3.0
        out_ref[1, at, :] = factor * d1
        out_ref[2, at, :] = factor * d2
        out_ref[3, at, :] = v - bz + 3.0
        return unused

    lax.fori_loop(0, rows // 16, step, 0)


def potential_of(density, core, local, after):
    rows = density.shape[1]
    steps = 8
    part = rows // steps
    return pl.pallas_call(
        functools.partial(potential_body, part),
        grid=(steps,),
        in_specs=[
            pl.BlockSpec((4, part, LANES), lambda i: (0, i, 0)),
            pl.BlockSpec((part, LANES), lambda i: (i, 0)),
            pl.BlockSpec((part, LANES), lambda i: (i, 0)),
            pl.BlockSpec(memory_space=pl.ANY),
        ],
        out_specs=pl.BlockSpec((4, part, LANES), lambda i: (0, i, 0)),
        out_shape=jax.ShapeDtypeStruct((4, rows, LANES), jnp.float32),
        compiler_params=pltpu.CompilerParams(vmem_limit_bytes=VMEM_LIMIT),
        cost_estimate=pl.CostEstimate(
            flops=rows * LANES * 40, bytes_accessed=rows * LANES * 32, transcendentals=rows * LANES * 6
        ),
        name="potential",
    )(density, core, local, after)


def apply_body(planes, rows, x_ref, pot_ref, near_ref, far_ref, carry_ref, out_ref, wide, ends, turned, flat):
    triples = 3
    half = 2 * NY - 2 * LANES - LANES // 2
    steps = rows // (planes * triples * SUB)
    stride = planes * triples * steps
    even = even_brick()
    near_slot = jnp.where(even, 1, 0)

    for c in range(4):
        wide[c] = x_ref[0, c].astype(jnp.float32)
        ends[near_slot, c] = near_ref[0, c].astype(jnp.float32)
        ends[1 - near_slot, c] = far_ref[0, c].astype(jnp.float32)

    def at(j, tile, plane):
        return pl.ds(j * (planes * triples) + tile * planes + plane, SUB, stride=stride)

    def turn(j, unused):
        for c in range(4):
            for tile in range(triples):
                for plane in range(planes):
                    turned[c, tile, plane, j + 1] = pltpu.roll(wide[c, at(j, tile, plane), :], half, 1)
        return unused

    lax.fori_loop(0, steps, turn, 0)
    for c in range(4):
        for tile in range(triples):
            for plane in range(planes):
                turned[c, tile, plane, 0] = pltpu.roll(turned[c, tile, plane, steps], 1, 0)
                turned[c, tile, plane, steps + 1] = pltpu.roll(turned[c, tile, plane, 1], SUB - 1, 0)

    lane = lax.broadcasted_iota(jnp.int32, (SUB, LANES), 1)
    low = lane < half
    initial, final = lane == 0, lane == LANES - 1
    inner_initial, inner_final = lane == half, lane == half - 1

    def neighbours(c, plane, j):
        v0, v1, v2 = (wide[c, at(j, tile, plane), :] for tile in range(triples))
        r0, r1, r2 = (turned[c, tile, plane, j + 1] for tile in range(triples))
        after0 = r0 + turned[c, 0, plane, j + 2]
        after1 = r1 + turned[c, 1, plane, j + 2]
        before1 = r1 + turned[c, 1, plane, j]
        before2 = r2 + turned[c, 2, plane, j]
        across = (
            jnp.where(low, before1, before2),
            jnp.where(low, before2, after0),
            jnp.where(low, after0, after1),
        )
        plus = (
            jnp.where(initial, v1, v0),
            jnp.where(inner_initial, r0, jnp.where(initial, v2, v1)),
            jnp.where(initial, r1, v2),
        )
        minus = (
            jnp.where(final, r1, v0),
            jnp.where(inner_final, r2, jnp.where(final, v0, v1)),
            jnp.where(final, v1, v2),
        )
        sums = []
        for tile in range(triples):
            outside = pl.ds(j * triples + tile, SUB, stride=triples * steps)
            below = ends[0, c, outside, :] if plane == 0 else wide[c, at(j, tile, plane - 1), :]
            above = ends[1, c, outside, :] if plane == planes - 1 else wide[c, at(j, tile, plane + 1), :]
            along = pltpu.roll(plus[tile], LANES - 1, 1) + pltpu.roll(minus[tile], 1, 1)
            sums.append((across[tile] + along) + (below + above))
        return (v0, v1, v2), sums

    def step(j, unused):
        for plane in range(planes):
            (ur, nur), (ui, nui), (dr, ndr), (di, ndi) = (neighbours(c, plane, j) for c in range(4))
            for tile in range(triples):
                spot = at(j, tile, plane)
                diag_up, bx, by, diag_down = (pot_ref[f, spot, :] for f in range(4))
                a, b, e, f = ur[tile], ui[tile], dr[tile], di[tile]
                flat[0, spot, :] = diag_up * a + bx * e + by * f - 0.5 * nur[tile]
                flat[1, spot, :] = diag_up * b + bx * f - by * e - 0.5 * nui[tile]
                flat[2, spot, :] = bx * a - by * b + diag_down * e - 0.5 * ndr[tile]
                flat[3, spot, :] = bx * b + by * a + diag_down * f - 0.5 * ndi[tile]
        return unused

    lax.fori_loop(0, steps, step, 0)
    for c in range(4):
        out_ref[0, c] = flat[c].astype(jnp.bfloat16)


def apply_bands(x, potential, near, far, planes, start, carry):
    count, rows = near.shape[0], x.shape[2]
    tiles = rows // planes
    steps = tiles // (3 * SUB)
    halo = pl.BlockSpec((1, 4, tiles, LANES), lambda b: (b, 0, 0, 0))
    body = functools.partial(apply_body, planes, rows)
    in_specs = [
        pl.BlockSpec((1, 4, rows, LANES), lambda b: (start + b, 0, 0, 0)),
        pl.BlockSpec((4, rows, LANES), lambda b: (0, 0, 0)),
        halo,
        halo,
    ]
    operands = [x, potential, near, far]
    aliases = {}
    if carry is not None:
        in_specs.append(pl.BlockSpec(memory_space=pl.ANY))
        operands.append(carry)
        aliases = {4: 0}
        call = body
    else:

        def call(x_ref, pot_ref, near_ref, far_ref, *rest):
            body(x_ref, pot_ref, near_ref, far_ref, None, *rest)

    return pl.pallas_call(
        call,
        grid=(count,),
        in_specs=in_specs,
        out_specs=pl.BlockSpec((1, 4, rows, LANES), lambda b: (start + b, 0, 0, 0)),
        out_shape=jax.ShapeDtypeStruct(x.shape, jnp.bfloat16),
        input_output_aliases=aliases,
        scratch_shapes=[
            pltpu.VMEM((4, rows, LANES), jnp.float32),
            pltpu.VMEM((2, 4, tiles, LANES), jnp.float32),
            pltpu.VMEM((4, 3, planes, steps + 2, SUB, LANES), jnp.float32),
            pltpu.VMEM((4, rows, LANES), jnp.float32),
        ],
        compiler_params=pltpu.CompilerParams(vmem_limit_bytes=VMEM_LIMIT),
        cost_estimate=pl.CostEstimate(
            flops=count * 4 * rows * LANES * 30, bytes_accessed=count * 4 * rows * LANES * 5, transcendentals=0
        ),
        name="apply",
    )(*operands)


def chunk_sizes(bands):
    if bands < 4:
        return [1] * bands
    middle, left = divmod(bands - 2, 2)
    return [1] + [2] * middle + [1] * left + [1]


def shards(spinors, kpt_mult, occupied, core_density, local_potential):
    bands, planes = spinors.shape[0], spinors.shape[2]
    total = bands * lax.axis_size("ka")
    size = lax.axis_size("brick")
    near_pairs = [(i, i ^ 1) for i in range(size) if i ^ 1 < size]
    far_pairs = [(i, j) for i in range(size) for j in [((i + 1) ^ 1) - 1] if 0 <= j < size]
    x = rows_view(spinors)
    core, local = rows_view(core_density), rows_view(local_potential)
    faces, halos, start = [], [], 0
    potential = None
    sizes = chunk_sizes(bands)
    for k, count in enumerate(sizes):
        after = halos[k - 2][1:] if k >= 2 else ()
        if potential is not None:
            after += (potential,)
        near, far = edges(x, planes, start, count, after)
        faces.append(near)
        halos.append((start, lax.ppermute(near, "brick", near_pairs), lax.ppermute(far, "brick", far_pairs)))
        start += count
        if k == min(1, len(sizes) - 1):
            density = lax.psum(density_of(x, kpt_mult, occupied, total, near), "ka")
        if k == min(3, len(sizes) - 1):
            potential = potential_of(density, core, local, near)
    out = None
    for start, near, far in halos:
        out = apply_bands(x, potential, near, far, planes, start, out)
    return planes_view(out, planes)


def solution(mesh):
    placed = (P("ka", None, "brick", None), P("ka"), P("ka"), P("brick", None), P("brick", None))
    return jax.shard_map(
        shards, mesh=mesh, in_specs=placed, out_specs=P("ka", None, "brick", None), check_vma=False
    )
```

```python
import functools
import math

import jax
import jax.numpy as jnp
from jax import lax
from jax.experimental import pallas as pl
from jax.experimental.pallas import tpu as pltpu
from jax.sharding import PartitionSpec as P

NY = 192
LANES = 128
SUB = 8
TRIPLE = 3
HALF = 2 * NY - 2 * LANES - LANES // 2
PACK = 16
FLOOR_FRACTION = 0.05
VMEM_LIMIT = 44 * 1024 * 1024
EDGES_VMEM_LIMIT = 58 * 1024 * 1024
SMALL = pl.CostEstimate(flops=0, bytes_accessed=0, transcendentals=0)


def rows_view(x):
    lead, planes, cells = x.shape[:-2], x.shape[-2], x.shape[-1]
    tiles = cells // LANES
    n = len(lead)
    x = x.reshape(lead + (planes, tiles, LANES))
    x = x.transpose(tuple(range(n)) + (n + 1, n, n + 2))
    return x.reshape(lead + (tiles * planes, LANES))


def planes_view(x, planes):
    lead, rows = x.shape[:-2], x.shape[-2]
    tiles = rows // planes
    n = len(lead)
    x = x.reshape(lead + (tiles, planes, LANES))
    x = x.transpose(tuple(range(n)) + (n + 1, n, n + 2))
    return x.reshape(lead + (planes, tiles * LANES))


def even_brick():
    return lax.axis_index("brick") % 2 == 0


def spread_matrix(back):
    size = SUB * PACK
    row = lax.broadcasted_iota(jnp.int32, (size, size), 0)
    column = lax.broadcasted_iota(jnp.int32, (size, size), 1)
    if back:
        row, column = column, row
    return (column == (row % SUB) * PACK + row // SUB).astype(jnp.bfloat16)


def gathered(read, segment, i):
    return jnp.concatenate(
        [read(pl.ds(pl.multiple_of(s * segment + i * PACK, PACK), PACK)) for s in range(SUB)], axis=0
    )


def product(matrix, values):
    return jnp.dot(matrix, values, preferred_element_type=jnp.float32)


def edges_body(planes, start, count, x_ref, *refs):
    near_ref, far_ref, held, sems = refs[-4:]
    rows = held.shape[2]
    segment = rows // SUB
    per = PACK // planes
    copies = [pltpu.make_async_copy(x_ref.at[start + b], held.at[b], sems.at[b]) for b in range(count)]
    for copy in copies:
        copy.start()
    out = per * SUB
    row = lax.broadcasted_iota(jnp.int32, (2 * out, SUB * PACK), 0)
    column = lax.broadcasted_iota(jnp.int32, (2 * out, SUB * PACK), 1)
    upper = (row < out) == even_brick()
    inner = row % out
    wanted = (inner % SUB) * PACK + (inner // SUB) * planes + jnp.where(upper, planes - 1, 0)
    select = (column == wanted).astype(jnp.bfloat16)
    for b in range(count):
        copies[b].wait()

        def step(i, unused):
            block = jnp.concatenate(
                [gathered(lambda at: held[b, c, at, :], segment, i) for c in range(4)], axis=1
            )
            faces = product(select, block).astype(jnp.bfloat16)
            at = pl.ds(pl.multiple_of(i * out, out), out)
            for c in range(4):
                lanes = slice(c * LANES, (c + 1) * LANES)
                near_ref[b, c, at, :] = faces[:out, lanes]
                far_ref[b, c, at, :] = faces[out:, lanes]
            return unused

        lax.fori_loop(0, segment // PACK, step, 0)


def weighed(amount):
    return pl.CostEstimate(flops=0, bytes_accessed=amount, transcendentals=0)


def edges(x, planes, start, count, after):
    rows = x.shape[2]
    shape = jax.ShapeDtypeStruct((count, 4, rows // planes, LANES), jnp.bfloat16)
    return pl.pallas_call(
        functools.partial(edges_body, planes, start, count),
        in_specs=[pl.BlockSpec(memory_space=pltpu.HBM)] + [pl.BlockSpec(memory_space=pl.ANY)] * len(after),
        out_shape=[shape, shape],
        scratch_shapes=[pltpu.VMEM((count, 4, rows, LANES), jnp.bfloat16), pltpu.SemaphoreType.DMA((count,))],
        compiler_params=pltpu.CompilerParams(vmem_limit_bytes=EDGES_VMEM_LIMIT),
        cost_estimate=weighed(count * 4 * rows * LANES * 3),
        name="edges",
    )(x, *after)


def gate(near, far, after):
    anywhere = pl.BlockSpec(memory_space=pl.ANY)
    return pl.pallas_call(
        lambda *refs: None,
        in_specs=[anywhere] * (2 + len(after)),
        out_specs=[anywhere, anywhere],
        out_shape=[jax.ShapeDtypeStruct(a.shape, a.dtype) for a in (near, far)],
        input_output_aliases={0: 0, 1: 1},
        name="gate",
    )(near, far, *after)


def density_body(bands, rows, scale, mult_ref, occ_ref, x_ref, after_ref, out_ref):
    weights = [(mult_ref[b] * occ_ref[b]).astype(jnp.float32) * scale for b in range(bands)]

    def step(i, unused):
        at = pl.ds(pl.multiple_of(i * PACK, PACK), PACK)
        up = down = real = imag = None
        for b in range(bands):
            ur, ui, dr, di = (x_ref[b, c, at, :].astype(jnp.float32) for c in range(4))
            wur, wui = weights[b] * ur, weights[b] * ui
            wdr, wdi = weights[b] * dr, weights[b] * di
            terms = (
                wur * ur + wui * ui,
                wdr * dr + wdi * di,
                wur * dr + wui * di,
                wur * di - wui * dr,
            )
            if b == 0:
                up, down, real, imag = terms
            else:
                up, down, real, imag = up + terms[0], down + terms[1], real + terms[2], imag + terms[3]
        out_ref[0, at, :] = (up + down).astype(jnp.bfloat16)
        out_ref[1, at, :] = (2.0 * real).astype(jnp.bfloat16)
        out_ref[2, at, :] = (2.0 * imag).astype(jnp.bfloat16)
        out_ref[3, at, :] = (up - down).astype(jnp.bfloat16)
        return unused

    lax.fori_loop(0, rows // PACK, step, 0)


def density_of(x, mult, occ, total, after):
    bands, rows = x.shape[0], x.shape[2]
    steps = 8
    part = rows // steps
    return pl.pallas_call(
        functools.partial(density_body, bands, part, 1.0 / (2.0 * total)),
        grid=(steps,),
        in_specs=[
            pl.BlockSpec(memory_space=pltpu.SMEM),
            pl.BlockSpec(memory_space=pltpu.SMEM),
            pl.BlockSpec((bands, 4, part, LANES), lambda i: (0, 0, i, 0)),
            pl.BlockSpec(memory_space=pl.ANY),
        ],
        out_specs=pl.BlockSpec((4, part, LANES), lambda i: (0, i, 0)),
        out_shape=jax.ShapeDtypeStruct((4, rows, LANES), jnp.bfloat16),
        compiler_params=pltpu.CompilerParams(vmem_limit_bytes=VMEM_LIMIT),
        cost_estimate=SMALL,
        name="density",
    )(mult, occ, x, after)


def cube_root(x):
    root = jnp.exp(jnp.log(jnp.abs(x)) * (1.0 / 3.0))
    return jnp.where(x < 0.0, -root, root)


def potential_body(rows, d_ref, core_ref, local_ref, after_ref, out_ref):
    segment = rows // SUB
    spread = spread_matrix(False)

    def step(i, unused):
        block = jnp.concatenate([gathered(lambda at: d_ref[f, at, :], segment, i) for f in range(4)], axis=1)
        fields = product(spread, block)
        d0, d1, d2, d3 = (fields[:, f * LANES : (f + 1) * LANES] for f in range(4))
        here = [pl.ds(i * PACK + r, SUB, stride=segment) for r in range(PACK)]
        core = jnp.concatenate([core_ref[at, :] for at in here], axis=0)
        local = jnp.concatenate([local_ref[at, :] for at in here], axis=0)
        electrons = d0 + core
        magnitude = jnp.sqrt(d1 * d1 + d2 * d2 + d3 * d3)
        upper = -cube_root((3.0 / math.pi) * (electrons + magnitude))
        lower = -cube_root((3.0 / math.pi) * (electrons - magnitude))
        factor = 0.5 * (upper - lower) / jnp.maximum(magnitude, FLOOR_FRACTION * electrons)
        v = 0.5 * (upper + lower) + local
        bz = factor * d3
        at = pl.ds(i * PACK, PACK)
        shape = (PACK, SUB, LANES)
        out_ref[0, at] = (v + bz + 3.0).reshape(shape)
        out_ref[1, at] = (factor * d1).reshape(shape)
        out_ref[2, at] = (factor * d2).reshape(shape)
        out_ref[3, at] = (v - bz + 3.0).reshape(shape)
        return unused

    lax.fori_loop(0, segment // PACK, step, 0)


def potential_of(density, core, local, after):
    rows = density.shape[1]
    whole = pl.BlockSpec(memory_space=pltpu.VMEM)
    return pl.pallas_call(
        functools.partial(potential_body, rows),
        in_specs=[whole, whole, whole, pl.BlockSpec(memory_space=pl.ANY)],
        out_specs=whole,
        out_shape=jax.ShapeDtypeStruct((4, rows // SUB, SUB, LANES), jnp.float32),
        compiler_params=pltpu.CompilerParams(vmem_limit_bytes=VMEM_LIMIT),
        cost_estimate=SMALL,
        name="potential",
    )(density, core, local, after)


def apply_body(planes, rows, x_ref, pot_ref, near_ref, far_ref, carry_ref, out_ref, wide, ends, turned, flat):
    segment = rows // SUB
    stride = planes * TRIPLE
    steps = segment // stride
    near_slot = jnp.where(even_brick(), 1, 0)
    spread, unspread = spread_matrix(False), spread_matrix(True)

    for c in range(4):
        ends[near_slot, c] = near_ref[0, c].astype(jnp.float32).reshape(ends.shape[2:])
        ends[1 - near_slot, c] = far_ref[0, c].astype(jnp.float32).reshape(ends.shape[2:])

    def load(i, unused):
        block = jnp.concatenate([gathered(lambda at: x_ref[0, c, at, :], segment, i) for c in range(4)], axis=1)
        values = product(spread, block)
        for c in range(4):
            part = values[:, c * LANES : (c + 1) * LANES]
            wide[c, pl.ds(i * PACK, PACK)] = part.reshape(PACK, SUB, LANES)
            turned[c, pl.ds(stride + i * PACK, PACK)] = pltpu.roll(part, HALF, 1).reshape(PACK, SUB, LANES)
        return unused

    lax.fori_loop(0, segment // PACK, load, 0)
    for c in range(4):
        for q in range(stride):
            turned[c, q] = pltpu.roll(turned[c, segment + q], 1, 0)
            turned[c, segment + stride + q] = pltpu.roll(turned[c, stride + q], SUB - 1, 0)

    lane = lax.broadcasted_iota(jnp.int32, (SUB, LANES), 1)
    low = lane < HALF
    initial, final = lane == 0, lane == LANES - 1
    inner_initial, inner_final = lane == HALF, lane == HALF - 1

    def neighbours(c, plane, j):
        spot = [j * stride + tile * planes + plane for tile in range(TRIPLE)]
        v0, v1, v2 = (wide[c, at] for at in spot)
        r0, r1, r2 = (turned[c, at + stride] for at in spot)
        after0 = r0 + turned[c, spot[0] + 2 * stride]
        after1 = r1 + turned[c, spot[1] + 2 * stride]
        before1 = r1 + turned[c, spot[1]]
        before2 = r2 + turned[c, spot[2]]
        across = (
            jnp.where(low, before1, before2),
            jnp.where(low, before2, after0),
            jnp.where(low, after0, after1),
        )
        plus = (
            jnp.where(initial, v1, v0),
            jnp.where(inner_initial, r0, jnp.where(initial, v2, v1)),
            jnp.where(initial, r1, v2),
        )
        minus = (
            jnp.where(final, r1, v0),
            jnp.where(inner_final, r2, jnp.where(final, v0, v1)),
            jnp.where(final, v1, v2),
        )
        sums = []
        for tile in range(TRIPLE):
            below = ends[0, c, j * TRIPLE + tile] if plane == 0 else wide[c, spot[tile] - 1]
            above = ends[1, c, j * TRIPLE + tile] if plane == planes - 1 else wide[c, spot[tile] + 1]
            along = pltpu.roll(plus[tile], LANES - 1, 1) + pltpu.roll(minus[tile], 1, 1)
            sums.append((across[tile] + along) + (below + above))
        return (v0, v1, v2), sums

    def step(j, unused):
        for plane in range(planes):
            (ur, nur), (ui, nui), (dr, ndr), (di, ndi) = (neighbours(c, plane, j) for c in range(4))
            for tile in range(TRIPLE):
                spot = j * stride + tile * planes + plane
                diag_up, bx, by, diag_down = (pot_ref[f, spot] for f in range(4))
                a, b, e, f = ur[tile], ui[tile], dr[tile], di[tile]
                flat[0, spot] = diag_up * a + bx * e + by * f - 0.5 * nur[tile]
                flat[1, spot] = diag_up * b + bx * f - by * e - 0.5 * nui[tile]
                flat[2, spot] = bx * a - by * b + diag_down * e - 0.5 * ndr[tile]
                flat[3, spot] = bx * b + by * a + diag_down * f - 0.5 * ndi[tile]
        return unused

    lax.fori_loop(0, steps, step, 0)

    def store(i, unused):
        at = pl.ds(i * PACK, PACK)
        block = jnp.concatenate([flat[c, at].reshape(PACK * SUB, LANES) for c in range(4)], axis=1)
        values = product(unspread, block.astype(jnp.bfloat16)).astype(jnp.bfloat16)
        for c in range(4):
            for s in range(SUB):
                out_ref[0, c, pl.ds(pl.multiple_of(s * segment + i * PACK, PACK), PACK), :] = values[
                    s * PACK : (s + 1) * PACK, c * LANES : (c + 1) * LANES
                ]
        return unused

    lax.fori_loop(0, segment // PACK, store, 0)


def apply_bands(x, potential, near, far, planes, start, carry):
    count, rows = near.shape[0], x.shape[2]
    segment = rows // SUB
    stride = planes * TRIPLE
    tiles = rows // planes
    halo = pl.BlockSpec((1, 4, tiles, LANES), lambda b: (b, 0, 0, 0))
    body = functools.partial(apply_body, planes, rows)
    in_specs = [
        pl.BlockSpec((1, 4, rows, LANES), lambda b: (start + b, 0, 0, 0)),
        pl.BlockSpec((4, segment, SUB, LANES), lambda b: (0, 0, 0, 0)),
        halo,
        halo,
    ]
    operands = [x, potential, near, far]
    aliases = {}
    if carry is not None:
        in_specs.append(pl.BlockSpec(memory_space=pl.ANY))
        operands.append(carry)
        aliases = {4: 0}
        call = body
    else:

        def call(x_ref, pot_ref, near_ref, far_ref, *rest):
            body(x_ref, pot_ref, near_ref, far_ref, None, *rest)

    return pl.pallas_call(
        call,
        grid=(count,),
        in_specs=in_specs,
        out_specs=pl.BlockSpec((1, 4, rows, LANES), lambda b: (start + b, 0, 0, 0)),
        out_shape=jax.ShapeDtypeStruct(x.shape, jnp.bfloat16),
        input_output_aliases=aliases,
        scratch_shapes=[
            pltpu.VMEM((4, segment, SUB, LANES), jnp.float32),
            pltpu.VMEM((2, 4, tiles // SUB, SUB, LANES), jnp.float32),
            pltpu.VMEM((4, segment + 2 * stride, SUB, LANES), jnp.float32),
            pltpu.VMEM((4, segment, SUB, LANES), jnp.float32),
        ],
        compiler_params=pltpu.CompilerParams(vmem_limit_bytes=VMEM_LIMIT),
        cost_estimate=SMALL,
        name="apply",
    )(*operands)


def chunk_sizes(bands):
    if bands < 6:
        return [1] * bands
    middle, left = divmod(bands - 4, 2)
    return [1, 1] + [2] * middle + [1] * left + [1, 1]


def shards(spinors, kpt_mult, occupied, core_density, local_potential):
    bands, planes = spinors.shape[0], spinors.shape[2]
    total = bands * lax.axis_size("ka")
    size = lax.axis_size("brick")
    near_pairs = [(i, i ^ 1) for i in range(size) if i ^ 1 < size]
    far_pairs = [(i, j) for i in range(size) for j in [((i + 1) ^ 1) - 1] if 0 <= j < size]
    x = rows_view(spinors)
    core, local = rows_view(core_density), rows_view(local_potential)
    sizes = chunk_sizes(bands)
    starts = [sum(sizes[:k]) for k in range(len(sizes))]

    faces, after = [], ()
    for k, count in enumerate(sizes):
        near, far = edges(x, planes, starts[k], count, after)
        faces.append((near, far))
        after = (near,)
        if k == 1:
            density = density_of(x, kpt_mult, occupied, total, near)
            after = (density,)
    halos, potential = [], None
    for k, (near, far) in enumerate(faces):
        if k >= 2:
            near, far = gate(near, far, halos[k - 2] + (() if potential is None else (potential,)))
        halos.append((lax.ppermute(near, "brick", near_pairs), lax.ppermute(far, "brick", far_pairs)))
        if k == min(3, len(faces) - 1):
            potential = potential_of(lax.psum(density, "ka"), core, local, near)
    out = None
    for start, (near, far) in zip(starts, halos):
        out = apply_bands(x, potential, near, far, planes, start, out)
    return planes_view(out, planes)


def solution(mesh):
    placed = (P("ka", None, "brick", None), P("ka"), P("ka"), P("brick", None), P("brick", None))
    return jax.shard_map(
        shards, mesh=mesh, in_specs=placed, out_specs=P("ka", None, "brick", None), check_vma=False
    )
```

```python
import functools
import math

import jax
import jax.numpy as jnp
from jax import lax
from jax.experimental import pallas as pl
from jax.experimental.pallas import tpu as pltpu
from jax.sharding import PartitionSpec as P

NY = 192
LANES = 128
SUB = 8
TRIPLE = 3
HALF = 2 * NY - 2 * LANES - LANES // 2
PACK = 16
FLOOR_FRACTION = 0.05
VMEM_LIMIT = 44 * 1024 * 1024
EDGES_VMEM_LIMIT = 58 * 1024 * 1024
SMALL = pl.CostEstimate(flops=0, bytes_accessed=0, transcendentals=0)


def rows_view(x):
    lead, planes, cells = x.shape[:-2], x.shape[-2], x.shape[-1]
    tiles = cells // LANES
    n = len(lead)
    x = x.reshape(lead + (planes, tiles, LANES))
    x = x.transpose(tuple(range(n)) + (n + 1, n, n + 2))
    return x.reshape(lead + (tiles * planes, LANES))


def planes_view(x, planes):
    lead, rows = x.shape[:-2], x.shape[-2]
    tiles = rows // planes
    n = len(lead)
    x = x.reshape(lead + (tiles, planes, LANES))
    x = x.transpose(tuple(range(n)) + (n + 1, n, n + 2))
    return x.reshape(lead + (planes, tiles * LANES))


def even_brick():
    return lax.axis_index("brick") % 2 == 0


def spread_matrix(back):
    size = SUB * PACK
    row = lax.broadcasted_iota(jnp.int32, (size, size), 0)
    column = lax.broadcasted_iota(jnp.int32, (size, size), 1)
    if back:
        row, column = column, row
    return (column == (row % SUB) * PACK + row // SUB).astype(jnp.bfloat16)


def gathered(read, segment, i):
    return jnp.concatenate(
        [read(pl.ds(pl.multiple_of(s * segment + i * PACK, PACK), PACK)) for s in range(SUB)], axis=0
    )


def product(matrix, values):
    return jnp.dot(matrix, values, preferred_element_type=jnp.float32)


def edges_body(planes, start, count, x_ref, *refs):
    near_ref, far_ref, held, sems = refs[-4:]
    rows = held.shape[2]
    segment = rows // SUB
    per = PACK // planes
    copies = [pltpu.make_async_copy(x_ref.at[start + b], held.at[b], sems.at[b]) for b in range(count)]
    for copy in copies:
        copy.start()
    out = per * SUB
    row = lax.broadcasted_iota(jnp.int32, (2 * out, SUB * PACK), 0)
    column = lax.broadcasted_iota(jnp.int32, (2 * out, SUB * PACK), 1)
    upper = (row < out) == even_brick()
    inner = row % out
    wanted = (inner % SUB) * PACK + (inner // SUB) * planes + jnp.where(upper, planes - 1, 0)
    select = (column == wanted).astype(jnp.bfloat16)
    for b in range(count):
        copies[b].wait()

        def step(i, unused):
            block = jnp.concatenate(
                [gathered(lambda at: held[b, c, at, :], segment, i) for c in range(4)], axis=1
            )
            faces = product(select, block).astype(jnp.bfloat16)
            at = pl.ds(pl.multiple_of(i * out, out), out)
            for c in range(4):
                lanes = slice(c * LANES, (c + 1) * LANES)
                near_ref[b, c, at, :] = faces[:out, lanes]
                far_ref[b, c, at, :] = faces[out:, lanes]
            return unused

        lax.fori_loop(0, segment // PACK, step, 0, unroll=True)


def weighed(amount):
    return pl.CostEstimate(flops=0, bytes_accessed=amount, transcendentals=0)


def edges(x, planes, start, count, after):
    rows = x.shape[2]
    shape = jax.ShapeDtypeStruct((count, 4, rows // planes, LANES), jnp.bfloat16)
    return pl.pallas_call(
        functools.partial(edges_body, planes, start, count),
        in_specs=[pl.BlockSpec(memory_space=pltpu.HBM)] + [pl.BlockSpec(memory_space=pl.ANY)] * len(after),
        out_shape=[shape, shape],
        scratch_shapes=[pltpu.VMEM((count, 4, rows, LANES), jnp.bfloat16), pltpu.SemaphoreType.DMA((count,))],
        compiler_params=pltpu.CompilerParams(vmem_limit_bytes=EDGES_VMEM_LIMIT),
        cost_estimate=weighed(count * 4 * rows * LANES * 3),
        name="edges",
    )(x, *after)


def gate(near, far, after):
    anywhere = pl.BlockSpec(memory_space=pl.ANY)
    return pl.pallas_call(
        lambda *refs: None,
        in_specs=[anywhere] * (2 + len(after)),
        out_specs=[anywhere, anywhere],
        out_shape=[jax.ShapeDtypeStruct(a.shape, a.dtype) for a in (near, far)],
        input_output_aliases={0: 0, 1: 1},
        name="gate",
    )(near, far, *after)


def density_body(bands, rows, scale, mult_ref, occ_ref, x_ref, after_ref, out_ref):
    weights = [(mult_ref[b] * occ_ref[b]).astype(jnp.float32) * scale for b in range(bands)]

    def step(i, unused):
        at = pl.ds(pl.multiple_of(i * PACK, PACK), PACK)
        up = down = real = imag = None
        for b in range(bands):
            ur, ui, dr, di = (x_ref[b, c, at, :].astype(jnp.float32) for c in range(4))
            wur, wui = weights[b] * ur, weights[b] * ui
            wdr, wdi = weights[b] * dr, weights[b] * di
            terms = (
                wur * ur + wui * ui,
                wdr * dr + wdi * di,
                wur * dr + wui * di,
                wur * di - wui * dr,
            )
            if b == 0:
                up, down, real, imag = terms
            else:
                up, down, real, imag = up + terms[0], down + terms[1], real + terms[2], imag + terms[3]
        out_ref[0, at, :] = (up + down).astype(jnp.bfloat16)
        out_ref[1, at, :] = (2.0 * real).astype(jnp.bfloat16)
        out_ref[2, at, :] = (2.0 * imag).astype(jnp.bfloat16)
        out_ref[3, at, :] = (up - down).astype(jnp.bfloat16)
        return unused

    lax.fori_loop(0, rows // PACK, step, 0)


def density_of(x, mult, occ, total, after):
    bands, rows = x.shape[0], x.shape[2]
    steps = 8
    part = rows // steps
    return pl.pallas_call(
        functools.partial(density_body, bands, part, 1.0 / (2.0 * total)),
        grid=(steps,),
        in_specs=[
            pl.BlockSpec(memory_space=pltpu.SMEM),
            pl.BlockSpec(memory_space=pltpu.SMEM),
            pl.BlockSpec((bands, 4, part, LANES), lambda i: (0, 0, i, 0)),
            pl.BlockSpec(memory_space=pl.ANY),
        ],
        out_specs=pl.BlockSpec((4, part, LANES), lambda i: (0, i, 0)),
        out_shape=jax.ShapeDtypeStruct((4, rows, LANES), jnp.bfloat16),
        compiler_params=pltpu.CompilerParams(vmem_limit_bytes=VMEM_LIMIT),
        cost_estimate=SMALL,
        name="density",
    )(mult, occ, x, after)


def cube_root(x):
    root = jnp.exp(jnp.log(jnp.abs(x)) * (1.0 / 3.0))
    return jnp.where(x < 0.0, -root, root)


def potential_body(rows, d_ref, core_ref, local_ref, after_ref, out_ref):
    segment = rows // SUB
    spread = spread_matrix(False)

    def step(i, unused):
        block = jnp.concatenate([gathered(lambda at: d_ref[f, at, :], segment, i) for f in range(4)], axis=1)
        fields = product(spread, block)
        d0, d1, d2, d3 = (fields[:, f * LANES : (f + 1) * LANES] for f in range(4))
        here = [pl.ds(i * PACK + r, SUB, stride=segment) for r in range(PACK)]
        core = jnp.concatenate([core_ref[at, :] for at in here], axis=0)
        local = jnp.concatenate([local_ref[at, :] for at in here], axis=0)
        electrons = d0 + core
        magnitude = jnp.sqrt(d1 * d1 + d2 * d2 + d3 * d3)
        upper = -cube_root((3.0 / math.pi) * (electrons + magnitude))
        lower = -cube_root((3.0 / math.pi) * (electrons - magnitude))
        factor = 0.5 * (upper - lower) / jnp.maximum(magnitude, FLOOR_FRACTION * electrons)
        v = 0.5 * (upper + lower) + local
        bz = factor * d3
        at = pl.ds(i * PACK, PACK)
        shape = (PACK, SUB, LANES)
        out_ref[0, at] = (v + bz + 3.0).reshape(shape)
        out_ref[1, at] = (factor * d1).reshape(shape)
        out_ref[2, at] = (factor * d2).reshape(shape)
        out_ref[3, at] = (v - bz + 3.0).reshape(shape)
        return unused

    lax.fori_loop(0, segment // PACK, step, 0, unroll=True)


def potential_of(density, core, local, after):
    rows = density.shape[1]
    whole = pl.BlockSpec(memory_space=pltpu.VMEM)
    return pl.pallas_call(
        functools.partial(potential_body, rows),
        in_specs=[whole, whole, whole, pl.BlockSpec(memory_space=pl.ANY)],
        out_specs=whole,
        out_shape=jax.ShapeDtypeStruct((4, rows // SUB, SUB, LANES), jnp.float32),
        compiler_params=pltpu.CompilerParams(vmem_limit_bytes=VMEM_LIMIT),
        cost_estimate=SMALL,
        name="potential",
    )(density, core, local, after)


def apply_body(planes, rows, x_ref, pot_ref, near_ref, far_ref, carry_ref, out_ref, token_ref, wide, ends, turned, flat):
    segment = rows // SUB
    stride = planes * TRIPLE
    steps = segment // stride
    near_slot = jnp.where(even_brick(), 1, 0)
    spread, unspread = spread_matrix(False), spread_matrix(True)

    for c in range(4):
        ends[near_slot, c] = near_ref[0, c].astype(jnp.float32).reshape(ends.shape[2:])
        ends[1 - near_slot, c] = far_ref[0, c].astype(jnp.float32).reshape(ends.shape[2:])

    def load(i, unused):
        block = jnp.concatenate([gathered(lambda at: x_ref[0, c, at, :], segment, i) for c in range(4)], axis=1)
        values = product(spread, block)
        for c in range(4):
            part = values[:, c * LANES : (c + 1) * LANES]
            wide[c, pl.ds(i * PACK, PACK)] = part.reshape(PACK, SUB, LANES)
            turned[c, pl.ds(stride + i * PACK, PACK)] = pltpu.roll(part, HALF, 1).reshape(PACK, SUB, LANES)
        return unused

    lax.fori_loop(0, segment // PACK, load, 0, unroll=True)
    for c in range(4):
        for q in range(stride):
            turned[c, q] = pltpu.roll(turned[c, segment + q], 1, 0)
            turned[c, segment + stride + q] = pltpu.roll(turned[c, stride + q], SUB - 1, 0)

    lane = lax.broadcasted_iota(jnp.int32, (SUB, LANES), 1)
    low = lane < HALF
    initial, final = lane == 0, lane == LANES - 1
    inner_initial, inner_final = lane == HALF, lane == HALF - 1

    def neighbours(c, plane, j):
        spot = [j * stride + tile * planes + plane for tile in range(TRIPLE)]
        v0, v1, v2 = (wide[c, at] for at in spot)
        r0, r1, r2 = (turned[c, at + stride] for at in spot)
        after0 = r0 + turned[c, spot[0] + 2 * stride]
        after1 = r1 + turned[c, spot[1] + 2 * stride]
        before1 = r1 + turned[c, spot[1]]
        before2 = r2 + turned[c, spot[2]]
        across = (
            jnp.where(low, before1, before2),
            jnp.where(low, before2, after0),
            jnp.where(low, after0, after1),
        )
        plus = (
            jnp.where(initial, v1, v0),
            jnp.where(inner_initial, r0, jnp.where(initial, v2, v1)),
            jnp.where(initial, r1, v2),
        )
        minus = (
            jnp.where(final, r1, v0),
            jnp.where(inner_final, r2, jnp.where(final, v0, v1)),
            jnp.where(final, v1, v2),
        )
        sums = []
        for tile in range(TRIPLE):
            below = ends[0, c, j * TRIPLE + tile] if plane == 0 else wide[c, spot[tile] - 1]
            above = ends[1, c, j * TRIPLE + tile] if plane == planes - 1 else wide[c, spot[tile] + 1]
            along = pltpu.roll(plus[tile], LANES - 1, 1) + pltpu.roll(minus[tile], 1, 1)
            sums.append((across[tile] + along) + (below + above))
        return (v0, v1, v2), sums

    def step(j, unused):
        for plane in range(planes):
            (ur, nur), (ui, nui), (dr, ndr), (di, ndi) = (neighbours(c, plane, j) for c in range(4))
            for tile in range(TRIPLE):
                spot = j * stride + tile * planes + plane
                diag_up, bx, by, diag_down = (pot_ref[f, spot] for f in range(4))
                a, b, e, f = ur[tile], ui[tile], dr[tile], di[tile]
                flat[0, spot] = diag_up * a + bx * e + by * f - 0.5 * nur[tile]
                flat[1, spot] = diag_up * b + bx * f - by * e - 0.5 * nui[tile]
                flat[2, spot] = bx * a - by * b + diag_down * e - 0.5 * ndr[tile]
                flat[3, spot] = bx * b + by * a + diag_down * f - 0.5 * ndi[tile]
        return unused

    lax.fori_loop(0, steps, step, 0)

    def store(i, unused):
        at = pl.ds(i * PACK, PACK)
        block = jnp.concatenate([flat[c, at].reshape(PACK * SUB, LANES) for c in range(4)], axis=1)
        values = product(unspread, block.astype(jnp.bfloat16)).astype(jnp.bfloat16)
        for c in range(4):
            for s in range(SUB):
                out_ref[0, c, pl.ds(pl.multiple_of(s * segment + i * PACK, PACK), PACK), :] = values[
                    s * PACK : (s + 1) * PACK, c * LANES : (c + 1) * LANES
                ]
        return unused

    lax.fori_loop(0, segment // PACK, store, 0, unroll=True)


def apply_bands(x, potential, near, far, planes, start, carry):
    count, rows = near.shape[0], x.shape[2]
    segment = rows // SUB
    stride = planes * TRIPLE
    tiles = rows // planes
    halo = pl.BlockSpec((1, 4, tiles, LANES), lambda b: (b, 0, 0, 0))
    body = functools.partial(apply_body, planes, rows)
    in_specs = [
        pl.BlockSpec((1, 4, rows, LANES), lambda b: (start + b, 0, 0, 0)),
        pl.BlockSpec((4, segment, SUB, LANES), lambda b: (0, 0, 0, 0)),
        halo,
        halo,
    ]
    operands = [x, potential, near, far]
    aliases = {}
    if carry is not None:
        in_specs.append(pl.BlockSpec(memory_space=pl.ANY))
        operands.append(carry)
        aliases = {4: 0}
        call = body
    else:

        def call(x_ref, pot_ref, near_ref, far_ref, *rest):
            body(x_ref, pot_ref, near_ref, far_ref, None, *rest)

    return pl.pallas_call(
        call,
        grid=(count,),
        in_specs=in_specs,
        out_specs=[
            pl.BlockSpec((1, 4, rows, LANES), lambda b: (start + b, 0, 0, 0)),
            pl.BlockSpec(memory_space=pl.ANY),
        ],
        out_shape=[
            jax.ShapeDtypeStruct(x.shape, jnp.bfloat16),
            jax.ShapeDtypeStruct((SUB, LANES), jnp.float32),
        ],
        input_output_aliases=aliases,
        scratch_shapes=[
            pltpu.VMEM((4, segment, SUB, LANES), jnp.float32),
            pltpu.VMEM((2, 4, tiles // SUB, SUB, LANES), jnp.float32),
            pltpu.VMEM((4, segment + 2 * stride, SUB, LANES), jnp.float32),
            pltpu.VMEM((4, segment, SUB, LANES), jnp.float32),
        ],
        compiler_params=pltpu.CompilerParams(vmem_limit_bytes=VMEM_LIMIT),
        cost_estimate=SMALL,
        name="apply",
    )(*operands)


def chunk_sizes(bands):
    if bands < 4:
        return [1] * bands
    middle, left = divmod(bands - 2, 2)
    return [1] + [2] * middle + [1] * left + [1]


def shards(spinors, kpt_mult, occupied, core_density, local_potential):
    bands, planes = spinors.shape[0], spinors.shape[2]
    total = bands * lax.axis_size("ka")
    size = lax.axis_size("brick")
    near_pairs = [(i, i ^ 1) for i in range(size) if i ^ 1 < size]
    far_pairs = [(i, j) for i in range(size) for j in [((i + 1) ^ 1) - 1] if 0 <= j < size]
    x = rows_view(spinors)
    core, local = rows_view(core_density), rows_view(local_potential)
    sizes = chunk_sizes(bands)
    starts = [sum(sizes[:k]) for k in range(len(sizes))]

    faces, after = [], ()
    for k, count in enumerate(sizes):
        near, far = edges(x, planes, starts[k], count, after)
        faces.append((near, far))
        after = (near,)
        if k == 1:
            density = density_of(x, kpt_mult, occupied, total, near)
            after = (density,)
    halos, potential, out, token = [], None, None, None
    for k, (near, far) in enumerate(faces):
        if k >= 2:
            near, far = gate(near, far, halos[k - 2] + (() if token is None else (token,)))
        halos.append((lax.ppermute(near, "brick", near_pairs), lax.ppermute(far, "brick", far_pairs)))
        if k == min(3, len(faces) - 1):
            potential = potential_of(lax.psum(density, "ka"), core, local, near)
        if potential is not None:
            for done in range(0 if out is None else k - 2, k - 1):
                out, token = apply_bands(x, potential, *halos[done], planes, starts[done], out)
    for done in range(len(faces) - 2, len(faces)):
        out, token = apply_bands(x, potential, *halos[done], planes, starts[done], out)
    return planes_view(out, planes)


def solution(mesh):
    placed = (P("ka", None, "brick", None), P("ka"), P("ka"), P("brick", None), P("brick", None))
    return jax.shard_map(
        shards, mesh=mesh, in_specs=placed, out_specs=P("ka", None, "brick", None), check_vma=False
    )
```

```python
import functools
import math

import jax
import jax.numpy as jnp
from jax import lax
from jax.experimental import pallas as pl
from jax.experimental.pallas import tpu as pltpu
from jax.sharding import PartitionSpec as P

NY = 192
LANES = 128
SUB = 8
TRIPLE = 3
HALF = 2 * NY - 2 * LANES - LANES // 2
PACK = 16
FLOOR_FRACTION = 0.05
VMEM_LIMIT = 63 * 1024 * 1024
SMALL = pl.CostEstimate(flops=0, bytes_accessed=0, transcendentals=0)


def rows_view(x):
    lead, planes, cells = x.shape[:-2], x.shape[-2], x.shape[-1]
    tiles = cells // LANES
    n = len(lead)
    x = x.reshape(lead + (planes, tiles, LANES))
    x = x.transpose(tuple(range(n)) + (n + 1, n, n + 2))
    return x.reshape(lead + (tiles * planes, LANES))


def planes_view(x, planes):
    lead, rows = x.shape[:-2], x.shape[-2]
    tiles = rows // planes
    n = len(lead)
    x = x.reshape(lead + (tiles, planes, LANES))
    x = x.transpose(tuple(range(n)) + (n + 1, n, n + 2))
    return x.reshape(lead + (planes, tiles * LANES))


def even_brick():
    return lax.axis_index("brick") % 2 == 0


def spread_matrix(back):
    size = SUB * PACK
    row = lax.broadcasted_iota(jnp.int32, (size, size), 0)
    column = lax.broadcasted_iota(jnp.int32, (size, size), 1)
    if back:
        row, column = column, row
    return (column == (row % SUB) * PACK + row // SUB).astype(jnp.bfloat16)


def gathered(read, segment, i):
    return jnp.concatenate(
        [read(pl.ds(s * segment + i * PACK, PACK)) for s in range(SUB)], axis=0
    )


def product(matrix, values):
    return jnp.dot(matrix, values, preferred_element_type=jnp.float32)


def edges_body(planes, chunks, x_ref, *refs):
    faces, held, sems = refs[-2 - 2 * len(chunks) : -2], refs[-2], refs[-1]
    first = chunks[0][0]
    bands = [(start - first + b, k, b) for k, (start, count) in enumerate(chunks) for b in range(count)]
    rows = held.shape[2]
    segment = rows // SUB
    copies = [pltpu.make_async_copy(x_ref.at[first + i], held.at[i], sems.at[i]) for i, _, _ in bands]
    for copy in copies:
        copy.start()
    out = PACK // planes * SUB
    row = lax.broadcasted_iota(jnp.int32, (2 * out, SUB * PACK), 0)
    column = lax.broadcasted_iota(jnp.int32, (2 * out, SUB * PACK), 1)
    upper = (row < out) == even_brick()
    inner = row % out
    wanted = (inner % SUB) * PACK + (inner // SUB) * planes + jnp.where(upper, planes - 1, 0)
    select = (column == wanted).astype(jnp.bfloat16)
    for i, k, b in bands:
        copies[i].wait()
        near_ref, far_ref = faces[2 * k], faces[2 * k + 1]
        for part in range(segment // PACK):
            block = jnp.concatenate(
                [gathered(lambda at: held[i, c, at, :], segment, part) for c in range(4)], axis=1
            )
            picked = product(select, block).astype(jnp.bfloat16)
            at = pl.ds(part * out, out)
            for c in range(4):
                lanes = slice(c * LANES, (c + 1) * LANES)
                near_ref[b, c, at, :] = picked[:out, lanes]
                far_ref[b, c, at, :] = picked[out:, lanes]


def edges(x, planes, chunks, after, limit):
    rows = x.shape[2]
    total = sum(count for _, count in chunks)
    shapes = [
        jax.ShapeDtypeStruct((count, 4, rows // planes, LANES), jnp.bfloat16) for _, count in chunks for _ in range(2)
    ]
    faces = pl.pallas_call(
        functools.partial(edges_body, planes, chunks),
        in_specs=[pl.BlockSpec(memory_space=pltpu.HBM)] + [pl.BlockSpec(memory_space=pl.ANY)] * len(after),
        out_shape=shapes,
        scratch_shapes=[pltpu.VMEM((total, 4, rows, LANES), jnp.bfloat16), pltpu.SemaphoreType.DMA((total,))],
        compiler_params=pltpu.CompilerParams(vmem_limit_bytes=limit),
        cost_estimate=SMALL,
        name="edges",
    )(x, *after)
    return [tuple(faces[2 * k : 2 * k + 2]) for k in range(len(chunks))]


def gate(near, far, after):
    anywhere = pl.BlockSpec(memory_space=pl.ANY)
    return pl.pallas_call(
        lambda *refs: None,
        in_specs=[anywhere] * (2 + len(after)),
        out_specs=[anywhere, anywhere],
        out_shape=[jax.ShapeDtypeStruct(a.shape, a.dtype) for a in (near, far)],
        input_output_aliases={0: 0, 1: 1},
        compiler_params=pltpu.CompilerParams(vmem_limit_bytes=VMEM_LIMIT),
        name="gate",
    )(near, far, *after)


def density_body(bands, rows, scale, mult_ref, occ_ref, x_ref, after_ref, out_ref):
    weights = [(mult_ref[b] * occ_ref[b]).astype(jnp.float32) * scale for b in range(bands)]

    def step(i, unused):
        at = pl.ds(pl.multiple_of(i * PACK, PACK), PACK)
        up = down = real = imag = None
        for b in range(bands):
            ur, ui, dr, di = (x_ref[b, c, at, :].astype(jnp.float32) for c in range(4))
            wur, wui = weights[b] * ur, weights[b] * ui
            wdr, wdi = weights[b] * dr, weights[b] * di
            terms = (
                wur * ur + wui * ui,
                wdr * dr + wdi * di,
                wur * dr + wui * di,
                wur * di - wui * dr,
            )
            if b == 0:
                up, down, real, imag = terms
            else:
                up, down, real, imag = up + terms[0], down + terms[1], real + terms[2], imag + terms[3]
        out_ref[0, at, :] = (up + down).astype(jnp.bfloat16)
        out_ref[1, at, :] = (2.0 * real).astype(jnp.bfloat16)
        out_ref[2, at, :] = (2.0 * imag).astype(jnp.bfloat16)
        out_ref[3, at, :] = (up - down).astype(jnp.bfloat16)
        return unused

    lax.fori_loop(0, rows // PACK, step, 0)


def density_of(x, mult, occ, total, after):
    bands, rows = x.shape[0], x.shape[2]
    steps = 8
    part = rows // steps
    return pl.pallas_call(
        functools.partial(density_body, bands, part, 1.0 / (2.0 * total)),
        grid=(steps,),
        in_specs=[
            pl.BlockSpec(memory_space=pltpu.SMEM),
            pl.BlockSpec(memory_space=pltpu.SMEM),
            pl.BlockSpec((bands, 4, part, LANES), lambda i: (0, 0, i, 0)),
            pl.BlockSpec(memory_space=pl.ANY),
        ],
        out_specs=pl.BlockSpec((4, part, LANES), lambda i: (0, i, 0)),
        out_shape=jax.ShapeDtypeStruct((4, rows, LANES), jnp.bfloat16),
        compiler_params=pltpu.CompilerParams(vmem_limit_bytes=VMEM_LIMIT),
        cost_estimate=SMALL,
        name="density",
    )(mult, occ, x, after)


def cube_root(x):
    root = jnp.exp(jnp.log(jnp.abs(x)) * (1.0 / 3.0))
    return jnp.where(x < 0.0, -root, root)


def potential_body(rows, d_ref, core_ref, local_ref, after_ref, out_ref):
    segment = rows // SUB
    spread = spread_matrix(False)

    def step(i, unused):
        block = jnp.concatenate([gathered(lambda at: d_ref[f, at, :], segment, i) for f in range(4)], axis=1)
        fields = product(spread, block)
        d0, d1, d2, d3 = (fields[:, f * LANES : (f + 1) * LANES] for f in range(4))
        here = [pl.ds(i * PACK + r, SUB, stride=segment) for r in range(PACK)]
        core = jnp.concatenate([core_ref[at, :] for at in here], axis=0)
        local = jnp.concatenate([local_ref[at, :] for at in here], axis=0)
        electrons = d0 + core
        magnitude = jnp.sqrt(d1 * d1 + d2 * d2 + d3 * d3)
        upper = -cube_root((3.0 / math.pi) * (electrons + magnitude))
        lower = -cube_root((3.0 / math.pi) * (electrons - magnitude))
        factor = 0.5 * (upper - lower) / jnp.maximum(magnitude, FLOOR_FRACTION * electrons)
        v = 0.5 * (upper + lower) + local
        bz = factor * d3
        at = pl.ds(i * PACK, PACK)
        shape = (PACK, SUB, LANES)
        out_ref[0, at] = (v + bz + 3.0).reshape(shape)
        out_ref[1, at] = (factor * d1).reshape(shape)
        out_ref[2, at] = (factor * d2).reshape(shape)
        out_ref[3, at] = (v - bz + 3.0).reshape(shape)
        return unused

    lax.fori_loop(0, segment // PACK, step, 0, unroll=True)


def potential_of(density, core, local, after):
    rows = density.shape[1]
    whole = pl.BlockSpec(memory_space=pltpu.VMEM)
    return pl.pallas_call(
        functools.partial(potential_body, rows),
        in_specs=[whole, whole, whole, pl.BlockSpec(memory_space=pl.ANY)],
        out_specs=whole,
        out_shape=jax.ShapeDtypeStruct((4, rows // SUB, SUB, LANES), jnp.float32),
        compiler_params=pltpu.CompilerParams(vmem_limit_bytes=VMEM_LIMIT),
        cost_estimate=SMALL,
        name="potential",
    )(density, core, local, after)


def kinetic_body(planes, rows, x_ref, after_ref, v_ref, n_ref, wide, turned):
    segment = rows // SUB
    stride = planes * TRIPLE
    steps = segment // stride
    spread = spread_matrix(False)

    for i in range(segment // PACK):
        block = jnp.concatenate([gathered(lambda at: x_ref[0, c, at, :], segment, i) for c in range(4)], axis=1)
        values = product(spread, block)
        for c in range(4):
            part = values[:, c * LANES : (c + 1) * LANES]
            v_ref[0, c, pl.ds(i * PACK * SUB, PACK * SUB), :] = part.astype(jnp.bfloat16)
            wide[c, pl.ds(i * PACK, PACK)] = part.reshape(PACK, SUB, LANES)
            turned[c, pl.ds(stride + i * PACK, PACK)] = pltpu.roll(part, HALF, 1).reshape(PACK, SUB, LANES)
    for c in range(4):
        for q in range(stride):
            turned[c, q] = pltpu.roll(turned[c, segment + q], 1, 0)
            turned[c, segment + stride + q] = pltpu.roll(turned[c, stride + q], SUB - 1, 0)

    lane = lax.broadcasted_iota(jnp.int32, (SUB, LANES), 1)
    low = lane < HALF
    initial, final = lane == 0, lane == LANES - 1
    inner_initial, inner_final = lane == HALF, lane == HALF - 1

    def neighbours(c, plane, j):
        spot = [j * stride + tile * planes + plane for tile in range(TRIPLE)]
        v0, v1, v2 = (wide[c, at] for at in spot)
        r0, r1, r2 = (turned[c, at + stride] for at in spot)
        after0 = r0 + turned[c, spot[0] + 2 * stride]
        after1 = r1 + turned[c, spot[1] + 2 * stride]
        before1 = r1 + turned[c, spot[1]]
        before2 = r2 + turned[c, spot[2]]
        across = (
            jnp.where(low, before1, before2),
            jnp.where(low, before2, after0),
            jnp.where(low, after0, after1),
        )
        plus = (
            jnp.where(initial, v1, v0),
            jnp.where(inner_initial, r0, jnp.where(initial, v2, v1)),
            jnp.where(initial, r1, v2),
        )
        minus = (
            jnp.where(final, r1, v0),
            jnp.where(inner_final, r2, jnp.where(final, v0, v1)),
            jnp.where(final, v1, v2),
        )
        sums = []
        for tile in range(TRIPLE):
            total = pltpu.roll(plus[tile], LANES - 1, 1) + pltpu.roll(minus[tile], 1, 1) + across[tile]
            if plane > 0:
                total = total + wide[c, spot[tile] - 1]
            if plane < planes - 1:
                total = total + wide[c, spot[tile] + 1]
            sums.append(total)
        return spot, sums

    def step(j, unused):
        for c in range(4):
            for plane in range(planes):
                spots, sums = neighbours(c, plane, j)
                for spot, total in zip(spots, sums):
                    n_ref[0, c, spot] = -0.5 * total
        return unused

    lax.fori_loop(0, steps, step, 0)


def kinetic_of(x, planes, start, count, after):
    rows = x.shape[2]
    segment = rows // SUB
    stride = planes * TRIPLE
    return pl.pallas_call(
        functools.partial(kinetic_body, planes, rows),
        grid=(count,),
        in_specs=[
            pl.BlockSpec((1, 4, rows, LANES), lambda b: (start + b, 0, 0, 0)),
            pl.BlockSpec(memory_space=pl.ANY),
        ],
        out_specs=[
            pl.BlockSpec((1, 4, rows, LANES), lambda b: (b, 0, 0, 0)),
            pl.BlockSpec((1, 4, segment, SUB, LANES), lambda b: (b, 0, 0, 0, 0)),
        ],
        out_shape=[
            jax.ShapeDtypeStruct((count, 4, rows, LANES), jnp.bfloat16),
            jax.ShapeDtypeStruct((count, 4, segment, SUB, LANES), jnp.float32),
        ],
        scratch_shapes=[
            pltpu.VMEM((4, segment, SUB, LANES), jnp.float32),
            pltpu.VMEM((4, segment + 2 * stride, SUB, LANES), jnp.float32),
        ],
        compiler_params=pltpu.CompilerParams(vmem_limit_bytes=VMEM_LIMIT),
        cost_estimate=SMALL,
        name="kinetic",
    )(x, after)


def mix_body(planes, rows, v_ref, n_ref, pot_ref, near_ref, far_ref, carry_ref, out_ref, token_ref):
    segment = rows // SUB
    size = PACK * SUB
    per = PACK // planes
    even = even_brick()
    unspread = spread_matrix(True)

    for i in range(segment // PACK):
        at = pl.ds(i * PACK, PACK)
        outside = pl.ds(i * per * SUB, per * SUB)
        cells, rest = [], []
        for c in range(4):
            cells.append(v_ref[0, c, pl.ds(i * size, size), :].astype(jnp.float32))
            near = near_ref[0, c, outside, :].astype(jnp.float32).reshape(per, SUB, LANES)
            far = far_ref[0, c, outside, :].astype(jnp.float32).reshape(per, SUB, LANES)
            below, above = jnp.where(even, far, near), jnp.where(even, near, far)
            n = n_ref[0, c, at]
            pieces = []
            for q in range(PACK):
                piece = n[q]
                if q % planes == 0:
                    piece = piece - 0.5 * below[q // planes]
                if q % planes == planes - 1:
                    piece = piece - 0.5 * above[q // planes]
                pieces.append(piece)
            rest.append(jnp.concatenate(pieces, axis=0))
        diag_up, bx, by, diag_down = (pot_ref[f, at].reshape(size, LANES) for f in range(4))
        ur, ui, dr, di = cells
        results = (
            rest[0] + diag_up * ur + bx * dr + by * di,
            rest[1] + diag_up * ui + bx * di - by * dr,
            rest[2] + bx * ur - by * ui + diag_down * dr,
            rest[3] + bx * ui + by * ur + diag_down * di,
        )
        block = jnp.concatenate([r.astype(jnp.bfloat16) for r in results], axis=1)
        values = product(unspread, block).astype(jnp.bfloat16)
        for c in range(4):
            for s in range(SUB):
                out_ref[0, c, pl.ds(s * segment + i * PACK, PACK), :] = values[
                    s * PACK : (s + 1) * PACK, c * LANES : (c + 1) * LANES
                ]


def mix_bands(v, n, potential, near, far, planes, start, bands, carry):
    count, rows = v.shape[0], v.shape[2]
    segment = rows // SUB
    halo = pl.BlockSpec((1, 4, rows // planes, LANES), lambda b: (b, 0, 0, 0))
    body = functools.partial(mix_body, planes, rows)
    in_specs = [
        pl.BlockSpec((1, 4, rows, LANES), lambda b: (b, 0, 0, 0)),
        pl.BlockSpec((1, 4, segment, SUB, LANES), lambda b: (b, 0, 0, 0, 0)),
        pl.BlockSpec((4, segment, SUB, LANES), lambda b: (0, 0, 0, 0)),
        halo,
        halo,
    ]
    operands = [v, n, potential, near, far]
    aliases = {}
    if carry is not None:
        in_specs.append(pl.BlockSpec(memory_space=pl.ANY))
        operands.append(carry)
        aliases = {5: 0}
        call = body
    else:

        def call(*refs):
            body(*refs[:5], None, *refs[5:])

    return pl.pallas_call(
        call,
        grid=(count,),
        in_specs=in_specs,
        out_specs=[
            pl.BlockSpec((1, 4, rows, LANES), lambda b: (start + b, 0, 0, 0)),
            pl.BlockSpec(memory_space=pl.ANY),
        ],
        out_shape=[
            jax.ShapeDtypeStruct((bands, 4, rows, LANES), jnp.bfloat16),
            jax.ShapeDtypeStruct((SUB, LANES), jnp.float32),
        ],
        input_output_aliases=aliases,
        compiler_params=pltpu.CompilerParams(vmem_limit_bytes=VMEM_LIMIT),
        cost_estimate=SMALL,
        name="mix",
    )(*operands)


def chunk_sizes(bands):
    if bands < 4:
        return [1] * bands
    middle, left = divmod(bands - 2, 2)
    return [1] + [2] * middle + [1] * left + [1]


def shards(spinors, kpt_mult, occupied, core_density, local_potential):
    bands, planes = spinors.shape[0], spinors.shape[2]
    total = bands * lax.axis_size("ka")
    size = lax.axis_size("brick")
    near_pairs = [(i, i ^ 1) for i in range(size) if i ^ 1 < size]
    far_pairs = [(i, j) for i in range(size) for j in [((i + 1) ^ 1) - 1] if 0 <= j < size]
    x = rows_view(spinors)
    core, local = rows_view(core_density), rows_view(local_potential)
    sizes = chunk_sizes(bands)
    starts = [sum(sizes[:k]) for k in range(len(sizes))]

    chunks = list(zip(starts, sizes))
    swap = lambda face: (lax.ppermute(face[0], "brick", near_pairs), lax.ppermute(face[1], "brick", far_pairs))
    faces = edges(x, planes, chunks[:1], (), VMEM_LIMIT)
    halos = [swap(faces[0])]
    if len(chunks) > 1:
        faces += edges(x, planes, chunks[1:2], (faces[0][0],), VMEM_LIMIT)
        halos.append(swap(faces[1]))
    density = density_of(x, kpt_mult, occupied, total, faces[-1][0])
    density_sum = lax.psum(density, "ka")
    if len(chunks) > 2:
        faces += edges(x, planes, chunks[2:], halos[0], VMEM_LIMIT)
        halos.append(swap(faces[2]))
    kinetic = [kinetic_of(x, planes, start, count, faces[-1][0]) for start, count in chunks]
    potential = out = token = None
    for k in range(min(3, len(chunks)), len(chunks) + 2):
        if k < len(chunks):
            before = tuple(v for v, _ in kinetic[:3]) if token is None else (token,)
            halos.append(swap(gate(*faces[k], halos[k - 2] + before)))
        if potential is None:
            potential = potential_of(density_sum, core, local, faces[-1][0])
        for done in range(0 if out is None else k - 2, k - 1):
            if done < len(chunks):
                out, token = mix_bands(
                    *kinetic[done], potential, *halos[done], planes, starts[done], bands, out
                )
    return planes_view(out, planes)


def solution(mesh):
    placed = (P("ka", None, "brick", None), P("ka"), P("ka"), P("brick", None), P("brick", None))
    return jax.shard_map(
        shards, mesh=mesh, in_specs=placed, out_specs=P("ka", None, "brick", None), check_vma=False
    )
```

```python
import functools
import math

import jax
import jax.numpy as jnp
from jax import lax
from jax.experimental import pallas as pl
from jax.experimental.pallas import tpu as pltpu
from jax.sharding import PartitionSpec as P

NY = 192
LANES = 128
SUB = 8
TRIPLE = 3
HALF = 2 * NY - 2 * LANES - LANES // 2
PACK = 16
FLOOR_FRACTION = 0.05
VMEM_LIMIT = 63 * 1024 * 1024
SMALL = pl.CostEstimate(flops=0, bytes_accessed=0, transcendentals=0)


def rows_view(x):
    lead, planes, cells = x.shape[:-2], x.shape[-2], x.shape[-1]
    tiles = cells // LANES
    n = len(lead)
    x = x.reshape(lead + (planes, tiles, LANES))
    x = x.transpose(tuple(range(n)) + (n + 1, n, n + 2))
    return x.reshape(lead + (tiles * planes, LANES))


def planes_view(x, planes):
    lead, rows = x.shape[:-2], x.shape[-2]
    tiles = rows // planes
    n = len(lead)
    x = x.reshape(lead + (tiles, planes, LANES))
    x = x.transpose(tuple(range(n)) + (n + 1, n, n + 2))
    return x.reshape(lead + (planes, tiles * LANES))


def even_brick():
    return lax.axis_index("brick") % 2 == 0


def spread_matrix(back):
    size = SUB * PACK
    row = lax.broadcasted_iota(jnp.int32, (size, size), 0)
    column = lax.broadcasted_iota(jnp.int32, (size, size), 1)
    if back:
        row, column = column, row
    return (column == (row % SUB) * PACK + row // SUB).astype(jnp.bfloat16)


def gathered(read, segment, i):
    return jnp.concatenate(
        [read(pl.ds(s * segment + i * PACK, PACK)) for s in range(SUB)], axis=0
    )


def product(matrix, values):
    return jnp.dot(matrix, values, preferred_element_type=jnp.float32)


def face_matrix(planes):
    out = PACK // planes * SUB
    row = lax.broadcasted_iota(jnp.int32, (2 * out, SUB * PACK), 0)
    column = lax.broadcasted_iota(jnp.int32, (2 * out, SUB * PACK), 1)
    upper = (row < out) == even_brick()
    inner = row % out
    wanted = (inner % SUB) * PACK + (inner // SUB) * planes + jnp.where(upper, planes - 1, 0)
    return (column == wanted).astype(jnp.bfloat16), out


def edges_body(planes, chunks, x_ref, *refs):
    faces, held, sems = refs[-2 - 2 * len(chunks) : -2], refs[-2], refs[-1]
    first = chunks[0][0]
    bands = [(start - first + b, k, b) for k, (start, count) in enumerate(chunks) for b in range(count)]
    rows = held.shape[2]
    segment = rows // SUB
    copies = [pltpu.make_async_copy(x_ref.at[first + i], held.at[i], sems.at[i]) for i, _, _ in bands]
    for copy in copies:
        copy.start()
    select, out = face_matrix(planes)
    for i, k, b in bands:
        copies[i].wait()
        near_ref, far_ref = faces[2 * k], faces[2 * k + 1]
        for part in range(segment // PACK):
            block = jnp.concatenate(
                [gathered(lambda at: held[i, c, at, :], segment, part) for c in range(4)], axis=1
            )
            picked = product(select, block).astype(jnp.bfloat16)
            at = pl.ds(part * out, out)
            for c in range(4):
                lanes = slice(c * LANES, (c + 1) * LANES)
                near_ref[b, c, at, :] = picked[:out, lanes]
                far_ref[b, c, at, :] = picked[out:, lanes]


def edges(x, planes, chunks, after, limit):
    rows = x.shape[2]
    total = sum(count for _, count in chunks)
    shapes = [
        jax.ShapeDtypeStruct((count, 4, rows // planes, LANES), jnp.bfloat16) for _, count in chunks for _ in range(2)
    ]
    faces = pl.pallas_call(
        functools.partial(edges_body, planes, chunks),
        in_specs=[pl.BlockSpec(memory_space=pltpu.HBM)] + [pl.BlockSpec(memory_space=pl.ANY)] * len(after),
        out_shape=shapes,
        scratch_shapes=[pltpu.VMEM((total, 4, rows, LANES), jnp.bfloat16), pltpu.SemaphoreType.DMA((total,))],
        compiler_params=pltpu.CompilerParams(vmem_limit_bytes=limit),
        cost_estimate=SMALL,
        name="edges",
    )(x, *after)
    return [tuple(faces[2 * k : 2 * k + 2]) for k in range(len(chunks))]


def gate(near, far, after):
    anywhere = pl.BlockSpec(memory_space=pl.ANY)
    return pl.pallas_call(
        lambda *refs: None,
        in_specs=[anywhere] * (2 + len(after)),
        out_specs=[anywhere, anywhere],
        out_shape=[jax.ShapeDtypeStruct(a.shape, a.dtype) for a in (near, far)],
        input_output_aliases={0: 0, 1: 1},
        compiler_params=pltpu.CompilerParams(vmem_limit_bytes=VMEM_LIMIT),
        name="gate",
    )(near, far, *after)


def front_body(planes, scale, counts, mult_ref, occ_ref, x_ref, *refs):
    bands = x_ref.shape[0]
    density_ref, faces = refs[-1 - 2 * len(counts)], refs[len(refs) - 2 * len(counts) :]
    weights = [(mult_ref[b] * occ_ref[b]).astype(jnp.float32) * scale for b in range(bands)]
    for s in range(SUB):
        up = down = real = imag = None
        for b in range(bands):
            ur, ui, dr, di = (x_ref[b, c, s].astype(jnp.float32) for c in range(4))
            wur, wui = weights[b] * ur, weights[b] * ui
            wdr, wdi = weights[b] * dr, weights[b] * di
            terms = (
                wur * ur + wui * ui,
                wdr * dr + wdi * di,
                wur * dr + wui * di,
                wur * di - wui * dr,
            )
            if b == 0:
                up, down, real, imag = terms
            else:
                up, down, real, imag = up + terms[0], down + terms[1], real + terms[2], imag + terms[3]
        density_ref[0, s] = (up + down).astype(jnp.bfloat16)
        density_ref[1, s] = (2.0 * real).astype(jnp.bfloat16)
        density_ref[2, s] = (2.0 * imag).astype(jnp.bfloat16)
        density_ref[3, s] = (up - down).astype(jnp.bfloat16)
    if counts:
        select, out = face_matrix(planes)
    band = bands - sum(counts)
    for k, count in enumerate(counts):
        for b in range(count):
            block = jnp.concatenate(
                [x_ref[band, c].reshape(SUB * PACK, LANES) for c in range(4)], axis=1
            )
            picked = product(select, block).astype(jnp.bfloat16)
            for c in range(4):
                lanes = slice(c * LANES, (c + 1) * LANES)
                faces[2 * k][b, c] = picked[:out, lanes]
                faces[2 * k + 1][b, c] = picked[out:, lanes]
            band += 1


def front(x, mult, occ, total, planes, counts, after):
    bands, rows = x.shape[0], x.shape[2]
    segment = rows // SUB
    out = PACK // planes * SUB
    anywhere = pl.BlockSpec(memory_space=pl.ANY)
    results = pl.pallas_call(
        functools.partial(front_body, planes, 1.0 / (2.0 * total), counts),
        grid=(segment // PACK,),
        in_specs=[
            pl.BlockSpec(memory_space=pltpu.SMEM),
            pl.BlockSpec(memory_space=pltpu.SMEM),
            pl.BlockSpec((bands, 4, SUB, PACK, LANES), lambda i: (0, 0, 0, i, 0)),
        ]
        + [anywhere] * len(after),
        out_specs=[pl.BlockSpec((4, SUB, PACK, LANES), lambda i: (0, 0, i, 0))]
        + [pl.BlockSpec((count, 4, out, LANES), lambda i: (0, 0, i, 0)) for count in counts for _ in range(2)],
        out_shape=[jax.ShapeDtypeStruct((4, SUB, segment, LANES), jnp.bfloat16)]
        + [
            jax.ShapeDtypeStruct((count, 4, rows // planes, LANES), jnp.bfloat16)
            for count in counts
            for _ in range(2)
        ],
        compiler_params=pltpu.CompilerParams(vmem_limit_bytes=VMEM_LIMIT),
        cost_estimate=SMALL,
        name="front",
    )(mult, occ, x.reshape(bands, 4, SUB, segment, LANES), *after)
    return results[0].reshape(4, rows, LANES), [tuple(results[1 + 2 * k : 3 + 2 * k]) for k in range(len(counts))]


def cube_root(x):
    root = jnp.exp(jnp.log(jnp.abs(x)) * (1.0 / 3.0))
    return jnp.where(x < 0.0, -root, root)


def potential_body(rows, d_ref, core_ref, local_ref, out_ref):
    segment = rows // SUB
    spread = spread_matrix(False)

    def step(i, unused):
        block = jnp.concatenate([gathered(lambda at: d_ref[f, at, :], segment, i) for f in range(4)], axis=1)
        fields = product(spread, block)
        d0, d1, d2, d3 = (fields[:, f * LANES : (f + 1) * LANES] for f in range(4))
        here = [pl.ds(i * PACK + r, SUB, stride=segment) for r in range(PACK)]
        core = jnp.concatenate([core_ref[at, :] for at in here], axis=0)
        local = jnp.concatenate([local_ref[at, :] for at in here], axis=0)
        electrons = d0 + core
        magnitude = jnp.sqrt(d1 * d1 + d2 * d2 + d3 * d3)
        upper = -cube_root((3.0 / math.pi) * (electrons + magnitude))
        lower = -cube_root((3.0 / math.pi) * (electrons - magnitude))
        factor = 0.5 * (upper - lower) / jnp.maximum(magnitude, FLOOR_FRACTION * electrons)
        v = 0.5 * (upper + lower) + local
        bz = factor * d3
        at = pl.ds(i * PACK, PACK)
        shape = (PACK, SUB, LANES)
        out_ref[0, at] = (v + bz + 3.0).reshape(shape)
        out_ref[1, at] = (factor * d1).reshape(shape)
        out_ref[2, at] = (factor * d2).reshape(shape)
        out_ref[3, at] = (v - bz + 3.0).reshape(shape)
        return unused

    lax.fori_loop(0, segment // PACK, step, 0, unroll=True)


def potential_of(density, core, local):
    rows = density.shape[1]
    whole = pl.BlockSpec(memory_space=pltpu.VMEM)
    return pl.pallas_call(
        functools.partial(potential_body, rows),
        in_specs=[whole, whole, whole],
        out_specs=whole,
        out_shape=jax.ShapeDtypeStruct((4, rows // SUB, SUB, LANES), jnp.float32),
        compiler_params=pltpu.CompilerParams(vmem_limit_bytes=VMEM_LIMIT),
        cost_estimate=SMALL,
        name="potential",
    )(density, core, local)


def apply_body(planes, rows, x_ref, pot_ref, near_ref, far_ref, carry_ref, out_ref, token_ref, wide, ends, turned, flat):
    segment = rows // SUB
    stride = planes * TRIPLE
    steps = segment // stride
    near_slot = jnp.where(even_brick(), 1, 0)
    spread, unspread = spread_matrix(False), spread_matrix(True)

    for c in range(4):
        ends[near_slot, c] = near_ref[0, c].astype(jnp.float32).reshape(ends.shape[2:])
        ends[1 - near_slot, c] = far_ref[0, c].astype(jnp.float32).reshape(ends.shape[2:])

    def load(i, unused):
        block = jnp.concatenate([gathered(lambda at: x_ref[0, c, at, :], segment, i) for c in range(4)], axis=1)
        values = product(spread, block)
        for c in range(4):
            part = values[:, c * LANES : (c + 1) * LANES]
            wide[c, pl.ds(i * PACK, PACK)] = part.reshape(PACK, SUB, LANES)
            turned[c, pl.ds(stride + i * PACK, PACK)] = pltpu.roll(part, HALF, 1).reshape(PACK, SUB, LANES)
        return unused

    lax.fori_loop(0, segment // PACK, load, 0, unroll=True)
    for c in range(4):
        for q in range(stride):
            turned[c, q] = pltpu.roll(turned[c, segment + q], 1, 0)
            turned[c, segment + stride + q] = pltpu.roll(turned[c, stride + q], SUB - 1, 0)

    lane = lax.broadcasted_iota(jnp.int32, (SUB, LANES), 1)
    low = lane < HALF
    initial, final = lane == 0, lane == LANES - 1
    inner_initial, inner_final = lane == HALF, lane == HALF - 1

    def neighbours(c, plane, j):
        spot = [j * stride + tile * planes + plane for tile in range(TRIPLE)]
        v0, v1, v2 = (wide[c, at] for at in spot)
        r0, r1, r2 = (turned[c, at + stride] for at in spot)
        after0 = r0 + turned[c, spot[0] + 2 * stride]
        after1 = r1 + turned[c, spot[1] + 2 * stride]
        before1 = r1 + turned[c, spot[1]]
        before2 = r2 + turned[c, spot[2]]
        across = (
            jnp.where(low, before1, before2),
            jnp.where(low, before2, after0),
            jnp.where(low, after0, after1),
        )
        plus = (
            jnp.where(initial, v1, v0),
            jnp.where(inner_initial, r0, jnp.where(initial, v2, v1)),
            jnp.where(initial, r1, v2),
        )
        minus = (
            jnp.where(final, r1, v0),
            jnp.where(inner_final, r2, jnp.where(final, v0, v1)),
            jnp.where(final, v1, v2),
        )
        sums = []
        for tile in range(TRIPLE):
            below = ends[0, c, j * TRIPLE + tile] if plane == 0 else wide[c, spot[tile] - 1]
            above = ends[1, c, j * TRIPLE + tile] if plane == planes - 1 else wide[c, spot[tile] + 1]
            along = pltpu.roll(plus[tile], LANES - 1, 1) + pltpu.roll(minus[tile], 1, 1)
            sums.append((across[tile] + along) + (below + above))
        return (v0, v1, v2), sums

    def step(j, unused):
        for plane in range(planes):
            (ur, nur), (ui, nui), (dr, ndr), (di, ndi) = (neighbours(c, plane, j) for c in range(4))
            for tile in range(TRIPLE):
                spot = j * stride + tile * planes + plane
                diag_up, bx, by, diag_down = (pot_ref[f, spot] for f in range(4))
                a, b, e, f = ur[tile], ui[tile], dr[tile], di[tile]
                flat[0, spot] = diag_up * a + bx * e + by * f - 0.5 * nur[tile]
                flat[1, spot] = diag_up * b + bx * f - by * e - 0.5 * nui[tile]
                flat[2, spot] = bx * a - by * b + diag_down * e - 0.5 * ndr[tile]
                flat[3, spot] = bx * b + by * a + diag_down * f - 0.5 * ndi[tile]
        return unused

    lax.fori_loop(0, steps, step, 0)

    def store(i, unused):
        at = pl.ds(i * PACK, PACK)
        block = jnp.concatenate([flat[c, at].reshape(PACK * SUB, LANES) for c in range(4)], axis=1)
        values = product(unspread, block.astype(jnp.bfloat16)).astype(jnp.bfloat16)
        for c in range(4):
            for s in range(SUB):
                out_ref[0, c, pl.ds(pl.multiple_of(s * segment + i * PACK, PACK), PACK), :] = values[
                    s * PACK : (s + 1) * PACK, c * LANES : (c + 1) * LANES
                ]
        return unused

    lax.fori_loop(0, segment // PACK, store, 0, unroll=True)


def apply_bands(x, potential, near, far, planes, start, carry):
    count, rows = near.shape[0], x.shape[2]
    segment = rows // SUB
    stride = planes * TRIPLE
    tiles = rows // planes
    halo = pl.BlockSpec((1, 4, tiles, LANES), lambda b: (b, 0, 0, 0))
    body = functools.partial(apply_body, planes, rows)
    in_specs = [
        pl.BlockSpec((1, 4, rows, LANES), lambda b: (start + b, 0, 0, 0)),
        pl.BlockSpec((4, segment, SUB, LANES), lambda b: (0, 0, 0, 0)),
        halo,
        halo,
    ]
    operands = [x, potential, near, far]
    aliases = {}
    if carry is not None:
        in_specs.append(pl.BlockSpec(memory_space=pl.ANY))
        operands.append(carry)
        aliases = {4: 0}
        call = body
    else:

        def call(x_ref, pot_ref, near_ref, far_ref, *rest):
            body(x_ref, pot_ref, near_ref, far_ref, None, *rest)

    return pl.pallas_call(
        call,
        grid=(count,),
        in_specs=in_specs,
        out_specs=[
            pl.BlockSpec((1, 4, rows, LANES), lambda b: (start + b, 0, 0, 0)),
            pl.BlockSpec(memory_space=pl.ANY),
        ],
        out_shape=[
            jax.ShapeDtypeStruct(x.shape, jnp.bfloat16),
            jax.ShapeDtypeStruct((SUB, LANES), jnp.float32),
        ],
        input_output_aliases=aliases,
        scratch_shapes=[
            pltpu.VMEM((4, segment, SUB, LANES), jnp.float32),
            pltpu.VMEM((2, 4, tiles // SUB, SUB, LANES), jnp.float32),
            pltpu.VMEM((4, segment + 2 * stride, SUB, LANES), jnp.float32),
            pltpu.VMEM((4, segment, SUB, LANES), jnp.float32),
        ],
        compiler_params=pltpu.CompilerParams(vmem_limit_bytes=VMEM_LIMIT),
        cost_estimate=SMALL,
        name="apply",
    )(*operands)


def chunk_sizes(bands):
    return [2] * (bands // 2) + [1] * (bands % 2)


def shards(spinors, kpt_mult, occupied, core_density, local_potential):
    bands, planes = spinors.shape[0], spinors.shape[2]
    total = bands * lax.axis_size("ka")
    size = lax.axis_size("brick")
    near_pairs = [(i, i ^ 1) for i in range(size) if i ^ 1 < size]
    far_pairs = [(i, j) for i in range(size) for j in [((i + 1) ^ 1) - 1] if 0 <= j < size]
    x = rows_view(spinors)
    core, local = rows_view(core_density), rows_view(local_potential)
    sizes = chunk_sizes(bands)
    starts = [sum(sizes[:k]) for k in range(len(sizes))]

    swap = lambda face: (lax.ppermute(face[0], "brick", near_pairs), lax.ppermute(face[1], "brick", far_pairs))
    faces = edges(x, planes, [(0, sizes[0])], (), VMEM_LIMIT)
    halos = [swap(faces[0])]
    density, others = front(x, kpt_mult, occupied, total, planes, sizes[1:], faces[0][:1])
    faces += others
    halos += [swap(face) for face in faces[1:2]]
    potential = potential_of(lax.psum(density, "ka"), core, local)
    out, token = None, ()
    for k, start in enumerate(starts):
        if k + 2 < len(starts):
            halos.append(swap(gate(*faces[k + 2], halos[k] + token)))
        out, done = apply_bands(x, potential, *halos[k], planes, start, out)
        token = (done,)
    return planes_view(out, planes)


def solution(mesh):
    placed = (P("ka", None, "brick", None), P("ka"), P("ka"), P("brick", None), P("brick", None))
    return jax.shard_map(
        shards, mesh=mesh, in_specs=placed, out_specs=P("ka", None, "brick", None), check_vma=False
    )
```

```python
import functools
import math

import jax
import jax.numpy as jnp
from jax import lax
from jax.experimental import pallas as pl
from jax.experimental.pallas import tpu as pltpu
from jax.sharding import PartitionSpec as P

NY = 192
LANES = 128
SUB = 8
TRIPLE = 3
HALF = 2 * NY - 2 * LANES - LANES // 2
PACK = 16
FLOOR_FRACTION = 0.05
VMEM_LIMIT = 63 * 1024 * 1024
SMALL = pl.CostEstimate(flops=0, bytes_accessed=0, transcendentals=0)


def rows_view(x):
    lead, planes, cells = x.shape[:-2], x.shape[-2], x.shape[-1]
    tiles = cells // LANES
    n = len(lead)
    x = x.reshape(lead + (planes, tiles, LANES))
    x = x.transpose(tuple(range(n)) + (n + 1, n, n + 2))
    return x.reshape(lead + (tiles * planes, LANES))


def planes_view(x, planes):
    lead, rows = x.shape[:-2], x.shape[-2]
    tiles = rows // planes
    n = len(lead)
    x = x.reshape(lead + (tiles, planes, LANES))
    x = x.transpose(tuple(range(n)) + (n + 1, n, n + 2))
    return x.reshape(lead + (planes, tiles * LANES))


def even_brick():
    return lax.axis_index("brick") % 2 == 0


def spread_matrix(back):
    size = SUB * PACK
    row = lax.broadcasted_iota(jnp.int32, (size, size), 0)
    column = lax.broadcasted_iota(jnp.int32, (size, size), 1)
    if back:
        row, column = column, row
    return (column == (row % SUB) * PACK + row // SUB).astype(jnp.bfloat16)


def gathered(read, segment, i):
    return jnp.concatenate(
        [read(pl.ds(s * segment + i * PACK, PACK)) for s in range(SUB)], axis=0
    )


def product(matrix, values):
    return jnp.dot(matrix, values, preferred_element_type=jnp.float32)


def face_matrix(planes):
    out = PACK // planes * SUB
    row = lax.broadcasted_iota(jnp.int32, (2 * out, SUB * PACK), 0)
    column = lax.broadcasted_iota(jnp.int32, (2 * out, SUB * PACK), 1)
    upper = (row < out) == even_brick()
    inner = row % out
    wanted = (inner % SUB) * PACK + (inner // SUB) * planes + jnp.where(upper, planes - 1, 0)
    return (column == wanted).astype(jnp.bfloat16), out


def gate(near, far, after):
    anywhere = pl.BlockSpec(memory_space=pl.ANY)
    return pl.pallas_call(
        lambda *refs: None,
        in_specs=[anywhere] * (2 + len(after)),
        out_specs=[anywhere, anywhere],
        out_shape=[jax.ShapeDtypeStruct(a.shape, a.dtype) for a in (near, far)],
        input_output_aliases={0: 0, 1: 1},
        compiler_params=pltpu.CompilerParams(vmem_limit_bytes=VMEM_LIMIT),
        name="gate",
    )(near, far, *after)


def front_body(planes, scale, counts, mult_ref, occ_ref, x_ref, *refs):
    bands = x_ref.shape[0]
    density_ref, faces = refs[-1 - 2 * len(counts)], refs[len(refs) - 2 * len(counts) :]
    weights = [(mult_ref[b] * occ_ref[b]).astype(jnp.float32) * scale for b in range(bands)]
    for s in range(SUB):
        up = down = real = imag = None
        for b in range(bands):
            ur, ui, dr, di = (x_ref[b, c, s].astype(jnp.float32) for c in range(4))
            wur, wui = weights[b] * ur, weights[b] * ui
            wdr, wdi = weights[b] * dr, weights[b] * di
            terms = (
                wur * ur + wui * ui,
                wdr * dr + wdi * di,
                wur * dr + wui * di,
                wur * di - wui * dr,
            )
            if b == 0:
                up, down, real, imag = terms
            else:
                up, down, real, imag = up + terms[0], down + terms[1], real + terms[2], imag + terms[3]
        density_ref[0, s] = (up + down).astype(jnp.bfloat16)
        density_ref[1, s] = (2.0 * real).astype(jnp.bfloat16)
        density_ref[2, s] = (2.0 * imag).astype(jnp.bfloat16)
        density_ref[3, s] = (up - down).astype(jnp.bfloat16)
    select, out = face_matrix(planes)
    band = 0
    for k, count in enumerate(counts):
        for b in range(count):
            block = jnp.concatenate(
                [x_ref[band, c].reshape(SUB * PACK, LANES) for c in range(4)], axis=1
            )
            picked = product(select, block).astype(jnp.bfloat16)
            for c in range(4):
                lanes = slice(c * LANES, (c + 1) * LANES)
                faces[2 * k][b, c] = picked[:out, lanes]
                faces[2 * k + 1][b, c] = picked[out:, lanes]
            band += 1


def front(x, mult, occ, total, planes, counts):
    bands, rows = x.shape[0], x.shape[2]
    segment = rows // SUB
    out = PACK // planes * SUB
    results = pl.pallas_call(
        functools.partial(front_body, planes, 1.0 / (2.0 * total), counts),
        grid=(segment // PACK,),
        in_specs=[
            pl.BlockSpec(memory_space=pltpu.SMEM),
            pl.BlockSpec(memory_space=pltpu.SMEM),
            pl.BlockSpec((bands, 4, SUB, PACK, LANES), lambda i: (0, 0, 0, i, 0)),
        ],
        out_specs=[pl.BlockSpec((4, SUB, PACK, LANES), lambda i: (0, 0, i, 0))]
        + [pl.BlockSpec((count, 4, out, LANES), lambda i: (0, 0, i, 0)) for count in counts for _ in range(2)],
        out_shape=[jax.ShapeDtypeStruct((4, SUB, segment, LANES), jnp.bfloat16)]
        + [
            jax.ShapeDtypeStruct((count, 4, rows // planes, LANES), jnp.bfloat16)
            for count in counts
            for _ in range(2)
        ],
        compiler_params=pltpu.CompilerParams(vmem_limit_bytes=VMEM_LIMIT),
        cost_estimate=SMALL,
        name="front",
    )(mult, occ, x.reshape(bands, 4, SUB, segment, LANES))
    return results[0].reshape(4, rows, LANES), [tuple(results[1 + 2 * k : 3 + 2 * k]) for k in range(len(counts))]


def add_body(a_ref, b_ref, *refs):
    out_ref = refs[-1]
    out_ref[...] = (a_ref[...].astype(jnp.float32) + b_ref[...].astype(jnp.float32)).astype(jnp.bfloat16)


def add(a, b, after):
    whole = pl.BlockSpec(memory_space=pltpu.VMEM)
    return pl.pallas_call(
        add_body,
        in_specs=[whole, whole] + [pl.BlockSpec(memory_space=pl.ANY)] * len(after),
        out_shape=jax.ShapeDtypeStruct(a.shape, a.dtype),
        compiler_params=pltpu.CompilerParams(vmem_limit_bytes=VMEM_LIMIT),
        cost_estimate=SMALL,
        name="add",
    )(a, b, *after)


def cube_root(x):
    root = jnp.exp(jnp.log(jnp.abs(x)) * (1.0 / 3.0))
    return jnp.where(x < 0.0, -root, root)


def potential_body(rows, d_ref, e_ref, core_ref, local_ref, out_ref):
    segment = rows // SUB
    spread = spread_matrix(False)

    def step(i, unused):
        block = jnp.concatenate(
            [gathered(lambda at: d_ref[f, at, :], segment, i) for f in range(4)]
            + [gathered(lambda at: e_ref[f, at, :], segment, i) for f in range(4)],
            axis=1,
        )
        fields = product(spread, block)
        d0, d1, d2, d3 = (
            fields[:, f * LANES : (f + 1) * LANES] + fields[:, (f + 4) * LANES : (f + 5) * LANES] for f in range(4)
        )
        here = [pl.ds(i * PACK + r, SUB, stride=segment) for r in range(PACK)]
        core = jnp.concatenate([core_ref[at, :] for at in here], axis=0)
        local = jnp.concatenate([local_ref[at, :] for at in here], axis=0)
        electrons = d0 + core
        magnitude = jnp.sqrt(d1 * d1 + d2 * d2 + d3 * d3)
        upper = -cube_root((3.0 / math.pi) * (electrons + magnitude))
        lower = -cube_root((3.0 / math.pi) * (electrons - magnitude))
        factor = 0.5 * (upper - lower) / jnp.maximum(magnitude, FLOOR_FRACTION * electrons)
        v = 0.5 * (upper + lower) + local
        bz = factor * d3
        at = pl.ds(i * PACK, PACK)
        shape = (PACK, SUB, LANES)
        out_ref[0, at] = (v + bz + 3.0).reshape(shape)
        out_ref[1, at] = (factor * d1).reshape(shape)
        out_ref[2, at] = (factor * d2).reshape(shape)
        out_ref[3, at] = (v - bz + 3.0).reshape(shape)
        return unused

    lax.fori_loop(0, segment // PACK, step, 0, unroll=True)


def potential_of(density, other, core, local):
    rows = density.shape[1]
    whole = pl.BlockSpec(memory_space=pltpu.VMEM)
    return pl.pallas_call(
        functools.partial(potential_body, rows),
        in_specs=[whole, whole, whole, whole],
        out_specs=whole,
        out_shape=jax.ShapeDtypeStruct((4, rows // SUB, SUB, LANES), jnp.float32),
        compiler_params=pltpu.CompilerParams(vmem_limit_bytes=VMEM_LIMIT),
        cost_estimate=SMALL,
        name="potential",
    )(density, other, core, local)


def apply_body(planes, rows, x_ref, pot_ref, near_ref, far_ref, carry_ref, out_ref, token_ref, wide, ends, turned, flat):
    segment = rows // SUB
    stride = planes * TRIPLE
    steps = segment // stride
    near_slot = jnp.where(even_brick(), 1, 0)
    spread, unspread = spread_matrix(False), spread_matrix(True)

    for c in range(4):
        ends[near_slot, c] = near_ref[0, c].astype(jnp.float32).reshape(ends.shape[2:])
        ends[1 - near_slot, c] = far_ref[0, c].astype(jnp.float32).reshape(ends.shape[2:])

    def load(i, unused):
        block = jnp.concatenate([gathered(lambda at: x_ref[0, c, at, :], segment, i) for c in range(4)], axis=1)
        values = product(spread, block)
        for c in range(4):
            part = values[:, c * LANES : (c + 1) * LANES]
            wide[c, pl.ds(i * PACK, PACK)] = part.reshape(PACK, SUB, LANES)
            turned[c, pl.ds(stride + i * PACK, PACK)] = pltpu.roll(part, HALF, 1).reshape(PACK, SUB, LANES)
        return unused

    lax.fori_loop(0, segment // PACK, load, 0, unroll=True)
    for c in range(4):
        for q in range(stride):
            turned[c, q] = pltpu.roll(turned[c, segment + q], 1, 0)
            turned[c, segment + stride + q] = pltpu.roll(turned[c, stride + q], SUB - 1, 0)

    lane = lax.broadcasted_iota(jnp.int32, (SUB, LANES), 1)
    low = lane < HALF
    initial, final = lane == 0, lane == LANES - 1
    inner_initial, inner_final = lane == HALF, lane == HALF - 1

    def neighbours(c, plane, j):
        spot = [j * stride + tile * planes + plane for tile in range(TRIPLE)]
        v0, v1, v2 = (wide[c, at] for at in spot)
        r0, r1, r2 = (turned[c, at + stride] for at in spot)
        after0 = r0 + turned[c, spot[0] + 2 * stride]
        after1 = r1 + turned[c, spot[1] + 2 * stride]
        before1 = r1 + turned[c, spot[1]]
        before2 = r2 + turned[c, spot[2]]
        across = (
            jnp.where(low, before1, before2),
            jnp.where(low, before2, after0),
            jnp.where(low, after0, after1),
        )
        plus = (
            jnp.where(initial, v1, v0),
            jnp.where(inner_initial, r0, jnp.where(initial, v2, v1)),
            jnp.where(initial, r1, v2),
        )
        minus = (
            jnp.where(final, r1, v0),
            jnp.where(inner_final, r2, jnp.where(final, v0, v1)),
            jnp.where(final, v1, v2),
        )
        sums = []
        for tile in range(TRIPLE):
            below = ends[0, c, j * TRIPLE + tile] if plane == 0 else wide[c, spot[tile] - 1]
            above = ends[1, c, j * TRIPLE + tile] if plane == planes - 1 else wide[c, spot[tile] + 1]
            along = pltpu.roll(plus[tile], LANES - 1, 1) + pltpu.roll(minus[tile], 1, 1)
            sums.append((across[tile] + along) + (below + above))
        return (v0, v1, v2), sums

    def step(j, unused):
        for plane in range(planes):
            (ur, nur), (ui, nui), (dr, ndr), (di, ndi) = (neighbours(c, plane, j) for c in range(4))
            for tile in range(TRIPLE):
                spot = j * stride + tile * planes + plane
                diag_up, bx, by, diag_down = (pot_ref[f, spot] for f in range(4))
                a, b, e, f = ur[tile], ui[tile], dr[tile], di[tile]
                flat[0, spot] = diag_up * a + bx * e + by * f - 0.5 * nur[tile]
                flat[1, spot] = diag_up * b + bx * f - by * e - 0.5 * nui[tile]
                flat[2, spot] = bx * a - by * b + diag_down * e - 0.5 * ndr[tile]
                flat[3, spot] = bx * b + by * a + diag_down * f - 0.5 * ndi[tile]
        return unused

    lax.fori_loop(0, steps, step, 0)

    def store(i, unused):
        at = pl.ds(i * PACK, PACK)
        block = jnp.concatenate([flat[c, at].reshape(PACK * SUB, LANES) for c in range(4)], axis=1)
        values = product(unspread, block.astype(jnp.bfloat16)).astype(jnp.bfloat16)
        for c in range(4):
            for s in range(SUB):
                out_ref[0, c, pl.ds(pl.multiple_of(s * segment + i * PACK, PACK), PACK), :] = values[
                    s * PACK : (s + 1) * PACK, c * LANES : (c + 1) * LANES
                ]
        return unused

    lax.fori_loop(0, segment // PACK, store, 0, unroll=True)


def apply_bands(x, potential, near, far, planes, start, carry):
    count, rows = near.shape[0], x.shape[2]
    segment = rows // SUB
    stride = planes * TRIPLE
    tiles = rows // planes
    halo = pl.BlockSpec((1, 4, tiles, LANES), lambda b: (b, 0, 0, 0))
    body = functools.partial(apply_body, planes, rows)
    in_specs = [
        pl.BlockSpec((1, 4, rows, LANES), lambda b: (start + b, 0, 0, 0)),
        pl.BlockSpec((4, segment, SUB, LANES), lambda b: (0, 0, 0, 0)),
        halo,
        halo,
    ]
    operands = [x, potential, near, far]
    aliases = {}
    if carry is not None:
        in_specs.append(pl.BlockSpec(memory_space=pl.ANY))
        operands.append(carry)
        aliases = {4: 0}
        call = body
    else:

        def call(x_ref, pot_ref, near_ref, far_ref, *rest):
            body(x_ref, pot_ref, near_ref, far_ref, None, *rest)

    return pl.pallas_call(
        call,
        grid=(count,),
        in_specs=in_specs,
        out_specs=[
            pl.BlockSpec((1, 4, rows, LANES), lambda b: (start + b, 0, 0, 0)),
            pl.BlockSpec(memory_space=pl.ANY),
        ],
        out_shape=[
            jax.ShapeDtypeStruct(x.shape, jnp.bfloat16),
            jax.ShapeDtypeStruct((SUB, LANES), jnp.float32),
        ],
        input_output_aliases=aliases,
        scratch_shapes=[
            pltpu.VMEM((4, segment, SUB, LANES), jnp.float32),
            pltpu.VMEM((2, 4, tiles // SUB, SUB, LANES), jnp.float32),
            pltpu.VMEM((4, segment + 2 * stride, SUB, LANES), jnp.float32),
            pltpu.VMEM((4, segment, SUB, LANES), jnp.float32),
        ],
        compiler_params=pltpu.CompilerParams(vmem_limit_bytes=VMEM_LIMIT),
        cost_estimate=SMALL,
        name="apply",
    )(*operands)


def chunk_sizes(bands):
    return [2] * (bands // 2) + [1] * (bands % 2)


def group_sum(partial, after):
    size = lax.axis_size("ka")
    if size & (size - 1) or size == 1:
        whole = lax.psum(partial, "ka")
        return whole, jnp.zeros_like(whole)
    step = 1
    while True:
        other = lax.ppermute(partial, "ka", [(i, i ^ step) for i in range(size)])
        step *= 2
        if step == size:
            return partial, other
        partial = add(partial, other, after)


def shards(spinors, kpt_mult, occupied, core_density, local_potential):
    bands, planes = spinors.shape[0], spinors.shape[2]
    total = bands * lax.axis_size("ka")
    size = lax.axis_size("brick")
    near_pairs = [(i, i ^ 1) for i in range(size) if i ^ 1 < size]
    far_pairs = [(i, j) for i in range(size) for j in [((i + 1) ^ 1) - 1] if 0 <= j < size]
    x = rows_view(spinors)
    core, local = rows_view(core_density), rows_view(local_potential)
    sizes = chunk_sizes(bands)
    starts = [sum(sizes[:k]) for k in range(len(sizes))]

    swap = lambda face: (lax.ppermute(face[0], "brick", near_pairs), lax.ppermute(face[1], "brick", far_pairs))
    density, faces = front(x, kpt_mult, occupied, total, planes, sizes)
    halos = [swap(face) for face in faces[:2]]
    own, other = group_sum(density, ())
    potential = potential_of(own, other, core, local)
    out, token = None, ()
    for k, start in enumerate(starts):
        if k + 2 < len(starts):
            halos.append(swap(gate(*faces[k + 2], halos[k] + token)))
        out, done = apply_bands(x, potential, *halos[k], planes, start, out)
        token = (done,)
    return planes_view(out, planes)


def solution(mesh):
    placed = (P("ka", None, "brick", None), P("ka"), P("ka"), P("brick", None), P("brick", None))
    return jax.shard_map(
        shards, mesh=mesh, in_specs=placed, out_specs=P("ka", None, "brick", None), check_vma=False
    )
```

```python
import functools
import math

import jax
import jax.numpy as jnp
from jax import lax
from jax.experimental import pallas as pl
from jax.experimental.pallas import tpu as pltpu
from jax.sharding import PartitionSpec as P

NY = 192
LANES = 128
SUB = 8
TRIPLE = 3
HALF = 2 * NY - 2 * LANES - LANES // 2
PACK = 16
FLOOR_FRACTION = 0.05
VMEM_LIMIT = 63 * 1024 * 1024
SMALL = pl.CostEstimate(flops=0, bytes_accessed=0, transcendentals=0)


def rows_view(x):
    lead, planes, cells = x.shape[:-2], x.shape[-2], x.shape[-1]
    tiles = cells // LANES
    n = len(lead)
    x = x.reshape(lead + (planes, tiles, LANES))
    x = x.transpose(tuple(range(n)) + (n + 1, n, n + 2))
    return x.reshape(lead + (tiles * planes, LANES))


def planes_view(x, planes):
    lead, rows = x.shape[:-2], x.shape[-2]
    tiles = rows // planes
    n = len(lead)
    x = x.reshape(lead + (tiles, planes, LANES))
    x = x.transpose(tuple(range(n)) + (n + 1, n, n + 2))
    return x.reshape(lead + (planes, tiles * LANES))


def even_brick():
    return lax.axis_index("brick") % 2 == 0


def spread_matrix(back):
    size = SUB * PACK
    row = lax.broadcasted_iota(jnp.int32, (size, size), 0)
    column = lax.broadcasted_iota(jnp.int32, (size, size), 1)
    if back:
        row, column = column, row
    return (column == (row % SUB) * PACK + row // SUB).astype(jnp.bfloat16)


def gathered(read, segment, i):
    return jnp.concatenate(
        [read(pl.ds(s * segment + i * PACK, PACK)) for s in range(SUB)], axis=0
    )


def product(matrix, values):
    return jnp.dot(matrix, values, preferred_element_type=jnp.float32)


def face_matrix(planes):
    out = PACK // planes * SUB
    row = lax.broadcasted_iota(jnp.int32, (2 * out, SUB * PACK), 0)
    column = lax.broadcasted_iota(jnp.int32, (2 * out, SUB * PACK), 1)
    upper = (row < out) == even_brick()
    inner = row % out
    wanted = (inner % SUB) * PACK + (inner // SUB) * planes + jnp.where(upper, planes - 1, 0)
    return (column == wanted).astype(jnp.bfloat16), out


def edges_body(planes, chunks, x_ref, *refs):
    faces, held, sems = refs[-2 - 2 * len(chunks) : -2], refs[-2], refs[-1]
    first = chunks[0][0]
    bands = [(start - first + b, k, b) for k, (start, count) in enumerate(chunks) for b in range(count)]
    rows = held.shape[2]
    segment = rows // SUB
    copies = [pltpu.make_async_copy(x_ref.at[first + i], held.at[i], sems.at[i]) for i, _, _ in bands]
    for copy in copies:
        copy.start()
    select, out = face_matrix(planes)
    for i, k, b in bands:
        copies[i].wait()
        near_ref, far_ref = faces[2 * k], faces[2 * k + 1]
        for part in range(segment // PACK):
            block = jnp.concatenate(
                [gathered(lambda at: held[i, c, at, :], segment, part) for c in range(4)], axis=1
            )
            picked = product(select, block).astype(jnp.bfloat16)
            at = pl.ds(part * out, out)
            for c in range(4):
                lanes = slice(c * LANES, (c + 1) * LANES)
                near_ref[b, c, at, :] = picked[:out, lanes]
                far_ref[b, c, at, :] = picked[out:, lanes]


def edges(x, planes, chunks, after, limit):
    rows = x.shape[2]
    total = sum(count for _, count in chunks)
    shapes = [
        jax.ShapeDtypeStruct((count, 4, rows // planes, LANES), jnp.bfloat16) for _, count in chunks for _ in range(2)
    ]
    faces = pl.pallas_call(
        functools.partial(edges_body, planes, chunks),
        in_specs=[pl.BlockSpec(memory_space=pltpu.HBM)] + [pl.BlockSpec(memory_space=pl.ANY)] * len(after),
        out_shape=shapes,
        scratch_shapes=[pltpu.VMEM((total, 4, rows, LANES), jnp.bfloat16), pltpu.SemaphoreType.DMA((total,))],
        compiler_params=pltpu.CompilerParams(vmem_limit_bytes=limit),
        cost_estimate=SMALL,
        name="edges",
    )(x, *after)
    return [tuple(faces[2 * k : 2 * k + 2]) for k in range(len(chunks))]


def gate(near, far, after):
    anywhere = pl.BlockSpec(memory_space=pl.ANY)
    return pl.pallas_call(
        lambda *refs: None,
        in_specs=[anywhere] * (2 + len(after)),
        out_specs=[anywhere, anywhere],
        out_shape=[jax.ShapeDtypeStruct(a.shape, a.dtype) for a in (near, far)],
        input_output_aliases={0: 0, 1: 1},
        compiler_params=pltpu.CompilerParams(vmem_limit_bytes=VMEM_LIMIT),
        name="gate",
    )(near, far, *after)


def front_body(planes, scale, counts, mult_ref, occ_ref, x_ref, *refs):
    bands = x_ref.shape[0]
    density_ref, faces = refs[-1 - 2 * len(counts)], refs[len(refs) - 2 * len(counts) :]
    weights = [(mult_ref[b] * occ_ref[b]).astype(jnp.float32) * scale for b in range(bands)]
    for s in range(SUB):
        up = down = real = imag = None
        for b in range(bands):
            ur, ui, dr, di = (x_ref[b, c, s].astype(jnp.float32) for c in range(4))
            wur, wui = weights[b] * ur, weights[b] * ui
            wdr, wdi = weights[b] * dr, weights[b] * di
            terms = (
                wur * ur + wui * ui,
                wdr * dr + wdi * di,
                wur * dr + wui * di,
                wur * di - wui * dr,
            )
            if b == 0:
                up, down, real, imag = terms
            else:
                up, down, real, imag = up + terms[0], down + terms[1], real + terms[2], imag + terms[3]
        density_ref[0, s] = (up + down).astype(jnp.bfloat16)
        density_ref[1, s] = (2.0 * real).astype(jnp.bfloat16)
        density_ref[2, s] = (2.0 * imag).astype(jnp.bfloat16)
        density_ref[3, s] = (up - down).astype(jnp.bfloat16)
    if counts:
        select, out = face_matrix(planes)
    band = bands - sum(counts)
    for k, count in enumerate(counts):
        for b in range(count):
            block = jnp.concatenate(
                [x_ref[band, c].reshape(SUB * PACK, LANES) for c in range(4)], axis=1
            )
            picked = product(select, block).astype(jnp.bfloat16)
            for c in range(4):
                lanes = slice(c * LANES, (c + 1) * LANES)
                faces[2 * k][b, c] = picked[:out, lanes]
                faces[2 * k + 1][b, c] = picked[out:, lanes]
            band += 1


def front(x, mult, occ, total, planes, counts, after):
    bands, rows = x.shape[0], x.shape[2]
    segment = rows // SUB
    out = PACK // planes * SUB
    anywhere = pl.BlockSpec(memory_space=pl.ANY)
    results = pl.pallas_call(
        functools.partial(front_body, planes, 1.0 / (2.0 * total), counts),
        grid=(segment // PACK,),
        in_specs=[
            pl.BlockSpec(memory_space=pltpu.SMEM),
            pl.BlockSpec(memory_space=pltpu.SMEM),
            pl.BlockSpec((bands, 4, SUB, PACK, LANES), lambda i: (0, 0, 0, i, 0)),
        ]
        + [anywhere] * len(after),
        out_specs=[pl.BlockSpec((4, SUB, PACK, LANES), lambda i: (0, 0, i, 0))]
        + [pl.BlockSpec((count, 4, out, LANES), lambda i: (0, 0, i, 0)) for count in counts for _ in range(2)],
        out_shape=[jax.ShapeDtypeStruct((4, SUB, segment, LANES), jnp.bfloat16)]
        + [
            jax.ShapeDtypeStruct((count, 4, rows // planes, LANES), jnp.bfloat16)
            for count in counts
            for _ in range(2)
        ],
        compiler_params=pltpu.CompilerParams(vmem_limit_bytes=VMEM_LIMIT),
        cost_estimate=SMALL,
        name="front",
    )(mult, occ, x.reshape(bands, 4, SUB, segment, LANES), *after)
    return results[0].reshape(4, rows, LANES), [tuple(results[1 + 2 * k : 3 + 2 * k]) for k in range(len(counts))]


def cube_root(x):
    root = jnp.exp(jnp.log(jnp.abs(x)) * (1.0 / 3.0))
    return jnp.where(x < 0.0, -root, root)


def potential_body(rows, d_ref, core_ref, local_ref, out_ref):
    segment = rows // SUB
    spread = spread_matrix(False)

    def step(i, unused):
        block = jnp.concatenate([gathered(lambda at: d_ref[f, at, :], segment, i) for f in range(4)], axis=1)
        fields = product(spread, block)
        d0, d1, d2, d3 = (fields[:, f * LANES : (f + 1) * LANES] for f in range(4))
        here = [pl.ds(i * PACK + r, SUB, stride=segment) for r in range(PACK)]
        core = jnp.concatenate([core_ref[at, :] for at in here], axis=0)
        local = jnp.concatenate([local_ref[at, :] for at in here], axis=0)
        electrons = d0 + core
        magnitude = jnp.sqrt(d1 * d1 + d2 * d2 + d3 * d3)
        upper = -cube_root((3.0 / math.pi) * (electrons + magnitude))
        lower = -cube_root((3.0 / math.pi) * (electrons - magnitude))
        factor = 0.5 * (upper - lower) / jnp.maximum(magnitude, FLOOR_FRACTION * electrons)
        v = 0.5 * (upper + lower) + local
        bz = factor * d3
        at = pl.ds(i * PACK, PACK)
        shape = (PACK, SUB, LANES)
        out_ref[0, at] = (v + bz + 3.0).reshape(shape)
        out_ref[1, at] = (factor * d1).reshape(shape)
        out_ref[2, at] = (factor * d2).reshape(shape)
        out_ref[3, at] = (v - bz + 3.0).reshape(shape)
        return unused

    lax.fori_loop(0, segment // PACK, step, 0, unroll=True)


def potential_of(density, core, local):
    rows = density.shape[1]
    whole = pl.BlockSpec(memory_space=pltpu.VMEM)
    return pl.pallas_call(
        functools.partial(potential_body, rows),
        in_specs=[whole, whole, whole],
        out_specs=whole,
        out_shape=jax.ShapeDtypeStruct((4, rows // SUB, SUB, LANES), jnp.float32),
        compiler_params=pltpu.CompilerParams(vmem_limit_bytes=VMEM_LIMIT),
        cost_estimate=SMALL,
        name="potential",
    )(density, core, local)


def apply_body(planes, rows, x_ref, pot_ref, near_ref, far_ref, carry_ref, out_ref, token_ref, wide, ends, turned, flat):
    segment = rows // SUB
    stride = planes * TRIPLE
    steps = segment // stride
    near_slot = jnp.where(even_brick(), 1, 0)
    spread, unspread = spread_matrix(False), spread_matrix(True)

    for c in range(4):
        ends[near_slot, c] = near_ref[0, c].astype(jnp.float32).reshape(ends.shape[2:])
        ends[1 - near_slot, c] = far_ref[0, c].astype(jnp.float32).reshape(ends.shape[2:])

    def load(i, unused):
        block = jnp.concatenate([gathered(lambda at: x_ref[0, c, at, :], segment, i) for c in range(4)], axis=1)
        values = product(spread, block)
        for c in range(4):
            part = values[:, c * LANES : (c + 1) * LANES]
            wide[c, pl.ds(i * PACK, PACK)] = part.reshape(PACK, SUB, LANES)
            turned[c, pl.ds(stride + i * PACK, PACK)] = pltpu.roll(part, HALF, 1).reshape(PACK, SUB, LANES)
        return unused

    lax.fori_loop(0, segment // PACK, load, 0, unroll=True)
    for c in range(4):
        for q in range(stride):
            turned[c, q] = pltpu.roll(turned[c, segment + q], 1, 0)
            turned[c, segment + stride + q] = pltpu.roll(turned[c, stride + q], SUB - 1, 0)

    lane = lax.broadcasted_iota(jnp.int32, (SUB, LANES), 1)
    low = lane < HALF
    initial, final = lane == 0, lane == LANES - 1
    inner_initial, inner_final = lane == HALF, lane == HALF - 1

    def neighbours(c, plane, j):
        spot = [j * stride + tile * planes + plane for tile in range(TRIPLE)]
        v0, v1, v2 = (wide[c, at] for at in spot)
        r0, r1, r2 = (turned[c, at + stride] for at in spot)
        after0 = r0 + turned[c, spot[0] + 2 * stride]
        after1 = r1 + turned[c, spot[1] + 2 * stride]
        before1 = r1 + turned[c, spot[1]]
        before2 = r2 + turned[c, spot[2]]
        across = (
            jnp.where(low, before1, before2),
            jnp.where(low, before2, after0),
            jnp.where(low, after0, after1),
        )
        plus = (
            jnp.where(initial, v1, v0),
            jnp.where(inner_initial, r0, jnp.where(initial, v2, v1)),
            jnp.where(initial, r1, v2),
        )
        minus = (
            jnp.where(final, r1, v0),
            jnp.where(inner_final, r2, jnp.where(final, v0, v1)),
            jnp.where(final, v1, v2),
        )
        sums = []
        for tile in range(TRIPLE):
            below = ends[0, c, j * TRIPLE + tile] if plane == 0 else wide[c, spot[tile] - 1]
            above = ends[1, c, j * TRIPLE + tile] if plane == planes - 1 else wide[c, spot[tile] + 1]
            along = pltpu.roll(plus[tile], LANES - 1, 1) + pltpu.roll(minus[tile], 1, 1)
            sums.append((across[tile] + along) + (below + above))
        return (v0, v1, v2), sums

    def step(j, unused):
        for plane in range(planes):
            (ur, nur), (ui, nui), (dr, ndr), (di, ndi) = (neighbours(c, plane, j) for c in range(4))
            for tile in range(TRIPLE):
                spot = j * stride + tile * planes + plane
                diag_up, bx, by, diag_down = (pot_ref[f, spot] for f in range(4))
                a, b, e, f = ur[tile], ui[tile], dr[tile], di[tile]
                flat[0, spot] = diag_up * a + bx * e + by * f - 0.5 * nur[tile]
                flat[1, spot] = diag_up * b + bx * f - by * e - 0.5 * nui[tile]
                flat[2, spot] = bx * a - by * b + diag_down * e - 0.5 * ndr[tile]
                flat[3, spot] = bx * b + by * a + diag_down * f - 0.5 * ndi[tile]
        return unused

    lax.fori_loop(0, steps, step, 0)

    def store(i, unused):
        at = pl.ds(i * PACK, PACK)
        block = jnp.concatenate([flat[c, at].reshape(PACK * SUB, LANES) for c in range(4)], axis=1)
        values = product(unspread, block.astype(jnp.bfloat16)).astype(jnp.bfloat16)
        for c in range(4):
            for s in range(SUB):
                out_ref[0, c, pl.ds(pl.multiple_of(s * segment + i * PACK, PACK), PACK), :] = values[
                    s * PACK : (s + 1) * PACK, c * LANES : (c + 1) * LANES
                ]
        return unused

    lax.fori_loop(0, segment // PACK, store, 0, unroll=True)


def apply_bands(x, potential, near, far, planes, start, carry):
    count, rows = near.shape[0], x.shape[2]
    segment = rows // SUB
    stride = planes * TRIPLE
    tiles = rows // planes
    halo = pl.BlockSpec((1, 4, tiles, LANES), lambda b: (b, 0, 0, 0))
    body = functools.partial(apply_body, planes, rows)
    in_specs = [
        pl.BlockSpec((1, 4, rows, LANES), lambda b: (start + b, 0, 0, 0)),
        pl.BlockSpec((4, segment, SUB, LANES), lambda b: (0, 0, 0, 0)),
        halo,
        halo,
    ]
    operands = [x, potential, near, far]
    aliases = {}
    if carry is not None:
        in_specs.append(pl.BlockSpec(memory_space=pl.ANY))
        operands.append(carry)
        aliases = {4: 0}
        call = body
    else:

        def call(x_ref, pot_ref, near_ref, far_ref, *rest):
            body(x_ref, pot_ref, near_ref, far_ref, None, *rest)

    return pl.pallas_call(
        call,
        grid=(count,),
        in_specs=in_specs,
        out_specs=[
            pl.BlockSpec((1, 4, rows, LANES), lambda b: (start + b, 0, 0, 0)),
            pl.BlockSpec(memory_space=pl.ANY),
        ],
        out_shape=[
            jax.ShapeDtypeStruct(x.shape, jnp.bfloat16),
            jax.ShapeDtypeStruct((SUB, LANES), jnp.float32),
        ],
        input_output_aliases=aliases,
        scratch_shapes=[
            pltpu.VMEM((4, segment, SUB, LANES), jnp.float32),
            pltpu.VMEM((2, 4, tiles // SUB, SUB, LANES), jnp.float32),
            pltpu.VMEM((4, segment + 2 * stride, SUB, LANES), jnp.float32),
            pltpu.VMEM((4, segment, SUB, LANES), jnp.float32),
        ],
        compiler_params=pltpu.CompilerParams(vmem_limit_bytes=VMEM_LIMIT),
        cost_estimate=SMALL,
        name="apply",
    )(*operands)


def chunk_sizes(bands):
    return [2] * (bands // 2) + [1] * (bands % 2)


def sum_body(parts_ref, out_ref):
    total = parts_ref[0].astype(jnp.float32)
    for k in range(1, parts_ref.shape[0]):
        total = total + parts_ref[k].astype(jnp.float32)
    total = total.astype(jnp.bfloat16)
    for k in range(out_ref.shape[0]):
        out_ref[k] = total


def group_sum(partial):
    size = lax.axis_size("ka")
    fields, rows = partial.shape[:2]
    parts = partial.reshape(fields * size, rows // size, LANES)
    parts = lax.all_to_all(parts.reshape(size, -1, LANES), "ka", 0, 0)
    copies = pl.pallas_call(
        sum_body,
        in_specs=[pl.BlockSpec(memory_space=pltpu.VMEM)],
        out_specs=pl.BlockSpec(memory_space=pltpu.VMEM),
        out_shape=jax.ShapeDtypeStruct(parts.shape, parts.dtype),
        compiler_params=pltpu.CompilerParams(vmem_limit_bytes=VMEM_LIMIT),
        cost_estimate=SMALL,
        name="sum",
    )(parts)
    return lax.all_to_all(copies, "ka", 0, 0).reshape(partial.shape)


def shards(spinors, kpt_mult, occupied, core_density, local_potential):
    bands, planes = spinors.shape[0], spinors.shape[2]
    total = bands * lax.axis_size("ka")
    size = lax.axis_size("brick")
    near_pairs = [(i, i ^ 1) for i in range(size) if i ^ 1 < size]
    far_pairs = [(i, j) for i in range(size) for j in [((i + 1) ^ 1) - 1] if 0 <= j < size]
    x = rows_view(spinors)
    core, local = rows_view(core_density), rows_view(local_potential)
    sizes = chunk_sizes(bands)
    starts = [sum(sizes[:k]) for k in range(len(sizes))]

    swap = lambda face: (lax.ppermute(face[0], "brick", near_pairs), lax.ppermute(face[1], "brick", far_pairs))
    faces = edges(x, planes, [(0, sizes[0])], (), VMEM_LIMIT)
    halos = [swap(faces[0])]
    density, others = front(x, kpt_mult, occupied, total, planes, sizes[1:], faces[0])
    faces += others
    halos += [swap(face) for face in faces[1:2]]
    potential = potential_of(group_sum(density), core, local)
    out, token = None, ()
    for k, start in enumerate(starts):
        if k + 2 < len(starts):
            halos.append(swap(gate(*faces[k + 2], halos[k] + token)))
        out, done = apply_bands(x, potential, *halos[k], planes, start, out)
        token = (done,)
    return planes_view(out, planes)


def solution(mesh):
    placed = (P("ka", None, "brick", None), P("ka"), P("ka"), P("brick", None), P("brick", None))
    return jax.shard_map(
        shards, mesh=mesh, in_specs=placed, out_specs=P("ka", None, "brick", None), check_vma=False
    )
```

```python
import functools
import math

import jax
import jax.numpy as jnp
from jax import lax
from jax.experimental import pallas as pl
from jax.experimental.pallas import tpu as pltpu
from jax.sharding import PartitionSpec as P

NY = 192
LANES = 128
SUB = 8
TRIPLE = 3
HALF = 2 * NY - 2 * LANES - LANES // 2
PACK = 16
FLOOR_FRACTION = 0.05
VMEM_LIMIT = 63 * 1024 * 1024
SMALL = pl.CostEstimate(flops=0, bytes_accessed=0, transcendentals=0)


def rows_view(x):
    lead, planes, cells = x.shape[:-2], x.shape[-2], x.shape[-1]
    tiles = cells // LANES
    n = len(lead)
    x = x.reshape(lead + (planes, tiles, LANES))
    x = x.transpose(tuple(range(n)) + (n + 1, n, n + 2))
    return x.reshape(lead + (tiles * planes, LANES))


def planes_view(x, planes):
    lead, rows = x.shape[:-2], x.shape[-2]
    tiles = rows // planes
    n = len(lead)
    x = x.reshape(lead + (tiles, planes, LANES))
    x = x.transpose(tuple(range(n)) + (n + 1, n, n + 2))
    return x.reshape(lead + (planes, tiles * LANES))


def even_brick():
    return lax.axis_index("brick") % 2 == 0


def spread_matrix(back):
    size = SUB * PACK
    row = lax.broadcasted_iota(jnp.int32, (size, size), 0)
    column = lax.broadcasted_iota(jnp.int32, (size, size), 1)
    if back:
        row, column = column, row
    return (column == (row % SUB) * PACK + row // SUB).astype(jnp.bfloat16)


def gathered(read, segment, i):
    return jnp.concatenate(
        [read(pl.ds(s * segment + i * PACK, PACK)) for s in range(SUB)], axis=0
    )


def product(matrix, values):
    return jnp.dot(matrix, values, preferred_element_type=jnp.float32)


def face_matrix(planes):
    out = PACK // planes * SUB
    row = lax.broadcasted_iota(jnp.int32, (2 * out, SUB * PACK), 0)
    column = lax.broadcasted_iota(jnp.int32, (2 * out, SUB * PACK), 1)
    upper = (row < out) == even_brick()
    inner = row % out
    wanted = (inner % SUB) * PACK + (inner // SUB) * planes + jnp.where(upper, planes - 1, 0)
    return (column == wanted).astype(jnp.bfloat16), out


def edges_body(planes, chunks, x_ref, *refs):
    faces, held, sems = refs[-2 - 2 * len(chunks) : -2], refs[-2], refs[-1]
    first = chunks[0][0]
    bands = [(start - first + b, k, b) for k, (start, count) in enumerate(chunks) for b in range(count)]
    rows = held.shape[2]
    segment = rows // SUB
    copies = [pltpu.make_async_copy(x_ref.at[first + i], held.at[i], sems.at[i]) for i, _, _ in bands]
    for copy in copies:
        copy.start()
    select, out = face_matrix(planes)
    for i, k, b in bands:
        copies[i].wait()
        near_ref, far_ref = faces[2 * k], faces[2 * k + 1]
        for part in range(segment // PACK):
            block = jnp.concatenate(
                [gathered(lambda at: held[i, c, at, :], segment, part) for c in range(4)], axis=1
            )
            picked = product(select, block).astype(jnp.bfloat16)
            at = pl.ds(part * out, out)
            for c in range(4):
                lanes = slice(c * LANES, (c + 1) * LANES)
                near_ref[b, c, at, :] = picked[:out, lanes]
                far_ref[b, c, at, :] = picked[out:, lanes]


def edges(x, planes, chunks, after, limit):
    rows = x.shape[2]
    total = sum(count for _, count in chunks)
    shapes = [
        jax.ShapeDtypeStruct((count, 4, rows // planes, LANES), jnp.bfloat16) for _, count in chunks for _ in range(2)
    ]
    faces = pl.pallas_call(
        functools.partial(edges_body, planes, chunks),
        in_specs=[pl.BlockSpec(memory_space=pltpu.HBM)] + [pl.BlockSpec(memory_space=pl.ANY)] * len(after),
        out_shape=shapes,
        scratch_shapes=[pltpu.VMEM((total, 4, rows, LANES), jnp.bfloat16), pltpu.SemaphoreType.DMA((total,))],
        compiler_params=pltpu.CompilerParams(vmem_limit_bytes=limit),
        cost_estimate=SMALL,
        name="edges",
    )(x, *after)
    return [tuple(faces[2 * k : 2 * k + 2]) for k in range(len(chunks))]


def gate(near, far, after):
    anywhere = pl.BlockSpec(memory_space=pl.ANY)
    return pl.pallas_call(
        lambda *refs: None,
        in_specs=[anywhere] * (2 + len(after)),
        out_specs=[anywhere, anywhere],
        out_shape=[jax.ShapeDtypeStruct(a.shape, a.dtype) for a in (near, far)],
        input_output_aliases={0: 0, 1: 1},
        compiler_params=pltpu.CompilerParams(vmem_limit_bytes=VMEM_LIMIT),
        name="gate",
    )(near, far, *after)


def front_body(planes, scale, counts, mult_ref, occ_ref, x_ref, *refs):
    bands = x_ref.shape[0]
    density_ref, faces = refs[-1 - 2 * len(counts)], refs[len(refs) - 2 * len(counts) :]
    weights = [(mult_ref[b] * occ_ref[b]).astype(jnp.float32) * scale for b in range(bands)]
    for s in range(SUB):
        up = down = real = imag = None
        for b in range(bands):
            ur, ui, dr, di = (x_ref[b, c, s].astype(jnp.float32) for c in range(4))
            wur, wui = weights[b] * ur, weights[b] * ui
            wdr, wdi = weights[b] * dr, weights[b] * di
            terms = (
                wur * ur + wui * ui,
                wdr * dr + wdi * di,
                wur * dr + wui * di,
                wur * di - wui * dr,
            )
            if b == 0:
                up, down, real, imag = terms
            else:
                up, down, real, imag = up + terms[0], down + terms[1], real + terms[2], imag + terms[3]
        density_ref[0, s] = (up + down).astype(jnp.bfloat16)
        density_ref[1, s] = (2.0 * real).astype(jnp.bfloat16)
        density_ref[2, s] = (2.0 * imag).astype(jnp.bfloat16)
        density_ref[3, s] = (up - down).astype(jnp.bfloat16)
    if counts:
        select, out = face_matrix(planes)
    band = bands - sum(counts)
    for k, count in enumerate(counts):
        for b in range(count):
            block = jnp.concatenate(
                [x_ref[band, c].reshape(SUB * PACK, LANES) for c in range(4)], axis=1
            )
            picked = product(select, block).astype(jnp.bfloat16)
            for c in range(4):
                lanes = slice(c * LANES, (c + 1) * LANES)
                faces[2 * k][b, c] = picked[:out, lanes]
                faces[2 * k + 1][b, c] = picked[out:, lanes]
            band += 1


def front(x, mult, occ, total, planes, counts, after):
    bands, rows = x.shape[0], x.shape[2]
    segment = rows // SUB
    out = PACK // planes * SUB
    anywhere = pl.BlockSpec(memory_space=pl.ANY)
    results = pl.pallas_call(
        functools.partial(front_body, planes, 1.0 / (2.0 * total), counts),
        grid=(segment // PACK,),
        in_specs=[
            pl.BlockSpec(memory_space=pltpu.SMEM),
            pl.BlockSpec(memory_space=pltpu.SMEM),
            pl.BlockSpec((bands, 4, SUB, PACK, LANES), lambda i: (0, 0, 0, i, 0)),
        ]
        + [anywhere] * len(after),
        out_specs=[pl.BlockSpec((4, SUB, PACK, LANES), lambda i: (0, 0, i, 0))]
        + [pl.BlockSpec((count, 4, out, LANES), lambda i: (0, 0, i, 0)) for count in counts for _ in range(2)],
        out_shape=[jax.ShapeDtypeStruct((4, SUB, segment, LANES), jnp.bfloat16)]
        + [
            jax.ShapeDtypeStruct((count, 4, rows // planes, LANES), jnp.bfloat16)
            for count in counts
            for _ in range(2)
        ],
        compiler_params=pltpu.CompilerParams(vmem_limit_bytes=VMEM_LIMIT),
        cost_estimate=SMALL,
        name="front",
    )(mult, occ, x.reshape(bands, 4, SUB, segment, LANES), *after)
    return results[0].reshape(4, rows, LANES), [tuple(results[1 + 2 * k : 3 + 2 * k]) for k in range(len(counts))]


def cube_root(x):
    root = jnp.exp(jnp.log(jnp.abs(x)) * (1.0 / 3.0))
    return jnp.where(x < 0.0, -root, root)


def potential_body(rows, d_ref, core_ref, local_ref, out_ref):
    segment = rows // SUB
    spread = spread_matrix(False)

    def step(i, unused):
        block = jnp.concatenate([gathered(lambda at: d_ref[f, at, :], segment, i) for f in range(4)], axis=1)
        fields = product(spread, block)
        d0, d1, d2, d3 = (fields[:, f * LANES : (f + 1) * LANES] for f in range(4))
        here = [pl.ds(i * PACK + r, SUB, stride=segment) for r in range(PACK)]
        core = jnp.concatenate([core_ref[at, :] for at in here], axis=0)
        local = jnp.concatenate([local_ref[at, :] for at in here], axis=0)
        electrons = d0 + core
        magnitude = jnp.sqrt(d1 * d1 + d2 * d2 + d3 * d3)
        upper = -cube_root((3.0 / math.pi) * (electrons + magnitude))
        lower = -cube_root((3.0 / math.pi) * (electrons - magnitude))
        factor = 0.5 * (upper - lower) / jnp.maximum(magnitude, FLOOR_FRACTION * electrons)
        v = 0.5 * (upper + lower) + local
        bz = factor * d3
        at = pl.ds(i * PACK, PACK)
        shape = (PACK, SUB, LANES)
        out_ref[0, at] = (v + bz + 3.0).reshape(shape)
        out_ref[1, at] = (factor * d1).reshape(shape)
        out_ref[2, at] = (factor * d2).reshape(shape)
        out_ref[3, at] = (v - bz + 3.0).reshape(shape)
        return unused

    lax.fori_loop(0, segment // PACK, step, 0, unroll=True)


def potential_of(density, core, local):
    rows = density.shape[1]
    whole = pl.BlockSpec(memory_space=pltpu.VMEM)
    return pl.pallas_call(
        functools.partial(potential_body, rows),
        in_specs=[whole, whole, whole],
        out_specs=whole,
        out_shape=jax.ShapeDtypeStruct((4, rows // SUB, SUB, LANES), jnp.float32),
        compiler_params=pltpu.CompilerParams(vmem_limit_bytes=VMEM_LIMIT),
        cost_estimate=SMALL,
        name="potential",
    )(density, core, local)


def apply_body(planes, rows, x_ref, pot_ref, near_ref, far_ref, carry_ref, out_ref, token_ref, wide, ends, turned, flat):
    segment = rows // SUB
    stride = planes * TRIPLE
    steps = segment // stride
    near_slot = jnp.where(even_brick(), 1, 0)
    spread, unspread = spread_matrix(False), spread_matrix(True)

    for c in range(4):
        ends[near_slot, c] = near_ref[0, c].astype(jnp.float32).reshape(ends.shape[2:])
        ends[1 - near_slot, c] = far_ref[0, c].astype(jnp.float32).reshape(ends.shape[2:])

    def load(i, unused):
        block = jnp.concatenate([gathered(lambda at: x_ref[0, c, at, :], segment, i) for c in range(4)], axis=1)
        values = product(spread, block)
        for c in range(4):
            part = values[:, c * LANES : (c + 1) * LANES]
            wide[c, pl.ds(i * PACK, PACK)] = part.reshape(PACK, SUB, LANES)
            turned[c, pl.ds(stride + i * PACK, PACK)] = pltpu.roll(part, HALF, 1).reshape(PACK, SUB, LANES)
        return unused

    lax.fori_loop(0, segment // PACK, load, 0, unroll=True)
    for c in range(4):
        for q in range(stride):
            turned[c, q] = pltpu.roll(turned[c, segment + q], 1, 0)
            turned[c, segment + stride + q] = pltpu.roll(turned[c, stride + q], SUB - 1, 0)

    lane = lax.broadcasted_iota(jnp.int32, (SUB, LANES), 1)
    low = lane < HALF
    initial, final = lane == 0, lane == LANES - 1
    inner_initial, inner_final = lane == HALF, lane == HALF - 1

    def neighbours(c, plane, j):
        spot = [j * stride + tile * planes + plane for tile in range(TRIPLE)]
        v0, v1, v2 = (wide[c, at] for at in spot)
        r0, r1, r2 = (turned[c, at + stride] for at in spot)
        after0 = r0 + turned[c, spot[0] + 2 * stride]
        after1 = r1 + turned[c, spot[1] + 2 * stride]
        before1 = r1 + turned[c, spot[1]]
        before2 = r2 + turned[c, spot[2]]
        across = (
            jnp.where(low, before1, before2),
            jnp.where(low, before2, after0),
            jnp.where(low, after0, after1),
        )
        plus = (
            jnp.where(initial, v1, v0),
            jnp.where(inner_initial, r0, jnp.where(initial, v2, v1)),
            jnp.where(initial, r1, v2),
        )
        minus = (
            jnp.where(final, r1, v0),
            jnp.where(inner_final, r2, jnp.where(final, v0, v1)),
            jnp.where(final, v1, v2),
        )
        sums = []
        for tile in range(TRIPLE):
            below = ends[0, c, j * TRIPLE + tile] if plane == 0 else wide[c, spot[tile] - 1]
            above = ends[1, c, j * TRIPLE + tile] if plane == planes - 1 else wide[c, spot[tile] + 1]
            along = pltpu.roll(plus[tile], LANES - 1, 1) + pltpu.roll(minus[tile], 1, 1)
            sums.append((across[tile] + along) + (below + above))
        return (v0, v1, v2), sums

    def step(j, unused):
        for plane in range(planes):
            (ur, nur), (ui, nui), (dr, ndr), (di, ndi) = (neighbours(c, plane, j) for c in range(4))
            for tile in range(TRIPLE):
                spot = j * stride + tile * planes + plane
                diag_up, bx, by, diag_down = (pot_ref[f, spot] for f in range(4))
                a, b, e, f = ur[tile], ui[tile], dr[tile], di[tile]
                flat[0, spot] = diag_up * a + bx * e + by * f - 0.5 * nur[tile]
                flat[1, spot] = diag_up * b + bx * f - by * e - 0.5 * nui[tile]
                flat[2, spot] = bx * a - by * b + diag_down * e - 0.5 * ndr[tile]
                flat[3, spot] = bx * b + by * a + diag_down * f - 0.5 * ndi[tile]
        return unused

    lax.fori_loop(0, steps, step, 0)

    def store(i, unused):
        at = pl.ds(i * PACK, PACK)
        block = jnp.concatenate([flat[c, at].reshape(PACK * SUB, LANES) for c in range(4)], axis=1)
        values = product(unspread, block.astype(jnp.bfloat16)).astype(jnp.bfloat16)
        for c in range(4):
            for s in range(SUB):
                out_ref[0, c, pl.ds(pl.multiple_of(s * segment + i * PACK, PACK), PACK), :] = values[
                    s * PACK : (s + 1) * PACK, c * LANES : (c + 1) * LANES
                ]
        return unused

    lax.fori_loop(0, segment // PACK, store, 0, unroll=True)


def apply_bands(x, potential, near, far, planes, start, carry):
    count, rows = near.shape[0], x.shape[2]
    segment = rows // SUB
    stride = planes * TRIPLE
    tiles = rows // planes
    halo = pl.BlockSpec((1, 4, tiles, LANES), lambda b: (b, 0, 0, 0))
    body = functools.partial(apply_body, planes, rows)
    in_specs = [
        pl.BlockSpec((1, 4, rows, LANES), lambda b: (start + b, 0, 0, 0)),
        pl.BlockSpec((4, segment, SUB, LANES), lambda b: (0, 0, 0, 0)),
        halo,
        halo,
    ]
    operands = [x, potential, near, far]
    aliases = {}
    if carry is not None:
        in_specs.append(pl.BlockSpec(memory_space=pl.ANY))
        operands.append(carry)
        aliases = {4: 0}
        call = body
    else:

        def call(x_ref, pot_ref, near_ref, far_ref, *rest):
            body(x_ref, pot_ref, near_ref, far_ref, None, *rest)

    return pl.pallas_call(
        call,
        grid=(count,),
        in_specs=in_specs,
        out_specs=[
            pl.BlockSpec((1, 4, rows, LANES), lambda b: (start + b, 0, 0, 0)),
            pl.BlockSpec(memory_space=pl.ANY),
        ],
        out_shape=[
            jax.ShapeDtypeStruct(x.shape, jnp.bfloat16),
            jax.ShapeDtypeStruct((SUB, LANES), jnp.float32),
        ],
        input_output_aliases=aliases,
        scratch_shapes=[
            pltpu.VMEM((4, segment, SUB, LANES), jnp.float32),
            pltpu.VMEM((2, 4, tiles // SUB, SUB, LANES), jnp.float32),
            pltpu.VMEM((4, segment + 2 * stride, SUB, LANES), jnp.float32),
            pltpu.VMEM((4, segment, SUB, LANES), jnp.float32),
        ],
        compiler_params=pltpu.CompilerParams(vmem_limit_bytes=VMEM_LIMIT),
        cost_estimate=SMALL,
        name="apply",
    )(*operands)


def chunk_sizes(bands):
    return [2] * (bands // 2) + [1] * (bands % 2)


def shards(spinors, kpt_mult, occupied, core_density, local_potential):
    bands, planes = spinors.shape[0], spinors.shape[2]
    total = bands * lax.axis_size("ka")
    size = lax.axis_size("brick")
    near_pairs = [(i, i ^ 1) for i in range(size) if i ^ 1 < size]
    far_pairs = [(i, j) for i in range(size) for j in [((i + 1) ^ 1) - 1] if 0 <= j < size]
    x = rows_view(spinors)
    core, local = rows_view(core_density), rows_view(local_potential)
    sizes = chunk_sizes(bands)
    starts = [sum(sizes[:k]) for k in range(len(sizes))]

    swap = lambda face: (lax.ppermute(face[0], "brick", near_pairs), lax.ppermute(face[1], "brick", far_pairs))
    faces = edges(x, planes, [(0, sizes[0])], (), VMEM_LIMIT)
    halos = [swap(faces[0])]
    density, others = front(x, kpt_mult, occupied, total, planes, sizes[1:], faces[0])
    faces += others
    halos += [swap(face) for face in faces[1:2]]
    density = lax.psum(density.astype(jnp.float32), "ka").astype(jnp.bfloat16)
    potential = potential_of(density, core, local)
    out, token = None, ()
    for k, start in enumerate(starts):
        if k + 2 < len(starts):
            halos.append(swap(gate(*faces[k + 2], halos[k] + token)))
        out, done = apply_bands(x, potential, *halos[k], planes, start, out)
        token = (done,)
    return planes_view(out, planes)


def solution(mesh):
    placed = (P("ka", None, "brick", None), P("ka"), P("ka"), P("brick", None), P("brick", None))
    return jax.shard_map(
        shards, mesh=mesh, in_specs=placed, out_specs=P("ka", None, "brick", None), check_vma=False
    )
```

```python
import functools
import math

import jax
import jax.numpy as jnp
from jax import lax
from jax.experimental import pallas as pl
from jax.experimental.pallas import tpu as pltpu
from jax.sharding import PartitionSpec as P

NY = 192
LANES = 128
SUB = 8
TRIPLE = 3
HALF = 2 * NY - 2 * LANES - LANES // 2
PACK = 16
FLOOR_FRACTION = 0.05
VMEM_LIMIT = 63 * 1024 * 1024
SMALL = pl.CostEstimate(flops=0, bytes_accessed=0, transcendentals=0)


def rows_view(x):
    lead, planes, cells = x.shape[:-2], x.shape[-2], x.shape[-1]
    tiles = cells // LANES
    n = len(lead)
    x = x.reshape(lead + (planes, tiles, LANES))
    x = x.transpose(tuple(range(n)) + (n + 1, n, n + 2))
    return x.reshape(lead + (tiles * planes, LANES))


def planes_view(x, planes):
    lead, rows = x.shape[:-2], x.shape[-2]
    tiles = rows // planes
    n = len(lead)
    x = x.reshape(lead + (tiles, planes, LANES))
    x = x.transpose(tuple(range(n)) + (n + 1, n, n + 2))
    return x.reshape(lead + (planes, tiles * LANES))


def even_brick():
    return lax.axis_index("brick") % 2 == 0


def spread_matrix(back):
    size = SUB * PACK
    row = lax.broadcasted_iota(jnp.int32, (size, size), 0)
    column = lax.broadcasted_iota(jnp.int32, (size, size), 1)
    if back:
        row, column = column, row
    return (column == (row % SUB) * PACK + row // SUB).astype(jnp.bfloat16)


def gathered(read, segment, i):
    return jnp.concatenate(
        [read(pl.ds(s * segment + i * PACK, PACK)) for s in range(SUB)], axis=0
    )


def product(matrix, values):
    return jnp.dot(matrix, values, preferred_element_type=jnp.float32)


def face_matrix(planes):
    out = PACK // planes * SUB
    row = lax.broadcasted_iota(jnp.int32, (2 * out, SUB * PACK), 0)
    column = lax.broadcasted_iota(jnp.int32, (2 * out, SUB * PACK), 1)
    upper = (row < out) == even_brick()
    inner = row % out
    wanted = (inner % SUB) * PACK + (inner // SUB) * planes + jnp.where(upper, planes - 1, 0)
    return (column == wanted).astype(jnp.bfloat16), out


def edges_body(planes, chunks, x_ref, *refs):
    faces, held, sems = refs[-2 - 2 * len(chunks) : -2], refs[-2], refs[-1]
    first = chunks[0][0]
    bands = [(start - first + b, k, b) for k, (start, count) in enumerate(chunks) for b in range(count)]
    rows = held.shape[2]
    segment = rows // SUB
    copies = [pltpu.make_async_copy(x_ref.at[first + i], held.at[i], sems.at[i]) for i, _, _ in bands]
    for copy in copies:
        copy.start()
    select, out = face_matrix(planes)
    for i, k, b in bands:
        copies[i].wait()
        near_ref, far_ref = faces[2 * k], faces[2 * k + 1]
        for part in range(segment // PACK):
            block = jnp.concatenate(
                [gathered(lambda at: held[i, c, at, :], segment, part) for c in range(4)], axis=1
            )
            picked = product(select, block).astype(jnp.bfloat16)
            at = pl.ds(part * out, out)
            for c in range(4):
                lanes = slice(c * LANES, (c + 1) * LANES)
                near_ref[b, c, at, :] = picked[:out, lanes]
                far_ref[b, c, at, :] = picked[out:, lanes]


def edges(x, planes, chunks, after, limit):
    rows = x.shape[2]
    total = sum(count for _, count in chunks)
    shapes = [
        jax.ShapeDtypeStruct((count, 4, rows // planes, LANES), jnp.bfloat16) for _, count in chunks for _ in range(2)
    ]
    faces = pl.pallas_call(
        functools.partial(edges_body, planes, chunks),
        in_specs=[pl.BlockSpec(memory_space=pltpu.HBM)] + [pl.BlockSpec(memory_space=pl.ANY)] * len(after),
        out_shape=shapes,
        scratch_shapes=[pltpu.VMEM((total, 4, rows, LANES), jnp.bfloat16), pltpu.SemaphoreType.DMA((total,))],
        compiler_params=pltpu.CompilerParams(vmem_limit_bytes=limit),
        cost_estimate=SMALL,
        name="edges",
    )(x, *after)
    return [tuple(faces[2 * k : 2 * k + 2]) for k in range(len(chunks))]


def gate(near, far, after):
    anywhere = pl.BlockSpec(memory_space=pl.ANY)
    return pl.pallas_call(
        lambda *refs: None,
        in_specs=[anywhere] * (2 + len(after)),
        out_specs=[anywhere, anywhere],
        out_shape=[jax.ShapeDtypeStruct(a.shape, a.dtype) for a in (near, far)],
        input_output_aliases={0: 0, 1: 1},
        compiler_params=pltpu.CompilerParams(vmem_limit_bytes=VMEM_LIMIT),
        name="gate",
    )(near, far, *after)


def front_body(planes, scale, counts, mult_ref, occ_ref, x_ref, *refs):
    bands = x_ref.shape[0]
    density_ref, faces = refs[-1 - 2 * len(counts)], refs[len(refs) - 2 * len(counts) :]
    weights = [(mult_ref[b] * occ_ref[b]).astype(jnp.float32) * scale for b in range(bands)]
    for s in range(SUB):
        up = down = real = imag = None
        for b in range(bands):
            ur, ui, dr, di = (x_ref[b, c, s].astype(jnp.float32) for c in range(4))
            wur, wui = weights[b] * ur, weights[b] * ui
            wdr, wdi = weights[b] * dr, weights[b] * di
            terms = (
                wur * ur + wui * ui,
                wdr * dr + wdi * di,
                wur * dr + wui * di,
                wur * di - wui * dr,
            )
            if b == 0:
                up, down, real, imag = terms
            else:
                up, down, real, imag = up + terms[0], down + terms[1], real + terms[2], imag + terms[3]
        density_ref[0, s] = up + down
        density_ref[1, s] = 2.0 * real
        density_ref[2, s] = 2.0 * imag
        density_ref[3, s] = up - down
    if counts:
        select, out = face_matrix(planes)
    band = bands - sum(counts)
    for k, count in enumerate(counts):
        for b in range(count):
            block = jnp.concatenate(
                [x_ref[band, c].reshape(SUB * PACK, LANES) for c in range(4)], axis=1
            )
            picked = product(select, block).astype(jnp.bfloat16)
            for c in range(4):
                lanes = slice(c * LANES, (c + 1) * LANES)
                faces[2 * k][b, c] = picked[:out, lanes]
                faces[2 * k + 1][b, c] = picked[out:, lanes]
            band += 1


def front(x, mult, occ, total, planes, counts, after):
    bands, rows = x.shape[0], x.shape[2]
    segment = rows // SUB
    out = PACK // planes * SUB
    anywhere = pl.BlockSpec(memory_space=pl.ANY)
    results = pl.pallas_call(
        functools.partial(front_body, planes, 1.0 / (2.0 * total), counts),
        grid=(segment // PACK,),
        in_specs=[
            pl.BlockSpec(memory_space=pltpu.SMEM),
            pl.BlockSpec(memory_space=pltpu.SMEM),
            pl.BlockSpec((bands, 4, SUB, PACK, LANES), lambda i: (0, 0, 0, i, 0)),
        ]
        + [anywhere] * len(after),
        out_specs=[pl.BlockSpec((4, SUB, PACK, LANES), lambda i: (0, 0, i, 0))]
        + [pl.BlockSpec((count, 4, out, LANES), lambda i: (0, 0, i, 0)) for count in counts for _ in range(2)],
        out_shape=[jax.ShapeDtypeStruct((4, SUB, segment, LANES), jnp.float32)]
        + [
            jax.ShapeDtypeStruct((count, 4, rows // planes, LANES), jnp.bfloat16)
            for count in counts
            for _ in range(2)
        ],
        compiler_params=pltpu.CompilerParams(vmem_limit_bytes=VMEM_LIMIT),
        cost_estimate=SMALL,
        name="front",
    )(mult, occ, x.reshape(bands, 4, SUB, segment, LANES), *after)
    return results[0].reshape(4, rows, LANES), [tuple(results[1 + 2 * k : 3 + 2 * k]) for k in range(len(counts))]


def cube_root(x):
    root = jnp.exp(jnp.log(jnp.abs(x)) * (1.0 / 3.0))
    return jnp.where(x < 0.0, -root, root)


def potential_body(d_ref, core_ref, local_ref, out_ref):
    size = SUB * PACK
    spread = spread_matrix(False)
    fields = product(spread, jnp.concatenate([d_ref[f].reshape(size, LANES) for f in range(4)], axis=1))
    d0, d1, d2, d3 = (fields[:, f * LANES : (f + 1) * LANES] for f in range(4))
    outer = jnp.concatenate([core_ref[...].reshape(size, LANES), local_ref[...].reshape(size, LANES)], axis=1)
    outer = jnp.dot(
        spread.astype(jnp.float32), outer, precision=lax.Precision.HIGHEST, preferred_element_type=jnp.float32
    )
    core, local = outer[:, :LANES], outer[:, LANES:]
    electrons = d0 + core
    magnitude = jnp.sqrt(d1 * d1 + d2 * d2 + d3 * d3)
    upper = -cube_root((3.0 / math.pi) * (electrons + magnitude))
    lower = -cube_root((3.0 / math.pi) * (electrons - magnitude))
    factor = 0.5 * (upper - lower) / jnp.maximum(magnitude, FLOOR_FRACTION * electrons)
    v = 0.5 * (upper + lower) + local
    bz = factor * d3
    for f, field in enumerate((v + bz + 3.0, factor * d1, factor * d2, v - bz + 3.0)):
        out_ref[f] = field.reshape(PACK, SUB, LANES)


def potential_of(density, core, local):
    rows = density.shape[1]
    segment = rows // SUB
    cut = lambda field: field.reshape(field.shape[:-2] + (SUB, segment, LANES))
    outer = pl.BlockSpec((SUB, PACK, LANES), lambda i: (0, i, 0))
    return pl.pallas_call(
        potential_body,
        grid=(segment // PACK,),
        in_specs=[pl.BlockSpec((4, SUB, PACK, LANES), lambda i: (0, 0, i, 0)), outer, outer],
        out_specs=pl.BlockSpec((4, PACK, SUB, LANES), lambda i: (0, i, 0, 0)),
        out_shape=jax.ShapeDtypeStruct((4, segment, SUB, LANES), jnp.float32),
        compiler_params=pltpu.CompilerParams(vmem_limit_bytes=VMEM_LIMIT),
        cost_estimate=SMALL,
        name="potential",
    )(cut(density), cut(core), cut(local))


def apply_body(planes, rows, x_ref, pot_ref, near_ref, far_ref, carry_ref, out_ref, token_ref, wide, ends, turned, flat):
    segment = rows // SUB
    stride = planes * TRIPLE
    steps = segment // stride
    near_slot = jnp.where(even_brick(), 1, 0)
    spread, unspread = spread_matrix(False), spread_matrix(True)

    for c in range(4):
        ends[near_slot, c] = near_ref[0, c].astype(jnp.float32).reshape(ends.shape[2:])
        ends[1 - near_slot, c] = far_ref[0, c].astype(jnp.float32).reshape(ends.shape[2:])

    def load(i, unused):
        block = jnp.concatenate([gathered(lambda at: x_ref[0, c, at, :], segment, i) for c in range(4)], axis=1)
        values = product(spread, block)
        for c in range(4):
            part = values[:, c * LANES : (c + 1) * LANES]
            wide[c, pl.ds(i * PACK, PACK)] = part.reshape(PACK, SUB, LANES)
            turned[c, pl.ds(stride + i * PACK, PACK)] = pltpu.roll(part, HALF, 1).reshape(PACK, SUB, LANES)
        return unused

    lax.fori_loop(0, segment // PACK, load, 0, unroll=True)
    for c in range(4):
        for q in range(stride):
            turned[c, q] = pltpu.roll(turned[c, segment + q], 1, 0)
            turned[c, segment + stride + q] = pltpu.roll(turned[c, stride + q], SUB - 1, 0)

    lane = lax.broadcasted_iota(jnp.int32, (SUB, LANES), 1)
    low = lane < HALF
    initial, final = lane == 0, lane == LANES - 1
    inner_initial, inner_final = lane == HALF, lane == HALF - 1

    def neighbours(c, plane, j):
        spot = [j * stride + tile * planes + plane for tile in range(TRIPLE)]
        v0, v1, v2 = (wide[c, at] for at in spot)
        r0, r1, r2 = (turned[c, at + stride] for at in spot)
        after0 = r0 + turned[c, spot[0] + 2 * stride]
        after1 = r1 + turned[c, spot[1] + 2 * stride]
        before1 = r1 + turned[c, spot[1]]
        before2 = r2 + turned[c, spot[2]]
        across = (
            jnp.where(low, before1, before2),
            jnp.where(low, before2, after0),
            jnp.where(low, after0, after1),
        )
        plus = (
            jnp.where(initial, v1, v0),
            jnp.where(inner_initial, r0, jnp.where(initial, v2, v1)),
            jnp.where(initial, r1, v2),
        )
        minus = (
            jnp.where(final, r1, v0),
            jnp.where(inner_final, r2, jnp.where(final, v0, v1)),
            jnp.where(final, v1, v2),
        )
        sums = []
        for tile in range(TRIPLE):
            below = ends[0, c, j * TRIPLE + tile] if plane == 0 else wide[c, spot[tile] - 1]
            above = ends[1, c, j * TRIPLE + tile] if plane == planes - 1 else wide[c, spot[tile] + 1]
            along = pltpu.roll(plus[tile], LANES - 1, 1) + pltpu.roll(minus[tile], 1, 1)
            sums.append((across[tile] + along) + (below + above))
        return (v0, v1, v2), sums

    def step(j, unused):
        for plane in range(planes):
            (ur, nur), (ui, nui), (dr, ndr), (di, ndi) = (neighbours(c, plane, j) for c in range(4))
            for tile in range(TRIPLE):
                spot = j * stride + tile * planes + plane
                diag_up, bx, by, diag_down = (pot_ref[f, spot] for f in range(4))
                a, b, e, f = ur[tile], ui[tile], dr[tile], di[tile]
                flat[0, spot] = diag_up * a + bx * e + by * f - 0.5 * nur[tile]
                flat[1, spot] = diag_up * b + bx * f - by * e - 0.5 * nui[tile]
                flat[2, spot] = bx * a - by * b + diag_down * e - 0.5 * ndr[tile]
                flat[3, spot] = bx * b + by * a + diag_down * f - 0.5 * ndi[tile]
        return unused

    lax.fori_loop(0, steps, step, 0)

    def store(i, unused):
        at = pl.ds(i * PACK, PACK)
        block = jnp.concatenate([flat[c, at].reshape(PACK * SUB, LANES) for c in range(4)], axis=1)
        values = product(unspread, block.astype(jnp.bfloat16)).astype(jnp.bfloat16)
        for c in range(4):
            for s in range(SUB):
                out_ref[0, c, pl.ds(pl.multiple_of(s * segment + i * PACK, PACK), PACK), :] = values[
                    s * PACK : (s + 1) * PACK, c * LANES : (c + 1) * LANES
                ]
        return unused

    lax.fori_loop(0, segment // PACK, store, 0, unroll=True)


def apply_bands(x, potential, near, far, planes, start, carry):
    count, rows = near.shape[0], x.shape[2]
    segment = rows // SUB
    stride = planes * TRIPLE
    tiles = rows // planes
    halo = pl.BlockSpec((1, 4, tiles, LANES), lambda b: (b, 0, 0, 0))
    body = functools.partial(apply_body, planes, rows)
    in_specs = [
        pl.BlockSpec((1, 4, rows, LANES), lambda b: (start + b, 0, 0, 0)),
        pl.BlockSpec((4, segment, SUB, LANES), lambda b: (0, 0, 0, 0)),
        halo,
        halo,
    ]
    operands = [x, potential, near, far]
    aliases = {}
    if carry is not None:
        in_specs.append(pl.BlockSpec(memory_space=pl.ANY))
        operands.append(carry)
        aliases = {4: 0}
        call = body
    else:

        def call(x_ref, pot_ref, near_ref, far_ref, *rest):
            body(x_ref, pot_ref, near_ref, far_ref, None, *rest)

    return pl.pallas_call(
        call,
        grid=(count,),
        in_specs=in_specs,
        out_specs=[
            pl.BlockSpec((1, 4, rows, LANES), lambda b: (start + b, 0, 0, 0)),
            pl.BlockSpec(memory_space=pl.ANY),
        ],
        out_shape=[
            jax.ShapeDtypeStruct(x.shape, jnp.bfloat16),
            jax.ShapeDtypeStruct((SUB, LANES), jnp.float32),
        ],
        input_output_aliases=aliases,
        scratch_shapes=[
            pltpu.VMEM((4, segment, SUB, LANES), jnp.float32),
            pltpu.VMEM((2, 4, tiles // SUB, SUB, LANES), jnp.float32),
            pltpu.VMEM((4, segment + 2 * stride, SUB, LANES), jnp.float32),
            pltpu.VMEM((4, segment, SUB, LANES), jnp.float32),
        ],
        compiler_params=pltpu.CompilerParams(vmem_limit_bytes=VMEM_LIMIT),
        cost_estimate=SMALL,
        name="apply",
    )(*operands)


def chunk_sizes(bands):
    ends = max(bands // 4, 1)
    return [n for n in (ends, bands - 2 * ends, ends) if n > 0] if bands > 1 else [1]


def shards(spinors, kpt_mult, occupied, core_density, local_potential):
    bands, planes = spinors.shape[0], spinors.shape[2]
    total = bands * lax.axis_size("ka")
    size = lax.axis_size("brick")
    near_pairs = [(i, i ^ 1) for i in range(size) if i ^ 1 < size]
    far_pairs = [(i, j) for i in range(size) for j in [((i + 1) ^ 1) - 1] if 0 <= j < size]
    x = rows_view(spinors)
    core, local = rows_view(core_density), rows_view(local_potential)
    sizes = chunk_sizes(bands)
    starts = [sum(sizes[:k]) for k in range(len(sizes))]

    swap = lambda face: (lax.ppermute(face[0], "brick", near_pairs), lax.ppermute(face[1], "brick", far_pairs))
    faces = edges(x, planes, [(0, sizes[0])], (), VMEM_LIMIT)
    halos = [swap(faces[0])]
    density, others = front(x, kpt_mult, occupied, total, planes, sizes[1:], faces[0])
    faces += others
    halos += [swap(face) for face in faces[1:2]]
    density = lax.psum(density, "ka").astype(jnp.bfloat16)
    potential = potential_of(density, core, local)
    out, token = None, (potential,)
    for k, start in enumerate(starts):
        if k + 2 < len(starts):
            halos.append(swap(gate(*faces[k + 2], halos[k] + token)))
        out, done = apply_bands(x, potential, *halos[k], planes, start, out)
        token = (done,)
    return planes_view(out, planes)


def solution(mesh):
    placed = (P("ka", None, "brick", None), P("ka"), P("ka"), P("brick", None), P("brick", None))
    return jax.shard_map(
        shards, mesh=mesh, in_specs=placed, out_specs=P("ka", None, "brick", None), check_vma=False
    )
```

```python
import functools
import math

import jax
import jax.numpy as jnp
from jax import lax
from jax.experimental import pallas as pl
from jax.experimental.pallas import tpu as pltpu
from jax.sharding import PartitionSpec as P

NY = 192
LANES = 128
SUB = 8
TRIPLE = 3
HALF = 2 * NY - 2 * LANES - LANES // 2
PACK = 16
FLOOR_FRACTION = 0.05
VMEM_LIMIT = 63 * 1024 * 1024
SMALL = pl.CostEstimate(flops=0, bytes_accessed=0, transcendentals=0)


def rows_view(x):
    lead, planes, cells = x.shape[:-2], x.shape[-2], x.shape[-1]
    tiles = cells // LANES
    n = len(lead)
    x = x.reshape(lead + (planes, tiles, LANES))
    x = x.transpose(tuple(range(n)) + (n + 1, n, n + 2))
    return x.reshape(lead + (tiles * planes, LANES))


def planes_view(x, planes):
    lead, rows = x.shape[:-2], x.shape[-2]
    tiles = rows // planes
    n = len(lead)
    x = x.reshape(lead + (tiles, planes, LANES))
    x = x.transpose(tuple(range(n)) + (n + 1, n, n + 2))
    return x.reshape(lead + (planes, tiles * LANES))


def even_brick():
    return lax.axis_index("brick") % 2 == 0


def spread_matrix(back):
    size = SUB * PACK
    row = lax.broadcasted_iota(jnp.int32, (size, size), 0)
    column = lax.broadcasted_iota(jnp.int32, (size, size), 1)
    if back:
        row, column = column, row
    return (column == (row % SUB) * PACK + row // SUB).astype(jnp.bfloat16)


def gathered(read, segment, i):
    return jnp.concatenate(
        [read(pl.ds(s * segment + i * PACK, PACK)) for s in range(SUB)], axis=0
    )


def product(matrix, values):
    return jnp.dot(matrix, values, preferred_element_type=jnp.float32)


def face_matrix(planes):
    out = PACK // planes * SUB
    row = lax.broadcasted_iota(jnp.int32, (2 * out, SUB * PACK), 0)
    column = lax.broadcasted_iota(jnp.int32, (2 * out, SUB * PACK), 1)
    upper = (row < out) == even_brick()
    inner = row % out
    wanted = (inner % SUB) * PACK + (inner // SUB) * planes + jnp.where(upper, planes - 1, 0)
    return (column == wanted).astype(jnp.bfloat16), out


def edges_body(planes, chunks, x_ref, *refs):
    faces, held, sems = refs[-2 - 2 * len(chunks) : -2], refs[-2], refs[-1]
    first = chunks[0][0]
    bands = [(start - first + b, k, b) for k, (start, count) in enumerate(chunks) for b in range(count)]
    rows = held.shape[2]
    segment = rows // SUB
    copies = [pltpu.make_async_copy(x_ref.at[first + i], held.at[i], sems.at[i]) for i, _, _ in bands]
    for copy in copies:
        copy.start()
    select, out = face_matrix(planes)
    for i, k, b in bands:
        copies[i].wait()
        near_ref, far_ref = faces[2 * k], faces[2 * k + 1]
        for part in range(segment // PACK):
            block = jnp.concatenate(
                [gathered(lambda at: held[i, c, at, :], segment, part) for c in range(4)], axis=1
            )
            picked = product(select, block).astype(jnp.bfloat16)
            at = pl.ds(part * out, out)
            for c in range(4):
                lanes = slice(c * LANES, (c + 1) * LANES)
                near_ref[b, c, at, :] = picked[:out, lanes]
                far_ref[b, c, at, :] = picked[out:, lanes]


def edges(x, planes, chunks, after, limit):
    rows = x.shape[2]
    total = sum(count for _, count in chunks)
    shapes = [
        jax.ShapeDtypeStruct((count, 4, rows // planes, LANES), jnp.bfloat16) for _, count in chunks for _ in range(2)
    ]
    faces = pl.pallas_call(
        functools.partial(edges_body, planes, chunks),
        in_specs=[pl.BlockSpec(memory_space=pltpu.HBM)] + [pl.BlockSpec(memory_space=pl.ANY)] * len(after),
        out_shape=shapes,
        scratch_shapes=[pltpu.VMEM((total, 4, rows, LANES), jnp.bfloat16), pltpu.SemaphoreType.DMA((total,))],
        compiler_params=pltpu.CompilerParams(vmem_limit_bytes=limit),
        cost_estimate=SMALL,
        name="edges",
    )(x, *after)
    return [tuple(faces[2 * k : 2 * k + 2]) for k in range(len(chunks))]


def gate(near, far, after):
    anywhere = pl.BlockSpec(memory_space=pl.ANY)
    return pl.pallas_call(
        lambda *refs: None,
        in_specs=[anywhere] * (2 + len(after)),
        out_specs=[anywhere, anywhere],
        out_shape=[jax.ShapeDtypeStruct(a.shape, a.dtype) for a in (near, far)],
        input_output_aliases={0: 0, 1: 1},
        compiler_params=pltpu.CompilerParams(vmem_limit_bytes=VMEM_LIMIT),
        name="gate",
    )(near, far, *after)


def front_body(planes, scale, counts, mult_ref, occ_ref, x_ref, *refs):
    bands = x_ref.shape[0]
    first = len(refs) - 2 * len(counts)
    mine_ref, other_ref, faces = refs[first - 2], refs[first - 1], refs[first:]
    lower_half = holds_lower_half()
    weights = [(mult_ref[b] * occ_ref[b]).astype(jnp.float32) * scale for b in range(bands)]
    for s in range(SUB):
        up = down = real = imag = None
        for b in range(bands):
            ur, ui, dr, di = (x_ref[b, c, s].astype(jnp.float32) for c in range(4))
            wur, wui = weights[b] * ur, weights[b] * ui
            wdr, wdi = weights[b] * dr, weights[b] * di
            terms = (
                wur * ur + wui * ui,
                wdr * dr + wdi * di,
                wur * dr + wui * di,
                wur * di - wui * dr,
            )
            if b == 0:
                up, down, real, imag = terms
            else:
                up, down, real, imag = up + terms[0], down + terms[1], real + terms[2], imag + terms[3]
        fields = (up + down, 2.0 * real, 2.0 * imag, up - down)
        for f in range(2):
            mine_ref[f, s] = jnp.where(lower_half, fields[f], fields[f + 2]).astype(jnp.bfloat16)
            other_ref[f, s] = jnp.where(lower_half, fields[f + 2], fields[f]).astype(jnp.bfloat16)
    if counts:
        select, out = face_matrix(planes)
    band = bands - sum(counts)
    for k, count in enumerate(counts):
        for b in range(count):
            block = jnp.concatenate(
                [x_ref[band, c].reshape(SUB * PACK, LANES) for c in range(4)], axis=1
            )
            picked = product(select, block).astype(jnp.bfloat16)
            for c in range(4):
                lanes = slice(c * LANES, (c + 1) * LANES)
                faces[2 * k][b, c] = picked[:out, lanes]
                faces[2 * k + 1][b, c] = picked[out:, lanes]
            band += 1


def front(x, mult, occ, total, planes, counts, after):
    bands, rows = x.shape[0], x.shape[2]
    segment = rows // SUB
    out = PACK // planes * SUB
    anywhere = pl.BlockSpec(memory_space=pl.ANY)
    results = pl.pallas_call(
        functools.partial(front_body, planes, 1.0 / (2.0 * total), counts),
        grid=(segment // PACK,),
        in_specs=[
            pl.BlockSpec(memory_space=pltpu.SMEM),
            pl.BlockSpec(memory_space=pltpu.SMEM),
            pl.BlockSpec((bands, 4, SUB, PACK, LANES), lambda i: (0, 0, 0, i, 0)),
        ]
        + [anywhere] * len(after),
        out_specs=[pl.BlockSpec((2, SUB, PACK, LANES), lambda i: (0, 0, i, 0))] * 2
        + [pl.BlockSpec((count, 4, out, LANES), lambda i: (0, 0, i, 0)) for count in counts for _ in range(2)],
        out_shape=[jax.ShapeDtypeStruct((2, SUB, segment, LANES), jnp.bfloat16)] * 2
        + [
            jax.ShapeDtypeStruct((count, 4, rows // planes, LANES), jnp.bfloat16)
            for count in counts
            for _ in range(2)
        ],
        compiler_params=pltpu.CompilerParams(vmem_limit_bytes=VMEM_LIMIT),
        cost_estimate=SMALL,
        name="front",
    )(mult, occ, x.reshape(bands, 4, SUB, segment, LANES), *after)
    halves = [half.reshape(2, rows, LANES) for half in results[:2]]
    return halves, [tuple(results[2 + 2 * k : 4 + 2 * k]) for k in range(len(counts))]


def add_body(a_ref, b_ref, out_ref):
    out_ref[...] = (a_ref[...].astype(jnp.float32) + b_ref[...].astype(jnp.float32)).astype(jnp.bfloat16)


def add(a, b):
    whole = pl.BlockSpec(memory_space=pltpu.VMEM)
    return pl.pallas_call(
        add_body,
        in_specs=[whole, whole],
        out_specs=whole,
        out_shape=jax.ShapeDtypeStruct(a.shape, a.dtype),
        compiler_params=pltpu.CompilerParams(vmem_limit_bytes=VMEM_LIMIT),
        cost_estimate=SMALL,
        name="add",
    )(a, b)


def holds_lower_half():
    return lax.axis_index("ka") % 2 == 0


def group_sum(mine, other):
    size = lax.axis_size("ka")
    assert size % 2 == 0
    partner = [(i, i ^ 1) for i in range(size)]

    def swaps(_, fields):
        total, given = fields
        total = add(total, lax.ppermute(given, "ka", partner))
        turning = total
        for _ in range(size // 2 - 1):
            turning = lax.ppermute(turning, "ka", [(i, (i + 2) % size) for i in range(size)])
            total = add(total, turning)
        return total, lax.ppermute(total, "ka", partner)

    trips = 1 + lax.div(lax.axis_index("ka"), size)
    return lax.fori_loop(0, trips, swaps, (mine, other))


def cube_root(x):
    root = jnp.exp(jnp.log(jnp.abs(x)) * (1.0 / 3.0))
    return jnp.where(x < 0.0, -root, root)


def potential_body(rows, mine_ref, other_ref, core_ref, local_ref, out_ref):
    segment = rows // SUB
    spread = spread_matrix(False)

    lower_half = holds_lower_half()

    def step(i, unused):
        block = jnp.concatenate(
            [gathered(lambda at: ref[f, at, :], segment, i) for ref in (mine_ref, other_ref) for f in range(2)], axis=1
        )
        fields = product(spread, block)
        m0, m1, o0, o1 = (fields[:, f * LANES : (f + 1) * LANES] for f in range(4))
        d0, d1 = jnp.where(lower_half, m0, o0), jnp.where(lower_half, m1, o1)
        d2, d3 = jnp.where(lower_half, o0, m0), jnp.where(lower_half, o1, m1)
        here = [pl.ds(i * PACK + r, SUB, stride=segment) for r in range(PACK)]
        core = jnp.concatenate([core_ref[at, :] for at in here], axis=0)
        local = jnp.concatenate([local_ref[at, :] for at in here], axis=0)
        electrons = d0 + core
        magnitude = jnp.sqrt(d1 * d1 + d2 * d2 + d3 * d3)
        upper = -cube_root((3.0 / math.pi) * (electrons + magnitude))
        lower = -cube_root((3.0 / math.pi) * (electrons - magnitude))
        factor = 0.5 * (upper - lower) / jnp.maximum(magnitude, FLOOR_FRACTION * electrons)
        v = 0.5 * (upper + lower) + local
        bz = factor * d3
        at = pl.ds(i * PACK, PACK)
        shape = (PACK, SUB, LANES)
        out_ref[0, at] = (v + bz + 3.0).reshape(shape)
        out_ref[1, at] = (factor * d1).reshape(shape)
        out_ref[2, at] = (factor * d2).reshape(shape)
        out_ref[3, at] = (v - bz + 3.0).reshape(shape)
        return unused

    lax.fori_loop(0, segment // PACK, step, 0, unroll=True)


def potential_of(mine, other, core, local):
    rows = mine.shape[1]
    whole = pl.BlockSpec(memory_space=pltpu.VMEM)
    return pl.pallas_call(
        functools.partial(potential_body, rows),
        in_specs=[whole, whole, whole, whole],
        out_specs=whole,
        out_shape=jax.ShapeDtypeStruct((4, rows // SUB, SUB, LANES), jnp.float32),
        compiler_params=pltpu.CompilerParams(vmem_limit_bytes=VMEM_LIMIT),
        cost_estimate=SMALL,
        name="potential",
    )(mine, other, core, local)


def apply_body(planes, rows, x_ref, pot_ref, near_ref, far_ref, carry_ref, out_ref, token_ref, wide, ends, turned, flat):
    segment = rows // SUB
    stride = planes * TRIPLE
    steps = segment // stride
    near_slot = jnp.where(even_brick(), 1, 0)
    spread, unspread = spread_matrix(False), spread_matrix(True)

    for c in range(4):
        ends[near_slot, c] = near_ref[0, c].astype(jnp.float32).reshape(ends.shape[2:])
        ends[1 - near_slot, c] = far_ref[0, c].astype(jnp.float32).reshape(ends.shape[2:])

    def load(i, unused):
        block = jnp.concatenate([gathered(lambda at: x_ref[0, c, at, :], segment, i) for c in range(4)], axis=1)
        values = product(spread, block)
        for c in range(4):
            part = values[:, c * LANES : (c + 1) * LANES]
            wide[c, pl.ds(i * PACK, PACK)] = part.reshape(PACK, SUB, LANES)
            turned[c, pl.ds(stride + i * PACK, PACK)] = pltpu.roll(part, HALF, 1).reshape(PACK, SUB, LANES)
        return unused

    lax.fori_loop(0, segment // PACK, load, 0, unroll=True)
    for c in range(4):
        for q in range(stride):
            turned[c, q] = pltpu.roll(turned[c, segment + q], 1, 0)
            turned[c, segment + stride + q] = pltpu.roll(turned[c, stride + q], SUB - 1, 0)

    lane = lax.broadcasted_iota(jnp.int32, (SUB, LANES), 1)
    low = lane < HALF
    initial, final = lane == 0, lane == LANES - 1
    inner_initial, inner_final = lane == HALF, lane == HALF - 1

    def neighbours(c, plane, j):
        spot = [j * stride + tile * planes + plane for tile in range(TRIPLE)]
        v0, v1, v2 = (wide[c, at] for at in spot)
        r0, r1, r2 = (turned[c, at + stride] for at in spot)
        after0 = r0 + turned[c, spot[0] + 2 * stride]
        after1 = r1 + turned[c, spot[1] + 2 * stride]
        before1 = r1 + turned[c, spot[1]]
        before2 = r2 + turned[c, spot[2]]
        across = (
            jnp.where(low, before1, before2),
            jnp.where(low, before2, after0),
            jnp.where(low, after0, after1),
        )
        plus = (
            jnp.where(initial, v1, v0),
            jnp.where(inner_initial, r0, jnp.where(initial, v2, v1)),
            jnp.where(initial, r1, v2),
        )
        minus = (
            jnp.where(final, r1, v0),
            jnp.where(inner_final, r2, jnp.where(final, v0, v1)),
            jnp.where(final, v1, v2),
        )
        sums = []
        for tile in range(TRIPLE):
            below = ends[0, c, j * TRIPLE + tile] if plane == 0 else wide[c, spot[tile] - 1]
            above = ends[1, c, j * TRIPLE + tile] if plane == planes - 1 else wide[c, spot[tile] + 1]
            along = pltpu.roll(plus[tile], LANES - 1, 1) + pltpu.roll(minus[tile], 1, 1)
            sums.append((across[tile] + along) + (below + above))
        return (v0, v1, v2), sums

    def step(j, unused):
        for plane in range(planes):
            (ur, nur), (ui, nui), (dr, ndr), (di, ndi) = (neighbours(c, plane, j) for c in range(4))
            for tile in range(TRIPLE):
                spot = j * stride + tile * planes + plane
                diag_up, bx, by, diag_down = (pot_ref[f, spot] for f in range(4))
                a, b, e, f = ur[tile], ui[tile], dr[tile], di[tile]
                flat[0, spot] = diag_up * a + bx * e + by * f - 0.5 * nur[tile]
                flat[1, spot] = diag_up * b + bx * f - by * e - 0.5 * nui[tile]
                flat[2, spot] = bx * a - by * b + diag_down * e - 0.5 * ndr[tile]
                flat[3, spot] = bx * b + by * a + diag_down * f - 0.5 * ndi[tile]
        return unused

    lax.fori_loop(0, steps, step, 0)

    def store(i, unused):
        at = pl.ds(i * PACK, PACK)
        block = jnp.concatenate([flat[c, at].reshape(PACK * SUB, LANES) for c in range(4)], axis=1)
        values = product(unspread, block.astype(jnp.bfloat16)).astype(jnp.bfloat16)
        for c in range(4):
            for s in range(SUB):
                out_ref[0, c, pl.ds(pl.multiple_of(s * segment + i * PACK, PACK), PACK), :] = values[
                    s * PACK : (s + 1) * PACK, c * LANES : (c + 1) * LANES
                ]
        return unused

    lax.fori_loop(0, segment // PACK, store, 0, unroll=True)


def apply_bands(x, potential, near, far, planes, start, carry):
    count, rows = near.shape[0], x.shape[2]
    segment = rows // SUB
    stride = planes * TRIPLE
    tiles = rows // planes
    halo = pl.BlockSpec((1, 4, tiles, LANES), lambda b: (b, 0, 0, 0))
    body = functools.partial(apply_body, planes, rows)
    in_specs = [
        pl.BlockSpec((1, 4, rows, LANES), lambda b: (start + b, 0, 0, 0)),
        pl.BlockSpec((4, segment, SUB, LANES), lambda b: (0, 0, 0, 0)),
        halo,
        halo,
    ]
    operands = [x, potential, near, far]
    aliases = {}
    if carry is not None:
        in_specs.append(pl.BlockSpec(memory_space=pl.ANY))
        operands.append(carry)
        aliases = {4: 0}
        call = body
    else:

        def call(x_ref, pot_ref, near_ref, far_ref, *rest):
            body(x_ref, pot_ref, near_ref, far_ref, None, *rest)

    return pl.pallas_call(
        call,
        grid=(count,),
        in_specs=in_specs,
        out_specs=[
            pl.BlockSpec((1, 4, rows, LANES), lambda b: (start + b, 0, 0, 0)),
            pl.BlockSpec(memory_space=pl.ANY),
        ],
        out_shape=[
            jax.ShapeDtypeStruct(x.shape, jnp.bfloat16),
            jax.ShapeDtypeStruct((SUB, LANES), jnp.float32),
        ],
        input_output_aliases=aliases,
        scratch_shapes=[
            pltpu.VMEM((4, segment, SUB, LANES), jnp.float32),
            pltpu.VMEM((2, 4, tiles // SUB, SUB, LANES), jnp.float32),
            pltpu.VMEM((4, segment + 2 * stride, SUB, LANES), jnp.float32),
            pltpu.VMEM((4, segment, SUB, LANES), jnp.float32),
        ],
        compiler_params=pltpu.CompilerParams(vmem_limit_bytes=VMEM_LIMIT),
        cost_estimate=SMALL,
        name="apply",
    )(*operands)


def chunk_sizes(bands):
    ends = max(bands // 4, 1)
    return [n for n in (ends, bands - 2 * ends, ends) if n > 0] if bands > 1 else [1]


def shards(spinors, kpt_mult, occupied, core_density, local_potential):
    bands, planes = spinors.shape[0], spinors.shape[2]
    total = bands * lax.axis_size("ka")
    size = lax.axis_size("brick")
    near_pairs = [(i, i ^ 1) for i in range(size) if i ^ 1 < size]
    far_pairs = [(i, j) for i in range(size) for j in [((i + 1) ^ 1) - 1] if 0 <= j < size]
    x = rows_view(spinors)
    core, local = rows_view(core_density), rows_view(local_potential)
    sizes = chunk_sizes(bands)
    starts = [sum(sizes[:k]) for k in range(len(sizes))]

    swap = lambda face: (lax.ppermute(face[0], "brick", near_pairs), lax.ppermute(face[1], "brick", far_pairs))
    faces = edges(x, planes, [(0, sizes[0])], (), VMEM_LIMIT)
    halos = [swap(faces[0])]
    density, others = front(x, kpt_mult, occupied, total, planes, sizes[1:], faces[0])
    faces += others
    halos += [swap(face) for face in faces[1:2]]
    potential = potential_of(*group_sum(*density), core, local)
    out, token = None, (potential,)
    for k, start in enumerate(starts):
        if k + 2 < len(starts):
            halos.append(swap(gate(*faces[k + 2], halos[k] + token)))
        out, done = apply_bands(x, potential, *halos[k], planes, start, out)
        token = (done,)
    return planes_view(out, planes)


def solution(mesh):
    placed = (P("ka", None, "brick", None), P("ka"), P("ka"), P("brick", None), P("brick", None))
    return jax.shard_map(
        shards, mesh=mesh, in_specs=placed, out_specs=P("ka", None, "brick", None), check_vma=False
    )
```

```python
import functools
import math

import jax
import jax.numpy as jnp
from jax import lax
from jax.experimental import pallas as pl
from jax.experimental.pallas import tpu as pltpu
from jax.sharding import PartitionSpec as P

NY = 192
LANES = 128
SUB = 8
TRIPLE = 3
HALF = 2 * NY - 2 * LANES - LANES // 2
PACK = 16
FLOOR_FRACTION = 0.05
VMEM_LIMIT = 63 * 1024 * 1024
SMALL = pl.CostEstimate(flops=0, bytes_accessed=0, transcendentals=0)


def rows_view(x):
    lead, planes, cells = x.shape[:-2], x.shape[-2], x.shape[-1]
    tiles = cells // LANES
    n = len(lead)
    x = x.reshape(lead + (planes, tiles, LANES))
    x = x.transpose(tuple(range(n)) + (n + 1, n, n + 2))
    return x.reshape(lead + (tiles * planes, LANES))


def planes_view(x, planes):
    lead, rows = x.shape[:-2], x.shape[-2]
    tiles = rows // planes
    n = len(lead)
    x = x.reshape(lead + (tiles, planes, LANES))
    x = x.transpose(tuple(range(n)) + (n + 1, n, n + 2))
    return x.reshape(lead + (planes, tiles * LANES))


def even_brick():
    return lax.axis_index("brick") % 2 == 0


def spread_matrix(back):
    size = SUB * PACK
    row = lax.broadcasted_iota(jnp.int32, (size, size), 0)
    column = lax.broadcasted_iota(jnp.int32, (size, size), 1)
    if back:
        row, column = column, row
    return (column == (row % SUB) * PACK + row // SUB).astype(jnp.bfloat16)


def gathered(read, segment, i):
    return jnp.concatenate(
        [read(pl.ds(s * segment + i * PACK, PACK)) for s in range(SUB)], axis=0
    )


def product(matrix, values):
    return jnp.dot(matrix, values, preferred_element_type=jnp.float32)


def face_matrix(planes):
    out = PACK // planes * SUB
    row = lax.broadcasted_iota(jnp.int32, (2 * out, SUB * PACK), 0)
    column = lax.broadcasted_iota(jnp.int32, (2 * out, SUB * PACK), 1)
    upper = (row < out) == even_brick()
    inner = row % out
    wanted = (inner % SUB) * PACK + (inner // SUB) * planes + jnp.where(upper, planes - 1, 0)
    return (column == wanted).astype(jnp.bfloat16), out


def edges_body(planes, chunks, x_ref, *refs):
    faces, held, sems = refs[-2 - 2 * len(chunks) : -2], refs[-2], refs[-1]
    first = chunks[0][0]
    bands = [(start - first + b, k, b) for k, (start, count) in enumerate(chunks) for b in range(count)]
    rows = held.shape[2]
    segment = rows // SUB
    copies = [pltpu.make_async_copy(x_ref.at[first + i], held.at[i], sems.at[i]) for i, _, _ in bands]
    for copy in copies:
        copy.start()
    select, out = face_matrix(planes)
    for i, k, b in bands:
        copies[i].wait()
        near_ref, far_ref = faces[2 * k], faces[2 * k + 1]
        for part in range(segment // PACK):
            block = jnp.concatenate(
                [gathered(lambda at: held[i, c, at, :], segment, part) for c in range(4)], axis=1
            )
            picked = product(select, block).astype(jnp.bfloat16)
            at = pl.ds(part * out, out)
            for c in range(4):
                lanes = slice(c * LANES, (c + 1) * LANES)
                near_ref[b, c, at, :] = picked[:out, lanes]
                far_ref[b, c, at, :] = picked[out:, lanes]


def edges(x, planes, chunks, after, limit):
    rows = x.shape[2]
    total = sum(count for _, count in chunks)
    shapes = [
        jax.ShapeDtypeStruct((count, 4, rows // planes, LANES), jnp.bfloat16) for _, count in chunks for _ in range(2)
    ]
    faces = pl.pallas_call(
        functools.partial(edges_body, planes, chunks),
        in_specs=[pl.BlockSpec(memory_space=pltpu.HBM)] + [pl.BlockSpec(memory_space=pl.ANY)] * len(after),
        out_shape=shapes,
        scratch_shapes=[pltpu.VMEM((total, 4, rows, LANES), jnp.bfloat16), pltpu.SemaphoreType.DMA((total,))],
        compiler_params=pltpu.CompilerParams(vmem_limit_bytes=limit),
        cost_estimate=SMALL,
        name="edges",
    )(x, *after)
    return [tuple(faces[2 * k : 2 * k + 2]) for k in range(len(chunks))]


def gate(near, far, after):
    anywhere = pl.BlockSpec(memory_space=pl.ANY)
    return pl.pallas_call(
        lambda *refs: None,
        in_specs=[anywhere] * (2 + len(after)),
        out_specs=[anywhere, anywhere],
        out_shape=[jax.ShapeDtypeStruct(a.shape, a.dtype) for a in (near, far)],
        input_output_aliases={0: 0, 1: 1},
        compiler_params=pltpu.CompilerParams(vmem_limit_bytes=VMEM_LIMIT),
        name="gate",
    )(near, far, *after)


def front_body(planes, scale, counts, mult_ref, occ_ref, x_ref, *refs):
    bands = x_ref.shape[0]
    first = len(refs) - 2 * len(counts)
    mine_ref, other_ref, faces = refs[first - 2], refs[first - 1], refs[first:]
    lower_half = holds_lower_half()
    weights = [(mult_ref[b] * occ_ref[b]).astype(jnp.float32) * scale for b in range(bands)]
    for s in range(SUB):
        up = down = real = imag = None
        for b in range(bands):
            ur, ui, dr, di = (x_ref[b, c, s].astype(jnp.float32) for c in range(4))
            wur, wui = weights[b] * ur, weights[b] * ui
            wdr, wdi = weights[b] * dr, weights[b] * di
            terms = (
                wur * ur + wui * ui,
                wdr * dr + wdi * di,
                wur * dr + wui * di,
                wur * di - wui * dr,
            )
            if b == 0:
                up, down, real, imag = terms
            else:
                up, down, real, imag = up + terms[0], down + terms[1], real + terms[2], imag + terms[3]
        fields = (up + down, 2.0 * real, 2.0 * imag, up - down)
        for f in range(2):
            mine_ref[f, s] = jnp.where(lower_half, fields[f], fields[f + 2]).astype(jnp.bfloat16)
            other_ref[f, s] = jnp.where(lower_half, fields[f + 2], fields[f]).astype(jnp.bfloat16)
    if counts:
        select, out = face_matrix(planes)
    band = bands - sum(counts)
    for k, count in enumerate(counts):
        for b in range(count):
            block = jnp.concatenate(
                [x_ref[band, c].reshape(SUB * PACK, LANES) for c in range(4)], axis=1
            )
            picked = product(select, block).astype(jnp.bfloat16)
            for c in range(4):
                lanes = slice(c * LANES, (c + 1) * LANES)
                faces[2 * k][b, c] = picked[:out, lanes]
                faces[2 * k + 1][b, c] = picked[out:, lanes]
            band += 1


def front(x, mult, occ, total, planes, counts, after):
    bands, rows = x.shape[0], x.shape[2]
    segment = rows // SUB
    out = PACK // planes * SUB
    anywhere = pl.BlockSpec(memory_space=pl.ANY)
    results = pl.pallas_call(
        functools.partial(front_body, planes, 1.0 / (2.0 * total), counts),
        grid=(segment // PACK,),
        in_specs=[
            pl.BlockSpec(memory_space=pltpu.SMEM),
            pl.BlockSpec(memory_space=pltpu.SMEM),
            pl.BlockSpec((bands, 4, SUB, PACK, LANES), lambda i: (0, 0, 0, i, 0)),
        ]
        + [anywhere] * len(after),
        out_specs=[pl.BlockSpec((2, SUB, PACK, LANES), lambda i: (0, 0, i, 0))] * 2
        + [pl.BlockSpec((count, 4, out, LANES), lambda i: (0, 0, i, 0)) for count in counts for _ in range(2)],
        out_shape=[jax.ShapeDtypeStruct((2, SUB, segment, LANES), jnp.bfloat16)] * 2
        + [
            jax.ShapeDtypeStruct((count, 4, rows // planes, LANES), jnp.bfloat16)
            for count in counts
            for _ in range(2)
        ],
        compiler_params=pltpu.CompilerParams(vmem_limit_bytes=VMEM_LIMIT),
        cost_estimate=SMALL,
        name="front",
    )(mult, occ, x.reshape(bands, 4, SUB, segment, LANES), *after)
    halves = [half.reshape(2, rows, LANES) for half in results[:2]]
    return halves, [tuple(results[2 + 2 * k : 4 + 2 * k]) for k in range(len(counts))]


def add_body(a_ref, b_ref, out_ref):
    out_ref[...] = (a_ref[...].astype(jnp.float32) + b_ref[...].astype(jnp.float32)).astype(jnp.bfloat16)


def add(a, b):
    whole = pl.BlockSpec(memory_space=pltpu.VMEM)
    return pl.pallas_call(
        add_body,
        in_specs=[whole, whole],
        out_specs=whole,
        out_shape=jax.ShapeDtypeStruct(a.shape, a.dtype),
        compiler_params=pltpu.CompilerParams(vmem_limit_bytes=VMEM_LIMIT),
        cost_estimate=SMALL,
        name="add",
    )(a, b)


def holds_lower_half():
    return lax.axis_index("ka") % 2 == 0


def group_sum(mine, other):
    size = lax.axis_size("ka")
    assert size % 2 == 0
    partner = [(i, i ^ 1) for i in range(size)]

    def swaps(_, fields):
        total, given = fields
        total = add(total, lax.ppermute(given, "ka", partner))
        turning = total
        for _ in range(size // 2 - 1):
            turning = lax.ppermute(turning, "ka", [(i, (i + 2) % size) for i in range(size)])
            total = add(total, turning)
        return total, lax.ppermute(total, "ka", partner)

    trips = 1 + lax.div(lax.axis_index("ka"), size)
    return lax.fori_loop(0, trips, swaps, (mine, other))


def cube_root(x):
    root = jnp.exp(jnp.log(jnp.abs(x)) * (1.0 / 3.0))
    return jnp.where(x < 0.0, -root, root)


def potential_body(rows, mine_ref, other_ref, core_ref, local_ref, *refs):
    out_ref = refs[-1]
    segment = rows // SUB
    spread = spread_matrix(False)

    lower_half = holds_lower_half()

    def step(i, unused):
        block = jnp.concatenate(
            [gathered(lambda at: ref[f, at, :], segment, i) for ref in (mine_ref, other_ref) for f in range(2)], axis=1
        )
        fields = product(spread, block)
        m0, m1, o0, o1 = (fields[:, f * LANES : (f + 1) * LANES] for f in range(4))
        d0, d1 = jnp.where(lower_half, m0, o0), jnp.where(lower_half, m1, o1)
        d2, d3 = jnp.where(lower_half, o0, m0), jnp.where(lower_half, o1, m1)
        here = [pl.ds(i * PACK + r, SUB, stride=segment) for r in range(PACK)]
        core = jnp.concatenate([core_ref[at, :] for at in here], axis=0)
        local = jnp.concatenate([local_ref[at, :] for at in here], axis=0)
        electrons = d0 + core
        magnitude = jnp.sqrt(d1 * d1 + d2 * d2 + d3 * d3)
        upper = -cube_root((3.0 / math.pi) * (electrons + magnitude))
        lower = -cube_root((3.0 / math.pi) * (electrons - magnitude))
        factor = 0.5 * (upper - lower) / jnp.maximum(magnitude, FLOOR_FRACTION * electrons)
        v = 0.5 * (upper + lower) + local
        bz = factor * d3
        at = pl.ds(i * PACK, PACK)
        shape = (PACK, SUB, LANES)
        out_ref[0, at] = (v + bz + 3.0).reshape(shape)
        out_ref[1, at] = (factor * d1).reshape(shape)
        out_ref[2, at] = (factor * d2).reshape(shape)
        out_ref[3, at] = (v - bz + 3.0).reshape(shape)
        return unused

    lax.fori_loop(0, segment // PACK, step, 0, unroll=True)


def potential_of(mine, other, core, local, after):
    rows = mine.shape[1]
    whole = pl.BlockSpec(memory_space=pltpu.VMEM)
    return pl.pallas_call(
        functools.partial(potential_body, rows),
        in_specs=[whole] * 4 + [pl.BlockSpec(memory_space=pl.ANY)] * len(after),
        out_specs=whole,
        out_shape=jax.ShapeDtypeStruct((4, rows // SUB, SUB, LANES), jnp.float32),
        compiler_params=pltpu.CompilerParams(vmem_limit_bytes=VMEM_LIMIT),
        cost_estimate=SMALL,
        name="potential",
    )(mine, other, core, local, *after)


def apply_body(planes, rows, x_ref, pot_ref, near_ref, far_ref, carry_ref, out_ref, token_ref, wide, ends, turned, flat):
    segment = rows // SUB
    stride = planes * TRIPLE
    steps = segment // stride
    near_slot = jnp.where(even_brick(), 1, 0)
    spread, unspread = spread_matrix(False), spread_matrix(True)

    for c in range(4):
        ends[near_slot, c] = near_ref[0, c].astype(jnp.float32).reshape(ends.shape[2:])
        ends[1 - near_slot, c] = far_ref[0, c].astype(jnp.float32).reshape(ends.shape[2:])

    def load(i, unused):
        block = jnp.concatenate([gathered(lambda at: x_ref[0, c, at, :], segment, i) for c in range(4)], axis=1)
        values = product(spread, block)
        for c in range(4):
            part = values[:, c * LANES : (c + 1) * LANES]
            wide[c, pl.ds(i * PACK, PACK)] = part.reshape(PACK, SUB, LANES)
            turned[c, pl.ds(stride + i * PACK, PACK)] = pltpu.roll(part, HALF, 1).reshape(PACK, SUB, LANES)
        return unused

    lax.fori_loop(0, segment // PACK, load, 0, unroll=True)
    for c in range(4):
        for q in range(stride):
            turned[c, q] = pltpu.roll(turned[c, segment + q], 1, 0)
            turned[c, segment + stride + q] = pltpu.roll(turned[c, stride + q], SUB - 1, 0)

    lane = lax.broadcasted_iota(jnp.int32, (SUB, LANES), 1)
    low = lane < HALF
    initial, final = lane == 0, lane == LANES - 1
    inner_initial, inner_final = lane == HALF, lane == HALF - 1

    def neighbours(c, plane, j):
        spot = [j * stride + tile * planes + plane for tile in range(TRIPLE)]
        v0, v1, v2 = (wide[c, at] for at in spot)
        r0, r1, r2 = (turned[c, at + stride] for at in spot)
        after0 = r0 + turned[c, spot[0] + 2 * stride]
        after1 = r1 + turned[c, spot[1] + 2 * stride]
        before1 = r1 + turned[c, spot[1]]
        before2 = r2 + turned[c, spot[2]]
        across = (
            jnp.where(low, before1, before2),
            jnp.where(low, before2, after0),
            jnp.where(low, after0, after1),
        )
        plus = (
            jnp.where(initial, v1, v0),
            jnp.where(inner_initial, r0, jnp.where(initial, v2, v1)),
            jnp.where(initial, r1, v2),
        )
        minus = (
            jnp.where(final, r1, v0),
            jnp.where(inner_final, r2, jnp.where(final, v0, v1)),
            jnp.where(final, v1, v2),
        )
        sums = []
        for tile in range(TRIPLE):
            below = ends[0, c, j * TRIPLE + tile] if plane == 0 else wide[c, spot[tile] - 1]
            above = ends[1, c, j * TRIPLE + tile] if plane == planes - 1 else wide[c, spot[tile] + 1]
            along = pltpu.roll(plus[tile], LANES - 1, 1) + pltpu.roll(minus[tile], 1, 1)
            sums.append((across[tile] + along) + (below + above))
        return (v0, v1, v2), sums

    def step(j, unused):
        for plane in range(planes):
            (ur, nur), (ui, nui), (dr, ndr), (di, ndi) = (neighbours(c, plane, j) for c in range(4))
            for tile in range(TRIPLE):
                spot = j * stride + tile * planes + plane
                diag_up, bx, by, diag_down = (pot_ref[f, spot] for f in range(4))
                a, b, e, f = ur[tile], ui[tile], dr[tile], di[tile]
                flat[0, spot] = diag_up * a + bx * e + by * f - 0.5 * nur[tile]
                flat[1, spot] = diag_up * b + bx * f - by * e - 0.5 * nui[tile]
                flat[2, spot] = bx * a - by * b + diag_down * e - 0.5 * ndr[tile]
                flat[3, spot] = bx * b + by * a + diag_down * f - 0.5 * ndi[tile]
        return unused

    lax.fori_loop(0, steps, step, 0)

    def store(i, unused):
        at = pl.ds(i * PACK, PACK)
        block = jnp.concatenate([flat[c, at].reshape(PACK * SUB, LANES) for c in range(4)], axis=1)
        values = product(unspread, block.astype(jnp.bfloat16)).astype(jnp.bfloat16)
        for c in range(4):
            for s in range(SUB):
                out_ref[0, c, pl.ds(pl.multiple_of(s * segment + i * PACK, PACK), PACK), :] = values[
                    s * PACK : (s + 1) * PACK, c * LANES : (c + 1) * LANES
                ]
        return unused

    lax.fori_loop(0, segment // PACK, store, 0, unroll=True)


def apply_bands(x, potential, near, far, planes, start, carry):
    count, rows = near.shape[0], x.shape[2]
    segment = rows // SUB
    stride = planes * TRIPLE
    tiles = rows // planes
    halo = pl.BlockSpec((1, 4, tiles, LANES), lambda b: (b, 0, 0, 0))
    body = functools.partial(apply_body, planes, rows)
    in_specs = [
        pl.BlockSpec((1, 4, rows, LANES), lambda b: (start + b, 0, 0, 0)),
        pl.BlockSpec((4, segment, SUB, LANES), lambda b: (0, 0, 0, 0)),
        halo,
        halo,
    ]
    operands = [x, potential, near, far]
    aliases = {}
    if carry is not None:
        in_specs.append(pl.BlockSpec(memory_space=pl.ANY))
        operands.append(carry)
        aliases = {4: 0}
        call = body
    else:

        def call(x_ref, pot_ref, near_ref, far_ref, *rest):
            body(x_ref, pot_ref, near_ref, far_ref, None, *rest)

    return pl.pallas_call(
        call,
        grid=(count,),
        in_specs=in_specs,
        out_specs=[
            pl.BlockSpec((1, 4, rows, LANES), lambda b: (start + b, 0, 0, 0)),
            pl.BlockSpec(memory_space=pl.ANY),
        ],
        out_shape=[
            jax.ShapeDtypeStruct(x.shape, jnp.bfloat16),
            jax.ShapeDtypeStruct((SUB, LANES), jnp.float32),
        ],
        input_output_aliases=aliases,
        scratch_shapes=[
            pltpu.VMEM((4, segment, SUB, LANES), jnp.float32),
            pltpu.VMEM((2, 4, tiles // SUB, SUB, LANES), jnp.float32),
            pltpu.VMEM((4, segment + 2 * stride, SUB, LANES), jnp.float32),
            pltpu.VMEM((4, segment, SUB, LANES), jnp.float32),
        ],
        compiler_params=pltpu.CompilerParams(vmem_limit_bytes=VMEM_LIMIT),
        cost_estimate=SMALL,
        name="apply",
    )(*operands)


def chunk_sizes(bands):
    return [2] * (bands // 2) + [1] * (bands % 2)


def shards(spinors, kpt_mult, occupied, core_density, local_potential):
    bands, planes = spinors.shape[0], spinors.shape[2]
    total = bands * lax.axis_size("ka")
    size = lax.axis_size("brick")
    near_pairs = [(i, i ^ 1) for i in range(size) if i ^ 1 < size]
    far_pairs = [(i, j) for i in range(size) for j in [((i + 1) ^ 1) - 1] if 0 <= j < size]
    x = rows_view(spinors)
    core, local = rows_view(core_density), rows_view(local_potential)
    sizes = chunk_sizes(bands)
    starts = [sum(sizes[:k]) for k in range(len(sizes))]

    swap = lambda face: (lax.ppermute(face[0], "brick", near_pairs), lax.ppermute(face[1], "brick", far_pairs))
    faces = edges(x, planes, [(0, sizes[0])], (), VMEM_LIMIT)
    halos = [swap(faces[0])]
    density, others = front(x, kpt_mult, occupied, total, planes, sizes[1:], faces[0])
    faces += others
    halos += [swap(face) for face in faces[1:2]]
    density = group_sum(*density)
    gated = ()
    if len(starts) > 2:
        gated = gate(*faces[2], halos[0] + (density[0],))
        halos.append(swap(gated))
    potential = potential_of(*density, core, local, gated)
    out, token = None, ()
    for k, start in enumerate(starts):
        if 0 < k < len(starts) - 2:
            halos.append(swap(gate(*faces[k + 2], halos[k] + token)))
        out, done = apply_bands(x, potential, *halos[k], planes, start, out)
        token = (done,)
    return planes_view(out, planes)


def solution(mesh):
    placed = (P("ka", None, "brick", None), P("ka"), P("ka"), P("brick", None), P("brick", None))
    return jax.shard_map(
        shards, mesh=mesh, in_specs=placed, out_specs=P("ka", None, "brick", None), check_vma=False
    )
```

```python
import functools
import math

import jax
import jax.numpy as jnp
from jax import lax
from jax.experimental import pallas as pl
from jax.experimental.pallas import tpu as pltpu
from jax.sharding import PartitionSpec as P

NY = 192
LANES = 128
SUB = 8
TRIPLE = 3
HALF = 2 * NY - 2 * LANES - LANES // 2
PACK = 16
FLOOR_FRACTION = 0.05
VMEM_LIMIT = 63 * 1024 * 1024
UNROLL = 2
SMALL = pl.CostEstimate(flops=0, bytes_accessed=0, transcendentals=0)


def rows_view(x):
    lead, planes, cells = x.shape[:-2], x.shape[-2], x.shape[-1]
    tiles = cells // LANES
    n = len(lead)
    x = x.reshape(lead + (planes, tiles, LANES))
    x = x.transpose(tuple(range(n)) + (n + 1, n, n + 2))
    return x.reshape(lead + (tiles * planes, LANES))


def planes_view(x, planes):
    lead, rows = x.shape[:-2], x.shape[-2]
    tiles = rows // planes
    n = len(lead)
    x = x.reshape(lead + (tiles, planes, LANES))
    x = x.transpose(tuple(range(n)) + (n + 1, n, n + 2))
    return x.reshape(lead + (planes, tiles * LANES))


def even_brick():
    return lax.axis_index("brick") % 2 == 0


def spread_matrix(back):
    size = SUB * PACK
    row = lax.broadcasted_iota(jnp.int32, (size, size), 0)
    column = lax.broadcasted_iota(jnp.int32, (size, size), 1)
    if back:
        row, column = column, row
    return (column == (row % SUB) * PACK + row // SUB).astype(jnp.bfloat16)


def gathered(read, segment, i):
    return jnp.concatenate(
        [read(pl.ds(s * segment + i * PACK, PACK)) for s in range(SUB)], axis=0
    )


def product(matrix, values):
    return jnp.dot(matrix, values, preferred_element_type=jnp.float32)


def face_matrix(planes):
    out = PACK // planes * SUB
    row = lax.broadcasted_iota(jnp.int32, (2 * out, SUB * PACK), 0)
    column = lax.broadcasted_iota(jnp.int32, (2 * out, SUB * PACK), 1)
    upper = (row < out) == even_brick()
    inner = row % out
    wanted = (inner % SUB) * PACK + (inner // SUB) * planes + jnp.where(upper, planes - 1, 0)
    return (column == wanted).astype(jnp.bfloat16), out


def edges_body(planes, chunks, x_ref, *refs):
    faces, held, sems = refs[-2 - 2 * len(chunks) : -2], refs[-2], refs[-1]
    first = chunks[0][0]
    bands = [(start - first + b, k, b) for k, (start, count) in enumerate(chunks) for b in range(count)]
    rows = held.shape[2]
    segment = rows // SUB
    copies = [pltpu.make_async_copy(x_ref.at[first + i], held.at[i], sems.at[i]) for i, _, _ in bands]
    for copy in copies:
        copy.start()
    select, out = face_matrix(planes)
    for i, k, b in bands:
        copies[i].wait()
        near_ref, far_ref = faces[2 * k], faces[2 * k + 1]
        for part in range(segment // PACK):
            block = jnp.concatenate(
                [gathered(lambda at: held[i, c, at, :], segment, part) for c in range(4)], axis=1
            )
            picked = product(select, block).astype(jnp.bfloat16)
            at = pl.ds(part * out, out)
            for c in range(4):
                lanes = slice(c * LANES, (c + 1) * LANES)
                near_ref[b, c, at, :] = picked[:out, lanes]
                far_ref[b, c, at, :] = picked[out:, lanes]


def edges(x, planes, chunks, after, limit):
    rows = x.shape[2]
    total = sum(count for _, count in chunks)
    shapes = [
        jax.ShapeDtypeStruct((count, 4, rows // planes, LANES), jnp.bfloat16) for _, count in chunks for _ in range(2)
    ]
    faces = pl.pallas_call(
        functools.partial(edges_body, planes, chunks),
        in_specs=[pl.BlockSpec(memory_space=pltpu.HBM)] + [pl.BlockSpec(memory_space=pl.ANY)] * len(after),
        out_shape=shapes,
        scratch_shapes=[pltpu.VMEM((total, 4, rows, LANES), jnp.bfloat16), pltpu.SemaphoreType.DMA((total,))],
        compiler_params=pltpu.CompilerParams(vmem_limit_bytes=limit),
        cost_estimate=SMALL,
        name="edges",
    )(x, *after)
    return [tuple(faces[2 * k : 2 * k + 2]) for k in range(len(chunks))]


def gate(near, far, after):
    anywhere = pl.BlockSpec(memory_space=pl.ANY)
    return pl.pallas_call(
        lambda *refs: None,
        in_specs=[anywhere] * (2 + len(after)),
        out_specs=[anywhere, anywhere],
        out_shape=[jax.ShapeDtypeStruct(a.shape, a.dtype) for a in (near, far)],
        input_output_aliases={0: 0, 1: 1},
        compiler_params=pltpu.CompilerParams(vmem_limit_bytes=VMEM_LIMIT),
        name="gate",
    )(near, far, *after)


def front_body(planes, scale, counts, mult_ref, occ_ref, x_ref, *refs):
    bands = x_ref.shape[0]
    first = len(refs) - 2 * len(counts)
    mine_ref, other_ref, faces = refs[first - 2], refs[first - 1], refs[first:]
    lower_half = holds_lower_half()
    weights = [(mult_ref[b] * occ_ref[b]).astype(jnp.float32) * scale for b in range(bands)]
    for s in range(SUB):
        up = down = real = imag = None
        for b in range(bands):
            ur, ui, dr, di = (x_ref[b, c, s].astype(jnp.float32) for c in range(4))
            wur, wui = weights[b] * ur, weights[b] * ui
            wdr, wdi = weights[b] * dr, weights[b] * di
            terms = (
                wur * ur + wui * ui,
                wdr * dr + wdi * di,
                wur * dr + wui * di,
                wur * di - wui * dr,
            )
            if b == 0:
                up, down, real, imag = terms
            else:
                up, down, real, imag = up + terms[0], down + terms[1], real + terms[2], imag + terms[3]
        fields = (up + down, 2.0 * real, 2.0 * imag, up - down)
        for f in range(2):
            mine_ref[f, s] = jnp.where(lower_half, fields[f], fields[f + 2]).astype(jnp.bfloat16)
            other_ref[f, s] = jnp.where(lower_half, fields[f + 2], fields[f]).astype(jnp.bfloat16)
    if counts:
        select, out = face_matrix(planes)
    band = bands - sum(counts)
    for k, count in enumerate(counts):
        for b in range(count):
            block = jnp.concatenate(
                [x_ref[band, c].reshape(SUB * PACK, LANES) for c in range(4)], axis=1
            )
            picked = product(select, block).astype(jnp.bfloat16)
            for c in range(4):
                lanes = slice(c * LANES, (c + 1) * LANES)
                faces[2 * k][b, c] = picked[:out, lanes]
                faces[2 * k + 1][b, c] = picked[out:, lanes]
            band += 1


def front(x, mult, occ, total, planes, counts, after):
    bands, rows = x.shape[0], x.shape[2]
    segment = rows // SUB
    out = PACK // planes * SUB
    anywhere = pl.BlockSpec(memory_space=pl.ANY)
    results = pl.pallas_call(
        functools.partial(front_body, planes, 1.0 / (2.0 * total), counts),
        grid=(segment // PACK,),
        in_specs=[
            pl.BlockSpec(memory_space=pltpu.SMEM),
            pl.BlockSpec(memory_space=pltpu.SMEM),
            pl.BlockSpec((bands, 4, SUB, PACK, LANES), lambda i: (0, 0, 0, i, 0)),
        ]
        + [anywhere] * len(after),
        out_specs=[pl.BlockSpec((2, SUB, PACK, LANES), lambda i: (0, 0, i, 0))] * 2
        + [pl.BlockSpec((count, 4, out, LANES), lambda i: (0, 0, i, 0)) for count in counts for _ in range(2)],
        out_shape=[jax.ShapeDtypeStruct((2, SUB, segment, LANES), jnp.bfloat16)] * 2
        + [
            jax.ShapeDtypeStruct((count, 4, rows // planes, LANES), jnp.bfloat16)
            for count in counts
            for _ in range(2)
        ],
        compiler_params=pltpu.CompilerParams(vmem_limit_bytes=VMEM_LIMIT),
        cost_estimate=SMALL,
        name="front",
    )(mult, occ, x.reshape(bands, 4, SUB, segment, LANES), *after)
    halves = [half.reshape(2, rows, LANES) for half in results[:2]]
    return halves, [tuple(results[2 + 2 * k : 4 + 2 * k]) for k in range(len(counts))]


def add_body(a_ref, b_ref, out_ref):
    out_ref[...] = (a_ref[...].astype(jnp.float32) + b_ref[...].astype(jnp.float32)).astype(jnp.bfloat16)


def add(a, b):
    whole = pl.BlockSpec(memory_space=pltpu.VMEM)
    return pl.pallas_call(
        add_body,
        in_specs=[whole, whole],
        out_specs=whole,
        out_shape=jax.ShapeDtypeStruct(a.shape, a.dtype),
        compiler_params=pltpu.CompilerParams(vmem_limit_bytes=VMEM_LIMIT),
        cost_estimate=SMALL,
        name="add",
    )(a, b)


def holds_lower_half():
    return lax.axis_index("ka") % 2 == 0


def group_sum(mine, other):
    size = lax.axis_size("ka")
    assert size % 2 == 0
    partner = [(i, i ^ 1) for i in range(size)]

    def swaps(_, fields):
        total, given = fields
        total = add(total, lax.ppermute(given, "ka", partner))
        turning = total
        for _ in range(size // 2 - 1):
            turning = lax.ppermute(turning, "ka", [(i, (i + 2) % size) for i in range(size)])
            total = add(total, turning)
        return total, lax.ppermute(total, "ka", partner)

    trips = 1 + lax.div(lax.axis_index("ka"), size)
    return lax.fori_loop(0, trips, swaps, (mine, other))


def cube_root(x):
    root = jnp.exp(jnp.log(jnp.abs(x)) * (1.0 / 3.0))
    return jnp.where(x < 0.0, -root, root)


def potential_body(rows, mine_ref, other_ref, core_ref, local_ref, *refs):
    out_ref = refs[-1]
    segment = rows // SUB
    spread = spread_matrix(False)

    lower_half = holds_lower_half()

    def step(i, unused):
        block = jnp.concatenate(
            [gathered(lambda at: ref[f, at, :], segment, i) for ref in (mine_ref, other_ref) for f in range(2)], axis=1
        )
        fields = product(spread, block)
        m0, m1, o0, o1 = (fields[:, f * LANES : (f + 1) * LANES] for f in range(4))
        d0, d1 = jnp.where(lower_half, m0, o0), jnp.where(lower_half, m1, o1)
        d2, d3 = jnp.where(lower_half, o0, m0), jnp.where(lower_half, o1, m1)
        here = [pl.ds(i * PACK + r, SUB, stride=segment) for r in range(PACK)]
        core = jnp.concatenate([core_ref[at, :] for at in here], axis=0)
        local = jnp.concatenate([local_ref[at, :] for at in here], axis=0)
        electrons = d0 + core
        magnitude = jnp.sqrt(d1 * d1 + d2 * d2 + d3 * d3)
        upper = -cube_root((3.0 / math.pi) * (electrons + magnitude))
        lower = -cube_root((3.0 / math.pi) * (electrons - magnitude))
        factor = 0.5 * (upper - lower) / jnp.maximum(magnitude, FLOOR_FRACTION * electrons)
        v = 0.5 * (upper + lower) + local
        bz = factor * d3
        at = pl.ds(i * PACK, PACK)
        shape = (PACK, SUB, LANES)
        out_ref[0, at] = (v + bz + 3.0).reshape(shape)
        out_ref[1, at] = (factor * d1).reshape(shape)
        out_ref[2, at] = (factor * d2).reshape(shape)
        out_ref[3, at] = (v - bz + 3.0).reshape(shape)
        return unused

    lax.fori_loop(0, segment // PACK, step, 0, unroll=True)


def potential_of(mine, other, core, local, after):
    rows = mine.shape[1]
    whole = pl.BlockSpec(memory_space=pltpu.VMEM)
    return pl.pallas_call(
        functools.partial(potential_body, rows),
        in_specs=[whole] * 4 + [pl.BlockSpec(memory_space=pl.ANY)] * len(after),
        out_specs=whole,
        out_shape=jax.ShapeDtypeStruct((4, rows // SUB, SUB, LANES), jnp.float32),
        compiler_params=pltpu.CompilerParams(vmem_limit_bytes=VMEM_LIMIT),
        cost_estimate=SMALL,
        name="potential",
    )(mine, other, core, local, *after)


def hamiltonian(planes, x_ref, pot_ref, ends, flat, wide, turned):
    segment = wide.shape[1]
    stride = planes * TRIPLE
    steps = segment // stride
    spread = spread_matrix(False)

    def load(i, unused):
        block = jnp.concatenate([gathered(lambda at: x_ref[0, c, at, :], segment, i) for c in range(4)], axis=1)
        values = product(spread, block)
        for c in range(4):
            part = values[:, c * LANES : (c + 1) * LANES]
            wide[c, pl.ds(i * PACK, PACK)] = part.reshape(PACK, SUB, LANES)
            turned[c, pl.ds(stride + i * PACK, PACK)] = pltpu.roll(part, HALF, 1).reshape(PACK, SUB, LANES)
        return unused

    lax.fori_loop(0, segment // PACK, load, 0, unroll=True)
    for c in range(4):
        for q in range(stride):
            turned[c, q] = pltpu.roll(turned[c, segment + q], 1, 0)
            turned[c, segment + stride + q] = pltpu.roll(turned[c, stride + q], SUB - 1, 0)

    lane = lax.broadcasted_iota(jnp.int32, (SUB, LANES), 1)
    low = lane < HALF
    initial, final = lane == 0, lane == LANES - 1
    inner_initial, inner_final = lane == HALF, lane == HALF - 1

    def neighbours(c, plane, j):
        spot = [j * stride + tile * planes + plane for tile in range(TRIPLE)]
        v0, v1, v2 = (wide[c, at] for at in spot)
        r0, r1, r2 = (turned[c, at + stride] for at in spot)
        after0 = r0 + turned[c, spot[0] + 2 * stride]
        after1 = r1 + turned[c, spot[1] + 2 * stride]
        before1 = r1 + turned[c, spot[1]]
        before2 = r2 + turned[c, spot[2]]
        across = (
            jnp.where(low, before1, before2),
            jnp.where(low, before2, after0),
            jnp.where(low, after0, after1),
        )
        plus = (
            jnp.where(initial, v1, v0),
            jnp.where(inner_initial, r0, jnp.where(initial, v2, v1)),
            jnp.where(initial, r1, v2),
        )
        minus = (
            jnp.where(final, r1, v0),
            jnp.where(inner_final, r2, jnp.where(final, v0, v1)),
            jnp.where(final, v1, v2),
        )
        sums = []
        for tile in range(TRIPLE):
            total = across[tile] + (pltpu.roll(plus[tile], LANES - 1, 1) + pltpu.roll(minus[tile], 1, 1))
            if plane > 0:
                total = total + wide[c, spot[tile] - 1]
            elif ends is not None:
                total = total + ends[0, c, j * TRIPLE + tile]
            if plane < planes - 1:
                total = total + wide[c, spot[tile] + 1]
            elif ends is not None:
                total = total + ends[1, c, j * TRIPLE + tile]
            sums.append(total)
        return (v0, v1, v2), sums

    def step(j, unused):
        for plane in range(planes):
            (ur, nur), (ui, nui), (dr, ndr), (di, ndi) = (neighbours(c, plane, j) for c in range(4))
            for tile in range(TRIPLE):
                spot = j * stride + tile * planes + plane
                diag_up, bx, by, diag_down = (pot_ref[f, spot] for f in range(4))
                a, b, e, f = ur[tile], ui[tile], dr[tile], di[tile]
                flat[0, spot] = diag_up * a + bx * e + by * f - 0.5 * nur[tile]
                flat[1, spot] = diag_up * b + bx * f - by * e - 0.5 * nui[tile]
                flat[2, spot] = bx * a - by * b + diag_down * e - 0.5 * ndr[tile]
                flat[3, spot] = bx * b + by * a + diag_down * f - 0.5 * ndi[tile]
        return unused

    lax.fori_loop(0, steps, step, 0, unroll=UNROLL)


def store_rows(parts, i, out_ref):
    block = jnp.concatenate([part.astype(jnp.bfloat16) for part in parts], axis=1)
    values = product(spread_matrix(True), block).astype(jnp.bfloat16)
    for c in range(4):
        for s in range(SUB):
            out_ref[0, c, s, pl.ds(i * PACK, PACK), :] = values[s * PACK : (s + 1) * PACK, c * LANES : (c + 1) * LANES]


def apply_body(planes, x_ref, pot_ref, near_ref, far_ref, *refs):
    out_ref, token_ref, wide, turned, ends, flat = refs[-6:]
    near_slot = jnp.where(even_brick(), 1, 0)
    for c in range(4):
        ends[near_slot, c] = near_ref[0, c].astype(jnp.float32).reshape(ends.shape[2:])
        ends[1 - near_slot, c] = far_ref[0, c].astype(jnp.float32).reshape(ends.shape[2:])
    hamiltonian(planes, x_ref, pot_ref, ends, flat, wide, turned)
    for i in range(wide.shape[1] // PACK):
        store_rows([flat[c, pl.ds(i * PACK, PACK)].reshape(PACK * SUB, LANES) for c in range(4)], i, out_ref)


def ahead_body(planes, x_ref, pot_ref, *refs):
    flat_ref, token_ref, wide, turned = refs[-4:]
    hamiltonian(planes, x_ref, pot_ref, None, flat_ref.at[0], wide, turned)


def finish_body(planes, flat_ref, near_ref, far_ref, *refs):
    out_ref, token_ref = refs[-2:]
    even = even_brick()
    per = PACK // planes
    for i in range(flat_ref.shape[2] // PACK):
        outside = pl.ds(i * per * SUB, per * SUB)
        parts = []
        for c in range(4):
            near = near_ref[0, c, outside, :].astype(jnp.float32).reshape(per, SUB, LANES)
            far = far_ref[0, c, outside, :].astype(jnp.float32).reshape(per, SUB, LANES)
            below, above = jnp.where(even, far, near), jnp.where(even, near, far)
            pieces = []
            for q in range(PACK):
                piece = flat_ref[0, c, i * PACK + q]
                if q % planes == 0:
                    piece = piece - 0.5 * below[q // planes]
                if q % planes == planes - 1:
                    piece = piece - 0.5 * above[q // planes]
                pieces.append(piece)
            parts.append(jnp.concatenate(pieces, axis=0))
        store_rows(parts, i, out_ref)


def per_band(body, name, grid, inputs, in_specs, output, out_spec, carry, after, scratch):
    anywhere = pl.BlockSpec(memory_space=pl.ANY)
    carried = () if carry is None else (carry,)
    return pl.pallas_call(
        body,
        grid=grid,
        in_specs=in_specs + [anywhere] * (len(carried) + len(after)),
        out_specs=[out_spec, anywhere],
        out_shape=[
            jax.ShapeDtypeStruct(*output),
            jax.ShapeDtypeStruct((SUB, LANES), jnp.float32),
        ],
        input_output_aliases={len(inputs): 0} if carried else {},
        scratch_shapes=scratch,
        compiler_params=pltpu.CompilerParams(vmem_limit_bytes=VMEM_LIMIT),
        cost_estimate=SMALL,
        name=name,
    )(*inputs, *carried, *after)


def stencil_specs(rows, planes, start):
    segment = rows // SUB
    scratch = [
        pltpu.VMEM((4, segment, SUB, LANES), jnp.float32),
        pltpu.VMEM((4, segment + 2 * planes * TRIPLE, SUB, LANES), jnp.float32),
    ]
    in_specs = [
        pl.BlockSpec((1, 4, rows, LANES), lambda b: (start + b, 0, 0, 0)),
        pl.BlockSpec((4, segment, SUB, LANES), lambda b: (0, 0, 0, 0)),
    ]
    return in_specs, scratch


def apply_bands(x, potential, near, far, planes, start, carry, after):
    count, bands, rows = near.shape[0], x.shape[0], x.shape[2]
    segment, tiles = rows // SUB, rows // planes
    in_specs, scratch = stencil_specs(rows, planes, start)
    halo = pl.BlockSpec((1, 4, tiles, LANES), lambda b: (b, 0, 0, 0))
    scratch += [
        pltpu.VMEM((2, 4, tiles // SUB, SUB, LANES), jnp.float32),
        pltpu.VMEM((4, segment, SUB, LANES), jnp.float32),
    ]
    return per_band(
        functools.partial(apply_body, planes),
        "apply",
        (count,),
        (x, potential, near, far),
        in_specs + [halo, halo],
        ((bands, 4, SUB, segment, LANES), jnp.bfloat16),
        pl.BlockSpec((1, 4, SUB, segment, LANES), lambda b: (start + b, 0, 0, 0, 0)),
        carry,
        after,
        scratch,
    )


def ahead_of(x, potential, planes, start, count, after):
    segment = x.shape[2] // SUB
    in_specs, scratch = stencil_specs(x.shape[2], planes, start)
    return per_band(
        functools.partial(ahead_body, planes),
        "ahead",
        (count,),
        (x, potential),
        in_specs,
        ((count, 4, segment, SUB, LANES), jnp.float32),
        pl.BlockSpec((1, 4, segment, SUB, LANES), lambda b: (b, 0, 0, 0, 0)),
        None,
        after,
        scratch,
    )


def finish(flat, near, far, planes, start, carry):
    count, segment = flat.shape[0], flat.shape[2]
    part = segment // 3 if segment % (3 * PACK) == 0 else segment
    halo = pl.BlockSpec((1, 4, part // planes * SUB, LANES), lambda b, i: (b, 0, i, 0))
    return per_band(
        functools.partial(finish_body, planes),
        "finish",
        (count, segment // part),
        (flat, near, far),
        [pl.BlockSpec((1, 4, part, SUB, LANES), lambda b, i: (b, 0, i, 0, 0)), halo, halo],
        (carry.shape, carry.dtype),
        pl.BlockSpec((1, 4, SUB, part, LANES), lambda b, i: (start + b, 0, 0, i, 0)),
        carry,
        (),
        [],
    )


def chunk_sizes(bands):
    return [2] * (bands // 2) + [1] * (bands % 2)


def shards(spinors, kpt_mult, occupied, core_density, local_potential):
    bands, planes = spinors.shape[0], spinors.shape[2]
    total = bands * lax.axis_size("ka")
    size = lax.axis_size("brick")
    near_pairs = [(i, i ^ 1) for i in range(size) if i ^ 1 < size]
    far_pairs = [(i, j) for i in range(size) for j in [((i + 1) ^ 1) - 1] if 0 <= j < size]
    x = rows_view(spinors)
    core, local = rows_view(core_density), rows_view(local_potential)
    sizes = chunk_sizes(bands)
    starts = [sum(sizes[:k]) for k in range(len(sizes))]

    swap = lambda face: (lax.ppermute(face[0], "brick", near_pairs), lax.ppermute(face[1], "brick", far_pairs))
    faces = edges(x, planes, [(0, sizes[0])], (), VMEM_LIMIT)
    halos = [swap(faces[0])]
    density, others = front(x, kpt_mult, occupied, total, planes, sizes[1:], faces[0])
    faces += others
    halos += [swap(face) for face in faces[1:2]]
    density = group_sum(*density)
    gated = ()
    if len(starts) > 2:
        gated = gate(*faces[2], halos[0] + (density[0],))
        halos.append(swap(gated))
    potential = potential_of(*density, core, local, gated)
    last = len(starts) - 1
    out, token, flat = None, (), None
    for k, start in enumerate(starts):
        if 0 < k < last - 1:
            halos.append(swap(gate(*faces[k + 2], halos[k] + token)))
        if k > 0 and k == last - 1:
            flat, done = ahead_of(x, potential, planes, starts[last], sizes[last], token)
            token = (done,)
        if flat is None or k < last:
            out, done = apply_bands(x, potential, *halos[k], planes, start, out, token)
        else:
            out, done = finish(flat, *halos[k], planes, start, out)
        token = (done,)
    return planes_view(out.reshape(x.shape), planes)


def solution(mesh):
    placed = (P("ka", None, "brick", None), P("ka"), P("ka"), P("brick", None), P("brick", None))
    return jax.shard_map(
        shards, mesh=mesh, in_specs=placed, out_specs=P("ka", None, "brick", None), check_vma=False
    )
```

```python
import functools
import math

import jax
import jax.numpy as jnp
from jax import lax
from jax.experimental import pallas as pl
from jax.experimental.pallas import tpu as pltpu
from jax.sharding import PartitionSpec as P

NY = 192
LANES = 128
SUB = 8
TRIPLE = 3
HALF = 2 * NY - 2 * LANES - LANES // 2
PACK = 16
FLOOR_FRACTION = 0.05
VMEM_LIMIT = 63 * 1024 * 1024
UNROLL = 2
SMALL = pl.CostEstimate(flops=0, bytes_accessed=0, transcendentals=0)


def rows_view(x):
    lead, planes, cells = x.shape[:-2], x.shape[-2], x.shape[-1]
    tiles = cells // LANES
    n = len(lead)
    x = x.reshape(lead + (planes, tiles, LANES))
    x = x.transpose(tuple(range(n)) + (n + 1, n, n + 2))
    return x.reshape(lead + (tiles * planes, LANES))


def planes_view(x, planes):
    lead, rows = x.shape[:-2], x.shape[-2]
    tiles = rows // planes
    n = len(lead)
    x = x.reshape(lead + (tiles, planes, LANES))
    x = x.transpose(tuple(range(n)) + (n + 1, n, n + 2))
    return x.reshape(lead + (planes, tiles * LANES))


def even_brick():
    return lax.axis_index("brick") % 2 == 0


def spread_matrix(back):
    size = SUB * PACK
    row = lax.broadcasted_iota(jnp.int32, (size, size), 0)
    column = lax.broadcasted_iota(jnp.int32, (size, size), 1)
    if back:
        row, column = column, row
    return (column == (row % SUB) * PACK + row // SUB).astype(jnp.bfloat16)


def gathered(read, segment, i):
    return jnp.concatenate(
        [read(pl.ds(s * segment + i * PACK, PACK)) for s in range(SUB)], axis=0
    )


def product(matrix, values):
    return jnp.dot(matrix, values, preferred_element_type=jnp.float32)


def face_matrix(planes):
    out = PACK // planes * SUB
    row = lax.broadcasted_iota(jnp.int32, (2 * out, SUB * PACK), 0)
    column = lax.broadcasted_iota(jnp.int32, (2 * out, SUB * PACK), 1)
    upper = (row < out) == even_brick()
    inner = row % out
    wanted = (inner % SUB) * PACK + (inner // SUB) * planes + jnp.where(upper, planes - 1, 0)
    return (column == wanted).astype(jnp.bfloat16), out


def edges_body(planes, chunks, x_ref, *refs):
    faces, held, sems = refs[-2 - 2 * len(chunks) : -2], refs[-2], refs[-1]
    first = chunks[0][0]
    bands = [(start - first + b, k, b) for k, (start, count) in enumerate(chunks) for b in range(count)]
    rows = held.shape[2]
    segment = rows // SUB
    copies = [pltpu.make_async_copy(x_ref.at[first + i], held.at[i], sems.at[i]) for i, _, _ in bands]
    for copy in copies:
        copy.start()
    select, out = face_matrix(planes)
    for i, k, b in bands:
        copies[i].wait()
        near_ref, far_ref = faces[2 * k], faces[2 * k + 1]
        for part in range(segment // PACK):
            block = jnp.concatenate(
                [gathered(lambda at: held[i, c, at, :], segment, part) for c in range(4)], axis=1
            )
            picked = product(select, block).astype(jnp.bfloat16)
            at = pl.ds(part * out, out)
            for c in range(4):
                lanes = slice(c * LANES, (c + 1) * LANES)
                near_ref[b, c, at, :] = picked[:out, lanes]
                far_ref[b, c, at, :] = picked[out:, lanes]


def edges(x, planes, chunks, after, limit):
    rows = x.shape[2]
    total = sum(count for _, count in chunks)
    shapes = [
        jax.ShapeDtypeStruct((count, 4, rows // planes, LANES), jnp.bfloat16) for _, count in chunks for _ in range(2)
    ]
    faces = pl.pallas_call(
        functools.partial(edges_body, planes, chunks),
        in_specs=[pl.BlockSpec(memory_space=pltpu.HBM)] + [pl.BlockSpec(memory_space=pl.ANY)] * len(after),
        out_shape=shapes,
        scratch_shapes=[pltpu.VMEM((total, 4, rows, LANES), jnp.bfloat16), pltpu.SemaphoreType.DMA((total,))],
        compiler_params=pltpu.CompilerParams(vmem_limit_bytes=limit),
        cost_estimate=SMALL,
        name="edges",
    )(x, *after)
    return [tuple(faces[2 * k : 2 * k + 2]) for k in range(len(chunks))]


def gate(near, far, after):
    anywhere = pl.BlockSpec(memory_space=pl.ANY)
    return pl.pallas_call(
        lambda *refs: None,
        in_specs=[anywhere] * (2 + len(after)),
        out_specs=[anywhere, anywhere],
        out_shape=[jax.ShapeDtypeStruct(a.shape, a.dtype) for a in (near, far)],
        input_output_aliases={0: 0, 1: 1},
        compiler_params=pltpu.CompilerParams(vmem_limit_bytes=VMEM_LIMIT),
        name="gate",
    )(near, far, *after)


def front_body(planes, scale, counts, mult_ref, occ_ref, x_ref, *refs):
    bands = x_ref.shape[0]
    first = len(refs) - 2 * len(counts)
    mine_ref, other_ref, faces = refs[first - 2], refs[first - 1], refs[first:]
    lower_half = holds_lower_half()
    weights = [(mult_ref[b] * occ_ref[b]).astype(jnp.float32) * scale for b in range(bands)]
    for s in range(SUB):
        up = down = real = imag = None
        for b in range(bands):
            ur, ui, dr, di = (x_ref[b, c, s].astype(jnp.float32) for c in range(4))
            wur, wui = weights[b] * ur, weights[b] * ui
            wdr, wdi = weights[b] * dr, weights[b] * di
            terms = (
                wur * ur + wui * ui,
                wdr * dr + wdi * di,
                wur * dr + wui * di,
                wur * di - wui * dr,
            )
            if b == 0:
                up, down, real, imag = terms
            else:
                up, down, real, imag = up + terms[0], down + terms[1], real + terms[2], imag + terms[3]
        fields = (up + down, 2.0 * real, 2.0 * imag, up - down)
        for f in range(2):
            mine_ref[f, s] = jnp.where(lower_half, fields[f], fields[f + 2]).astype(jnp.bfloat16)
            other_ref[f, s] = jnp.where(lower_half, fields[f + 2], fields[f]).astype(jnp.bfloat16)
    if counts:
        select, out = face_matrix(planes)
    band = bands - sum(counts)
    for k, count in enumerate(counts):
        for b in range(count):
            block = jnp.concatenate(
                [x_ref[band, c].reshape(SUB * PACK, LANES) for c in range(4)], axis=1
            )
            picked = product(select, block).astype(jnp.bfloat16)
            for c in range(4):
                lanes = slice(c * LANES, (c + 1) * LANES)
                faces[2 * k][b, c] = picked[:out, lanes]
                faces[2 * k + 1][b, c] = picked[out:, lanes]
            band += 1


def front(x, mult, occ, total, planes, counts, after):
    bands, rows = x.shape[0], x.shape[2]
    segment = rows // SUB
    out = PACK // planes * SUB
    anywhere = pl.BlockSpec(memory_space=pl.ANY)
    results = pl.pallas_call(
        functools.partial(front_body, planes, 1.0 / (2.0 * total), counts),
        grid=(segment // PACK,),
        in_specs=[
            pl.BlockSpec(memory_space=pltpu.SMEM),
            pl.BlockSpec(memory_space=pltpu.SMEM),
            pl.BlockSpec((bands, 4, SUB, PACK, LANES), lambda i: (0, 0, 0, i, 0)),
        ]
        + [anywhere] * len(after),
        out_specs=[pl.BlockSpec((2, SUB, PACK, LANES), lambda i: (0, 0, i, 0))] * 2
        + [pl.BlockSpec((count, 4, out, LANES), lambda i: (0, 0, i, 0)) for count in counts for _ in range(2)],
        out_shape=[jax.ShapeDtypeStruct((2, SUB, segment, LANES), jnp.bfloat16)] * 2
        + [
            jax.ShapeDtypeStruct((count, 4, rows // planes, LANES), jnp.bfloat16)
            for count in counts
            for _ in range(2)
        ],
        compiler_params=pltpu.CompilerParams(vmem_limit_bytes=VMEM_LIMIT),
        cost_estimate=SMALL,
        name="front",
    )(mult, occ, x.reshape(bands, 4, SUB, segment, LANES), *after)
    halves = [half.reshape(2, rows, LANES) for half in results[:2]]
    return halves, [tuple(results[2 + 2 * k : 4 + 2 * k]) for k in range(len(counts))]


def add_body(a_ref, b_ref, out_ref):
    out_ref[...] = (a_ref[...].astype(jnp.float32) + b_ref[...].astype(jnp.float32)).astype(jnp.bfloat16)


def add(a, b):
    whole = pl.BlockSpec(memory_space=pltpu.VMEM)
    return pl.pallas_call(
        add_body,
        in_specs=[whole, whole],
        out_specs=whole,
        out_shape=jax.ShapeDtypeStruct(a.shape, a.dtype),
        compiler_params=pltpu.CompilerParams(vmem_limit_bytes=VMEM_LIMIT),
        cost_estimate=SMALL,
        name="add",
    )(a, b)


def holds_lower_half():
    return lax.axis_index("ka") % 2 == 0


def group_sum(mine, other):
    size = lax.axis_size("ka")
    assert size % 2 == 0
    partner = [(i, i ^ 1) for i in range(size)]

    def swaps(_, fields):
        total, given = fields
        total = add(total, lax.ppermute(given, "ka", partner))
        turning = total
        for _ in range(size // 2 - 1):
            turning = lax.ppermute(turning, "ka", [(i, (i + 2) % size) for i in range(size)])
            total = add(total, turning)
        return total, lax.ppermute(total, "ka", partner)

    trips = 1 + lax.div(lax.axis_index("ka"), size)
    return lax.fori_loop(0, trips, swaps, (mine, other))


def cube_root(x):
    root = jnp.exp(jnp.log(jnp.abs(x)) * (1.0 / 3.0))
    return jnp.where(x < 0.0, -root, root)


def potential_body(rows, mine_ref, other_ref, core_ref, local_ref, *refs):
    out_ref = refs[-1]
    segment = rows // SUB
    spread = spread_matrix(False)

    lower_half = holds_lower_half()

    def step(i, unused):
        block = jnp.concatenate(
            [gathered(lambda at: ref[f, at, :], segment, i) for ref in (mine_ref, other_ref) for f in range(2)], axis=1
        )
        fields = product(spread, block)
        m0, m1, o0, o1 = (fields[:, f * LANES : (f + 1) * LANES] for f in range(4))
        d0, d1 = jnp.where(lower_half, m0, o0), jnp.where(lower_half, m1, o1)
        d2, d3 = jnp.where(lower_half, o0, m0), jnp.where(lower_half, o1, m1)
        here = [pl.ds(i * PACK + r, SUB, stride=segment) for r in range(PACK)]
        core = jnp.concatenate([core_ref[at, :] for at in here], axis=0)
        local = jnp.concatenate([local_ref[at, :] for at in here], axis=0)
        electrons = d0 + core
        magnitude = jnp.sqrt(d1 * d1 + d2 * d2 + d3 * d3)
        upper = -cube_root((3.0 / math.pi) * (electrons + magnitude))
        lower = -cube_root((3.0 / math.pi) * (electrons - magnitude))
        factor = 0.5 * (upper - lower) / jnp.maximum(magnitude, FLOOR_FRACTION * electrons)
        v = 0.5 * (upper + lower) + local
        bz = factor * d3
        at = pl.ds(i * PACK, PACK)
        shape = (PACK, SUB, LANES)
        out_ref[0, at] = (v + bz + 3.0).reshape(shape)
        out_ref[1, at] = (factor * d1).reshape(shape)
        out_ref[2, at] = (factor * d2).reshape(shape)
        out_ref[3, at] = (v - bz + 3.0).reshape(shape)
        return unused

    lax.fori_loop(0, segment // PACK, step, 0, unroll=True)


def potential_of(mine, other, core, local, after):
    rows = mine.shape[1]
    whole = pl.BlockSpec(memory_space=pltpu.VMEM)
    return pl.pallas_call(
        functools.partial(potential_body, rows),
        in_specs=[whole] * 4 + [pl.BlockSpec(memory_space=pl.ANY)] * len(after),
        out_specs=whole,
        out_shape=jax.ShapeDtypeStruct((4, rows // SUB, SUB, LANES), jnp.float32),
        compiler_params=pltpu.CompilerParams(vmem_limit_bytes=VMEM_LIMIT),
        cost_estimate=SMALL,
        name="potential",
    )(mine, other, core, local, *after)


def hamiltonian(planes, x_ref, pot_ref, ends, flat, wide, turned):
    segment = wide.shape[1]
    stride = planes * TRIPLE
    steps = segment // stride
    spread = spread_matrix(False)

    def load(i, unused):
        block = jnp.concatenate([gathered(lambda at: x_ref[0, c, at, :], segment, i) for c in range(4)], axis=1)
        values = product(spread, block)
        for c in range(4):
            part = values[:, c * LANES : (c + 1) * LANES]
            wide[c, pl.ds(i * PACK, PACK)] = part.reshape(PACK, SUB, LANES)
            turned[c, pl.ds(stride + i * PACK, PACK)] = pltpu.roll(part, HALF, 1).reshape(PACK, SUB, LANES)
        return unused

    lax.fori_loop(0, segment // PACK, load, 0, unroll=True)
    for c in range(4):
        for q in range(stride):
            turned[c, q] = pltpu.roll(turned[c, segment + q], 1, 0)
            turned[c, segment + stride + q] = pltpu.roll(turned[c, stride + q], SUB - 1, 0)

    lane = lax.broadcasted_iota(jnp.int32, (SUB, LANES), 1)
    low = lane < HALF
    initial, final = lane == 0, lane == LANES - 1
    inner_initial, inner_final = lane == HALF, lane == HALF - 1

    def neighbours(c, plane, j):
        spot = [j * stride + tile * planes + plane for tile in range(TRIPLE)]
        v0, v1, v2 = (wide[c, at] for at in spot)
        r0, r1, r2 = (turned[c, at + stride] for at in spot)
        after0 = r0 + turned[c, spot[0] + 2 * stride]
        after1 = r1 + turned[c, spot[1] + 2 * stride]
        before1 = r1 + turned[c, spot[1]]
        before2 = r2 + turned[c, spot[2]]
        across = (
            jnp.where(low, before1, before2),
            jnp.where(low, before2, after0),
            jnp.where(low, after0, after1),
        )
        plus = (
            jnp.where(initial, v1, v0),
            jnp.where(inner_initial, r0, jnp.where(initial, v2, v1)),
            jnp.where(initial, r1, v2),
        )
        minus = (
            jnp.where(final, r1, v0),
            jnp.where(inner_final, r2, jnp.where(final, v0, v1)),
            jnp.where(final, v1, v2),
        )
        sums = []
        for tile in range(TRIPLE):
            total = across[tile] + (pltpu.roll(plus[tile], LANES - 1, 1) + pltpu.roll(minus[tile], 1, 1))
            if plane > 0:
                total = total + wide[c, spot[tile] - 1]
            elif ends is not None:
                total = total + ends[0, c, j * TRIPLE + tile]
            if plane < planes - 1:
                total = total + wide[c, spot[tile] + 1]
            elif ends is not None:
                total = total + ends[1, c, j * TRIPLE + tile]
            sums.append(total)
        return (v0, v1, v2), sums

    def step(j, unused):
        for plane in range(planes):
            (ur, nur), (ui, nui), (dr, ndr), (di, ndi) = (neighbours(c, plane, j) for c in range(4))
            for tile in range(TRIPLE):
                spot = j * stride + tile * planes + plane
                diag_up, bx, by, diag_down = (pot_ref[f, spot] for f in range(4))
                a, b, e, f = ur[tile], ui[tile], dr[tile], di[tile]
                flat[0, spot] = diag_up * a + bx * e + by * f - 0.5 * nur[tile]
                flat[1, spot] = diag_up * b + bx * f - by * e - 0.5 * nui[tile]
                flat[2, spot] = bx * a - by * b + diag_down * e - 0.5 * ndr[tile]
                flat[3, spot] = bx * b + by * a + diag_down * f - 0.5 * ndi[tile]
        return unused

    lax.fori_loop(0, steps, step, 0, unroll=UNROLL)


def store_rows(parts, i, out_ref):
    block = jnp.concatenate([part.astype(jnp.bfloat16) for part in parts], axis=1)
    values = product(spread_matrix(True), block).astype(jnp.bfloat16)
    for c in range(4):
        for s in range(SUB):
            out_ref[0, c, s, pl.ds(i * PACK, PACK), :] = values[s * PACK : (s + 1) * PACK, c * LANES : (c + 1) * LANES]


def apply_body(planes, x_ref, pot_ref, near_ref, far_ref, *refs):
    out_ref, token_ref, wide, turned, ends, flat = refs[-6:]
    near_slot = jnp.where(even_brick(), 1, 0)
    for c in range(4):
        ends[near_slot, c] = near_ref[0, c].astype(jnp.float32).reshape(ends.shape[2:])
        ends[1 - near_slot, c] = far_ref[0, c].astype(jnp.float32).reshape(ends.shape[2:])
    hamiltonian(planes, x_ref, pot_ref, ends, flat, wide, turned)
    for i in range(wide.shape[1] // PACK):
        store_rows([flat[c, pl.ds(i * PACK, PACK)].reshape(PACK * SUB, LANES) for c in range(4)], i, out_ref)


def ahead_body(planes, x_ref, pot_ref, *refs):
    flat_ref, token_ref, wide, turned = refs[-4:]
    hamiltonian(planes, x_ref, pot_ref, None, flat_ref.at[0], wide, turned)


def finish_body(planes, flat_ref, near_ref, far_ref, *refs):
    out_ref, token_ref = refs[-2:]
    even = even_brick()
    per = PACK // planes
    for i in range(flat_ref.shape[2] // PACK):
        outside = pl.ds(i * per * SUB, per * SUB)
        parts = []
        for c in range(4):
            near = near_ref[0, c, outside, :].astype(jnp.float32).reshape(per, SUB, LANES)
            far = far_ref[0, c, outside, :].astype(jnp.float32).reshape(per, SUB, LANES)
            below, above = jnp.where(even, far, near), jnp.where(even, near, far)
            pieces = []
            for q in range(PACK):
                piece = flat_ref[0, c, i * PACK + q]
                if q % planes == 0:
                    piece = piece - 0.5 * below[q // planes]
                if q % planes == planes - 1:
                    piece = piece - 0.5 * above[q // planes]
                pieces.append(piece)
            parts.append(jnp.concatenate(pieces, axis=0))
        store_rows(parts, i, out_ref)


def per_band(body, name, grid, inputs, in_specs, output, out_spec, carry, after, scratch, limit=VMEM_LIMIT):
    anywhere = pl.BlockSpec(memory_space=pl.ANY)
    carried = () if carry is None else (carry,)
    return pl.pallas_call(
        body,
        grid=grid,
        in_specs=in_specs + [anywhere] * (len(carried) + len(after)),
        out_specs=[out_spec, anywhere],
        out_shape=[
            jax.ShapeDtypeStruct(*output),
            jax.ShapeDtypeStruct((SUB, LANES), jnp.float32),
        ],
        input_output_aliases={len(inputs): 0} if carried else {},
        scratch_shapes=scratch,
        compiler_params=pltpu.CompilerParams(vmem_limit_bytes=limit),
        cost_estimate=SMALL,
        name=name,
    )(*inputs, *carried, *after)


def stencil_specs(rows, planes, start):
    segment = rows // SUB
    scratch = [
        pltpu.VMEM((4, segment, SUB, LANES), jnp.float32),
        pltpu.VMEM((4, segment + 2 * planes * TRIPLE, SUB, LANES), jnp.float32),
    ]
    in_specs = [
        pl.BlockSpec((1, 4, rows, LANES), lambda b: (start + b, 0, 0, 0)),
        pl.BlockSpec((4, segment, SUB, LANES), lambda b: (0, 0, 0, 0)),
    ]
    return in_specs, scratch


def apply_bands(x, potential, near, far, planes, start, carry, after):
    count, bands, rows = near.shape[0], x.shape[0], x.shape[2]
    segment, tiles = rows // SUB, rows // planes
    in_specs, scratch = stencil_specs(rows, planes, start)
    halo = pl.BlockSpec((1, 4, tiles, LANES), lambda b: (b, 0, 0, 0))
    scratch += [
        pltpu.VMEM((2, 4, tiles // SUB, SUB, LANES), jnp.float32),
        pltpu.VMEM((4, segment, SUB, LANES), jnp.float32),
    ]
    return per_band(
        functools.partial(apply_body, planes),
        "apply",
        (count,),
        (x, potential, near, far),
        in_specs + [halo, halo],
        ((bands, 4, SUB, segment, LANES), jnp.bfloat16),
        pl.BlockSpec((1, 4, SUB, segment, LANES), lambda b: (start + b, 0, 0, 0, 0)),
        carry,
        after,
        scratch,
    )


def ahead_of(x, potential, planes, start, count, after):
    segment = x.shape[2] // SUB
    in_specs, scratch = stencil_specs(x.shape[2], planes, start)
    return per_band(
        functools.partial(ahead_body, planes),
        "ahead",
        (count,),
        (x, potential),
        in_specs,
        ((count, 4, segment, SUB, LANES), jnp.float32),
        pl.BlockSpec((1, 4, segment, SUB, LANES), lambda b: (b, 0, 0, 0, 0)),
        None,
        after,
        scratch,
    )


def finish(flat, near, far, planes, start, skip, carry):
    count, segment = near.shape[0], flat.shape[2]
    part = segment // 3 if segment % (3 * PACK) == 0 else segment
    halo = pl.BlockSpec((1, 4, part // planes * SUB, LANES), lambda b, i: (b, 0, i, 0))
    return per_band(
        functools.partial(finish_body, planes),
        "finish",
        (count, segment // part),
        (flat, near, far),
        [pl.BlockSpec((1, 4, part, SUB, LANES), lambda b, i: (skip + b, 0, i, 0, 0)), halo, halo],
        (carry.shape, carry.dtype),
        pl.BlockSpec((1, 4, SUB, part, LANES), lambda b, i: (start + b, 0, 0, i, 0)),
        carry,
        (),
        [],
        VMEM_LIMIT - 3 * 1024 * 1024,
    )


def chunk_sizes(bands):
    quarter, small = bands // 4, bands // 8
    return [quarter, bands - 2 * quarter - small, quarter, small] if small else [bands]


def shards(spinors, kpt_mult, occupied, core_density, local_potential):
    bands, planes = spinors.shape[0], spinors.shape[2]
    total = bands * lax.axis_size("ka")
    size = lax.axis_size("brick")
    near_pairs = [(i, i ^ 1) for i in range(size) if i ^ 1 < size]
    far_pairs = [(i, j) for i in range(size) for j in [((i + 1) ^ 1) - 1] if 0 <= j < size]
    x = rows_view(spinors)
    core, local = rows_view(core_density), rows_view(local_potential)
    sizes = chunk_sizes(bands)
    starts = [sum(sizes[:k]) for k in range(len(sizes))]

    swap = lambda face: (lax.ppermute(face[0], "brick", near_pairs), lax.ppermute(face[1], "brick", far_pairs))
    faces = edges(x, planes, [(0, sizes[0])], (), VMEM_LIMIT)
    halos = [swap(faces[0])]
    density, others = front(x, kpt_mult, occupied, total, planes, sizes[1:], faces[0])
    faces += others
    halos += [swap(face) for face in faces[1:2]]
    density = group_sum(*density)
    gated = ()
    if len(sizes) > 2:
        gated = gate(*faces[2], halos[0] + (density[0],))
        halos.append(swap(gated))
    potential = potential_of(*density, core, local, gated)
    out, done = apply_bands(x, potential, *halos[0], planes, 0, None, ())
    if len(sizes) > 2:
        flat, done = ahead_of(x, potential, planes, starts[2], sizes[2] + sizes[3], (done,))
        halos.append(swap(gate(*faces[3], halos[1] + (done,))))
        out, done = apply_bands(x, potential, *halos[1], planes, starts[1], out, (done,))
        for k in (2, 3):
            out, done = finish(flat, *halos[k], planes, starts[k], starts[k] - starts[2], out)
    return planes_view(out.reshape(x.shape), planes)


def solution(mesh):
    placed = (P("ka", None, "brick", None), P("ka"), P("ka"), P("brick", None), P("brick", None))
    return jax.shard_map(
        shards, mesh=mesh, in_specs=placed, out_specs=P("ka", None, "brick", None), check_vma=False
    )
```

```python
import functools
import math

import jax
import jax.numpy as jnp
from jax import lax
from jax.experimental import pallas as pl
from jax.experimental.pallas import tpu as pltpu
from jax.sharding import PartitionSpec as P

NY = 192
LANES = 128
SUB = 8
TRIPLE = 3
HALF = 2 * NY - 2 * LANES - LANES // 2
PACK = 16
FLOOR_FRACTION = 0.05
VMEM_LIMIT = 63 * 1024 * 1024
UNROLL = 2
SMALL = pl.CostEstimate(flops=0, bytes_accessed=0, transcendentals=0)


def rows_view(x):
    lead, planes, cells = x.shape[:-2], x.shape[-2], x.shape[-1]
    tiles = cells // LANES
    n = len(lead)
    x = x.reshape(lead + (planes, tiles, LANES))
    x = x.transpose(tuple(range(n)) + (n + 1, n, n + 2))
    return x.reshape(lead + (tiles * planes, LANES))


def planes_view(x, planes):
    lead, rows = x.shape[:-2], x.shape[-2]
    tiles = rows // planes
    n = len(lead)
    x = x.reshape(lead + (tiles, planes, LANES))
    x = x.transpose(tuple(range(n)) + (n + 1, n, n + 2))
    return x.reshape(lead + (planes, tiles * LANES))


def even_brick():
    return lax.axis_index("brick") % 2 == 0


def spread_matrix(back):
    size = SUB * PACK
    row = lax.broadcasted_iota(jnp.int32, (size, size), 0)
    column = lax.broadcasted_iota(jnp.int32, (size, size), 1)
    if back:
        row, column = column, row
    return (column == (row % SUB) * PACK + row // SUB).astype(jnp.bfloat16)


def gathered(read, segment, i):
    return jnp.concatenate(
        [read(pl.ds(s * segment + i * PACK, PACK)) for s in range(SUB)], axis=0
    )


def product(matrix, values):
    return jnp.dot(matrix, values, preferred_element_type=jnp.float32)


def face_matrix(planes):
    out = PACK // planes * SUB
    row = lax.broadcasted_iota(jnp.int32, (2 * out, SUB * PACK), 0)
    column = lax.broadcasted_iota(jnp.int32, (2 * out, SUB * PACK), 1)
    upper = (row < out) == even_brick()
    inner = row % out
    wanted = (inner % SUB) * PACK + (inner // SUB) * planes + jnp.where(upper, planes - 1, 0)
    return (column == wanted).astype(jnp.bfloat16), out


def edges_body(planes, chunks, x_ref, *refs):
    faces, held, sems = refs[-2 - 2 * len(chunks) : -2], refs[-2], refs[-1]
    first = chunks[0][0]
    bands = [(start - first + b, k, b) for k, (start, count) in enumerate(chunks) for b in range(count)]
    rows = held.shape[2]
    segment = rows // SUB
    copies = [pltpu.make_async_copy(x_ref.at[first + i], held.at[i], sems.at[i]) for i, _, _ in bands]
    for copy in copies:
        copy.start()
    select, out = face_matrix(planes)
    for i, k, b in bands:
        copies[i].wait()
        near_ref, far_ref = faces[2 * k], faces[2 * k + 1]
        for part in range(segment // PACK):
            block = jnp.concatenate(
                [gathered(lambda at: held[i, c, at, :], segment, part) for c in range(4)], axis=1
            )
            picked = product(select, block).astype(jnp.bfloat16)
            at = pl.ds(part * out, out)
            for c in range(4):
                lanes = slice(c * LANES, (c + 1) * LANES)
                near_ref[b, c, at, :] = picked[:out, lanes]
                far_ref[b, c, at, :] = picked[out:, lanes]


def edges(x, planes, chunks, after, limit):
    rows = x.shape[2]
    total = sum(count for _, count in chunks)
    shapes = [
        jax.ShapeDtypeStruct((count, 4, rows // planes, LANES), jnp.bfloat16) for _, count in chunks for _ in range(2)
    ]
    faces = pl.pallas_call(
        functools.partial(edges_body, planes, chunks),
        in_specs=[pl.BlockSpec(memory_space=pltpu.HBM)] + [pl.BlockSpec(memory_space=pl.ANY)] * len(after),
        out_shape=shapes,
        scratch_shapes=[pltpu.VMEM((total, 4, rows, LANES), jnp.bfloat16), pltpu.SemaphoreType.DMA((total,))],
        compiler_params=pltpu.CompilerParams(vmem_limit_bytes=limit),
        cost_estimate=SMALL,
        name="edges",
    )(x, *after)
    return [tuple(faces[2 * k : 2 * k + 2]) for k in range(len(chunks))]


def gate(near, far, after):
    anywhere = pl.BlockSpec(memory_space=pl.ANY)
    return pl.pallas_call(
        lambda *refs: None,
        in_specs=[anywhere] * (2 + len(after)),
        out_specs=[anywhere, anywhere],
        out_shape=[jax.ShapeDtypeStruct(a.shape, a.dtype) for a in (near, far)],
        input_output_aliases={0: 0, 1: 1},
        compiler_params=pltpu.CompilerParams(vmem_limit_bytes=VMEM_LIMIT),
        name="gate",
    )(near, far, *after)


def front_body(planes, scale, counts, mult_ref, occ_ref, x_ref, *refs):
    bands = x_ref.shape[0]
    first = len(refs) - 2 * len(counts)
    mine_ref, other_ref, faces = refs[first - 2], refs[first - 1], refs[first:]
    lower_half = holds_lower_half()
    weights = [(mult_ref[b] * occ_ref[b]).astype(jnp.float32) * scale for b in range(bands)]
    for s in range(SUB):
        up = down = real = imag = None
        for b in range(bands):
            ur, ui, dr, di = (x_ref[b, c, s].astype(jnp.float32) for c in range(4))
            wur, wui = weights[b] * ur, weights[b] * ui
            wdr, wdi = weights[b] * dr, weights[b] * di
            terms = (
                wur * ur + wui * ui,
                wdr * dr + wdi * di,
                wur * dr + wui * di,
                wur * di - wui * dr,
            )
            if b == 0:
                up, down, real, imag = terms
            else:
                up, down, real, imag = up + terms[0], down + terms[1], real + terms[2], imag + terms[3]
        fields = (up + down, 2.0 * real, 2.0 * imag, up - down)
        for f in range(2):
            mine_ref[f, s] = jnp.where(lower_half, fields[f], fields[f + 2]).astype(jnp.bfloat16)
            other_ref[f, s] = jnp.where(lower_half, fields[f + 2], fields[f]).astype(jnp.bfloat16)
    if counts:
        select, out = face_matrix(planes)
    band = bands - sum(counts)
    for k, count in enumerate(counts):
        for b in range(count):
            block = jnp.concatenate(
                [x_ref[band, c].reshape(SUB * PACK, LANES) for c in range(4)], axis=1
            )
            picked = product(select, block).astype(jnp.bfloat16)
            for c in range(4):
                lanes = slice(c * LANES, (c + 1) * LANES)
                faces[2 * k][b, c] = picked[:out, lanes]
                faces[2 * k + 1][b, c] = picked[out:, lanes]
            band += 1


def front(x, mult, occ, total, planes, counts, after):
    bands, rows = x.shape[0], x.shape[2]
    segment = rows // SUB
    out = PACK // planes * SUB
    anywhere = pl.BlockSpec(memory_space=pl.ANY)
    results = pl.pallas_call(
        functools.partial(front_body, planes, 1.0 / (2.0 * total), counts),
        grid=(segment // PACK,),
        in_specs=[
            pl.BlockSpec(memory_space=pltpu.SMEM),
            pl.BlockSpec(memory_space=pltpu.SMEM),
            pl.BlockSpec((bands, 4, SUB, PACK, LANES), lambda i: (0, 0, 0, i, 0)),
        ]
        + [anywhere] * len(after),
        out_specs=[pl.BlockSpec((2, SUB, PACK, LANES), lambda i: (0, 0, i, 0))] * 2
        + [pl.BlockSpec((count, 4, out, LANES), lambda i: (0, 0, i, 0)) for count in counts for _ in range(2)],
        out_shape=[jax.ShapeDtypeStruct((2, SUB, segment, LANES), jnp.bfloat16)] * 2
        + [
            jax.ShapeDtypeStruct((count, 4, rows // planes, LANES), jnp.bfloat16)
            for count in counts
            for _ in range(2)
        ],
        compiler_params=pltpu.CompilerParams(vmem_limit_bytes=VMEM_LIMIT),
        cost_estimate=SMALL,
        name="front",
    )(mult, occ, x.reshape(bands, 4, SUB, segment, LANES), *after)
    halves = [half.reshape(2, rows, LANES) for half in results[:2]]
    return halves, [tuple(results[2 + 2 * k : 4 + 2 * k]) for k in range(len(counts))]


def add_body(a_ref, b_ref, out_ref):
    out_ref[...] = (a_ref[...].astype(jnp.float32) + b_ref[...].astype(jnp.float32)).astype(jnp.bfloat16)


def add(a, b):
    whole = pl.BlockSpec(memory_space=pltpu.VMEM)
    return pl.pallas_call(
        add_body,
        in_specs=[whole, whole],
        out_specs=whole,
        out_shape=jax.ShapeDtypeStruct(a.shape, a.dtype),
        compiler_params=pltpu.CompilerParams(vmem_limit_bytes=VMEM_LIMIT),
        cost_estimate=SMALL,
        name="add",
    )(a, b)


def holds_lower_half():
    return lax.axis_index("ka") % 2 == 0


def group_sum(mine, other):
    size = lax.axis_size("ka")
    assert size % 2 == 0
    partner = [(i, i ^ 1) for i in range(size)]

    def swaps(_, fields):
        total, given = fields
        total = add(total, lax.ppermute(given, "ka", partner))
        turning = total
        for _ in range(size // 2 - 1):
            turning = lax.ppermute(turning, "ka", [(i, (i + 2) % size) for i in range(size)])
            total = add(total, turning)
        return total, lax.ppermute(total, "ka", partner)

    trips = 1 + lax.div(lax.axis_index("ka"), size)
    return lax.fori_loop(0, trips, swaps, (mine, other))


def cube_root(x):
    root = jnp.exp(jnp.log(jnp.abs(x)) * (1.0 / 3.0))
    return jnp.where(x < 0.0, -root, root)


def potential_body(rows, mine_ref, other_ref, core_ref, local_ref, *refs):
    out_ref = refs[-1]
    segment = rows // SUB
    spread = spread_matrix(False)

    lower_half = holds_lower_half()

    def step(i, unused):
        block = jnp.concatenate(
            [gathered(lambda at: ref[f, at, :], segment, i) for ref in (mine_ref, other_ref) for f in range(2)], axis=1
        )
        fields = product(spread, block)
        m0, m1, o0, o1 = (fields[:, f * LANES : (f + 1) * LANES] for f in range(4))
        d0, d1 = jnp.where(lower_half, m0, o0), jnp.where(lower_half, m1, o1)
        d2, d3 = jnp.where(lower_half, o0, m0), jnp.where(lower_half, o1, m1)
        here = [pl.ds(i * PACK + r, SUB, stride=segment) for r in range(PACK)]
        core = jnp.concatenate([core_ref[at, :] for at in here], axis=0)
        local = jnp.concatenate([local_ref[at, :] for at in here], axis=0)
        electrons = d0 + core
        magnitude = jnp.sqrt(d1 * d1 + d2 * d2 + d3 * d3)
        upper = -cube_root((3.0 / math.pi) * (electrons + magnitude))
        lower = -cube_root((3.0 / math.pi) * (electrons - magnitude))
        factor = 0.5 * (upper - lower) / jnp.maximum(magnitude, FLOOR_FRACTION * electrons)
        v = 0.5 * (upper + lower) + local
        bz = factor * d3
        at = pl.ds(i * PACK, PACK)
        shape = (PACK, SUB, LANES)
        out_ref[0, at] = (v + bz + 3.0).reshape(shape)
        out_ref[1, at] = (factor * d1).reshape(shape)
        out_ref[2, at] = (factor * d2).reshape(shape)
        out_ref[3, at] = (v - bz + 3.0).reshape(shape)
        return unused

    lax.fori_loop(0, segment // PACK, step, 0, unroll=True)


def potential_of(mine, other, core, local, after):
    rows = mine.shape[1]
    whole = pl.BlockSpec(memory_space=pltpu.VMEM)
    return pl.pallas_call(
        functools.partial(potential_body, rows),
        in_specs=[whole] * 4 + [pl.BlockSpec(memory_space=pl.ANY)] * len(after),
        out_specs=whole,
        out_shape=jax.ShapeDtypeStruct((4, rows // SUB, SUB, LANES), jnp.float32),
        compiler_params=pltpu.CompilerParams(vmem_limit_bytes=VMEM_LIMIT),
        cost_estimate=SMALL,
        name="potential",
    )(mine, other, core, local, *after)


def hamiltonian(planes, x_ref, pot_ref, ends, flat, wide, turned):
    segment = wide.shape[1]
    stride = planes * TRIPLE
    steps = segment // stride
    spread = spread_matrix(False)

    def load(i, unused):
        block = jnp.concatenate([gathered(lambda at: x_ref[0, c, at, :], segment, i) for c in range(4)], axis=1)
        values = product(spread, block)
        for c in range(4):
            part = values[:, c * LANES : (c + 1) * LANES]
            wide[c, pl.ds(i * PACK, PACK)] = part.reshape(PACK, SUB, LANES)
            turned[c, pl.ds(stride + i * PACK, PACK)] = pltpu.roll(part, HALF, 1).reshape(PACK, SUB, LANES)
        return unused

    lax.fori_loop(0, segment // PACK, load, 0, unroll=True)
    for c in range(4):
        for q in range(stride):
            turned[c, q] = pltpu.roll(turned[c, segment + q], 1, 0)
            turned[c, segment + stride + q] = pltpu.roll(turned[c, stride + q], SUB - 1, 0)

    lane = lax.broadcasted_iota(jnp.int32, (SUB, LANES), 1)
    low = lane < HALF
    initial, final = lane == 0, lane == LANES - 1
    inner_initial, inner_final = lane == HALF, lane == HALF - 1

    def neighbours(c, plane, j):
        spot = [j * stride + tile * planes + plane for tile in range(TRIPLE)]
        v0, v1, v2 = (wide[c, at] for at in spot)
        r0, r1, r2 = (turned[c, at + stride] for at in spot)
        after0 = r0 + turned[c, spot[0] + 2 * stride]
        after1 = r1 + turned[c, spot[1] + 2 * stride]
        before1 = r1 + turned[c, spot[1]]
        before2 = r2 + turned[c, spot[2]]
        across = (
            jnp.where(low, before1, before2),
            jnp.where(low, before2, after0),
            jnp.where(low, after0, after1),
        )
        plus = (
            jnp.where(initial, v1, v0),
            jnp.where(inner_initial, r0, jnp.where(initial, v2, v1)),
            jnp.where(initial, r1, v2),
        )
        minus = (
            jnp.where(final, r1, v0),
            jnp.where(inner_final, r2, jnp.where(final, v0, v1)),
            jnp.where(final, v1, v2),
        )
        sums = []
        for tile in range(TRIPLE):
            total = across[tile] + (pltpu.roll(plus[tile], LANES - 1, 1) + pltpu.roll(minus[tile], 1, 1))
            if plane > 0:
                total = total + wide[c, spot[tile] - 1]
            elif ends is not None:
                total = total + ends[0, c, j * TRIPLE + tile]
            if plane < planes - 1:
                total = total + wide[c, spot[tile] + 1]
            elif ends is not None:
                total = total + ends[1, c, j * TRIPLE + tile]
            sums.append(total)
        return (v0, v1, v2), sums

    def step(j, unused):
        for plane in range(planes):
            (ur, nur), (ui, nui), (dr, ndr), (di, ndi) = (neighbours(c, plane, j) for c in range(4))
            for tile in range(TRIPLE):
                spot = j * stride + tile * planes + plane
                diag_up, bx, by, diag_down = (pot_ref[f, spot] for f in range(4))
                a, b, e, f = ur[tile], ui[tile], dr[tile], di[tile]
                flat[0, spot] = diag_up * a + bx * e + by * f - 0.5 * nur[tile]
                flat[1, spot] = diag_up * b + bx * f - by * e - 0.5 * nui[tile]
                flat[2, spot] = bx * a - by * b + diag_down * e - 0.5 * ndr[tile]
                flat[3, spot] = bx * b + by * a + diag_down * f - 0.5 * ndi[tile]
        return unused

    lax.fori_loop(0, steps, step, 0, unroll=UNROLL)


def store_rows(parts, i, out_ref):
    block = jnp.concatenate([part.astype(jnp.bfloat16) for part in parts], axis=1)
    values = product(spread_matrix(True), block).astype(jnp.bfloat16)
    for c in range(4):
        for s in range(SUB):
            out_ref[0, c, s, pl.ds(i * PACK, PACK), :] = values[s * PACK : (s + 1) * PACK, c * LANES : (c + 1) * LANES]


def apply_body(planes, x_ref, pot_ref, near_ref, far_ref, *refs):
    out_ref, token_ref, wide, turned, ends, flat = refs[-6:]
    near_slot = jnp.where(even_brick(), 1, 0)
    for c in range(4):
        ends[near_slot, c] = near_ref[0, c].astype(jnp.float32).reshape(ends.shape[2:])
        ends[1 - near_slot, c] = far_ref[0, c].astype(jnp.float32).reshape(ends.shape[2:])
    hamiltonian(planes, x_ref, pot_ref, ends, flat, wide, turned)
    for i in range(wide.shape[1] // PACK):
        store_rows([flat[c, pl.ds(i * PACK, PACK)].reshape(PACK * SUB, LANES) for c in range(4)], i, out_ref)


def ahead_body(planes, x_ref, pot_ref, *refs):
    flat_ref, token_ref, wide, turned = refs[-4:]
    hamiltonian(planes, x_ref, pot_ref, None, flat_ref.at[0], wide, turned)


def finish_body(planes, flat_ref, near_ref, far_ref, *refs):
    out_ref, token_ref = refs[-2:]
    even = even_brick()
    per = PACK // planes
    for i in range(flat_ref.shape[2] // PACK):
        outside = pl.ds(i * per * SUB, per * SUB)
        parts = []
        for c in range(4):
            near = near_ref[0, c, outside, :].astype(jnp.float32).reshape(per, SUB, LANES)
            far = far_ref[0, c, outside, :].astype(jnp.float32).reshape(per, SUB, LANES)
            below, above = jnp.where(even, far, near), jnp.where(even, near, far)
            pieces = []
            for q in range(PACK):
                piece = flat_ref[0, c, i * PACK + q]
                if q % planes == 0:
                    piece = piece - 0.5 * below[q // planes]
                if q % planes == planes - 1:
                    piece = piece - 0.5 * above[q // planes]
                pieces.append(piece)
            parts.append(jnp.concatenate(pieces, axis=0))
        store_rows(parts, i, out_ref)


def per_band(body, name, grid, inputs, in_specs, output, out_spec, carry, after, scratch, limit=VMEM_LIMIT):
    anywhere = pl.BlockSpec(memory_space=pl.ANY)
    carried = () if carry is None else (carry,)
    return pl.pallas_call(
        body,
        grid=grid,
        in_specs=in_specs + [anywhere] * (len(carried) + len(after)),
        out_specs=[out_spec, anywhere],
        out_shape=[
            jax.ShapeDtypeStruct(*output),
            jax.ShapeDtypeStruct((SUB, LANES), jnp.float32),
        ],
        input_output_aliases={len(inputs): 0} if carried else {},
        scratch_shapes=scratch,
        compiler_params=pltpu.CompilerParams(vmem_limit_bytes=limit),
        cost_estimate=SMALL,
        name=name,
    )(*inputs, *carried, *after)


def stencil_specs(rows, planes, start):
    segment = rows // SUB
    scratch = [
        pltpu.VMEM((4, segment, SUB, LANES), jnp.float32),
        pltpu.VMEM((4, segment + 2 * planes * TRIPLE, SUB, LANES), jnp.float32),
    ]
    in_specs = [
        pl.BlockSpec((1, 4, rows, LANES), lambda b: (start + b, 0, 0, 0)),
        pl.BlockSpec((4, segment, SUB, LANES), lambda b: (0, 0, 0, 0)),
    ]
    return in_specs, scratch


def apply_bands(x, potential, near, far, planes, start, carry, after):
    count, bands, rows = near.shape[0], x.shape[0], x.shape[2]
    segment, tiles = rows // SUB, rows // planes
    in_specs, scratch = stencil_specs(rows, planes, start)
    halo = pl.BlockSpec((1, 4, tiles, LANES), lambda b: (b, 0, 0, 0))
    scratch += [
        pltpu.VMEM((2, 4, tiles // SUB, SUB, LANES), jnp.float32),
        pltpu.VMEM((4, segment, SUB, LANES), jnp.float32),
    ]
    return per_band(
        functools.partial(apply_body, planes),
        "apply",
        (count,),
        (x, potential, near, far),
        in_specs + [halo, halo],
        ((bands, 4, SUB, segment, LANES), jnp.bfloat16),
        pl.BlockSpec((1, 4, SUB, segment, LANES), lambda b: (start + b, 0, 0, 0, 0)),
        carry,
        after,
        scratch,
    )


def ahead_of(x, potential, planes, start, count, after):
    segment = x.shape[2] // SUB
    in_specs, scratch = stencil_specs(x.shape[2], planes, start)
    return per_band(
        functools.partial(ahead_body, planes),
        "ahead",
        (count,),
        (x, potential),
        in_specs,
        ((count, 4, segment, SUB, LANES), jnp.float32),
        pl.BlockSpec((1, 4, segment, SUB, LANES), lambda b: (b, 0, 0, 0, 0)),
        None,
        after,
        scratch,
    )


def finish(flat, near, far, planes, start, skip, carry):
    count, segment = near.shape[0], flat.shape[2]
    halo = pl.BlockSpec((1, 4, segment // planes * SUB, LANES), lambda b: (b, 0, 0, 0))
    return per_band(
        functools.partial(finish_body, planes),
        "finish",
        (count,),
        (flat, near, far),
        [pl.BlockSpec((1, 4, segment, SUB, LANES), lambda b: (skip + b, 0, 0, 0, 0)), halo, halo],
        (carry.shape, carry.dtype),
        pl.BlockSpec((1, 4, SUB, segment, LANES), lambda b: (start + b, 0, 0, 0, 0)),
        carry,
        (),
        [],
        VMEM_LIMIT - 16 * 1024 * 1024,
    )


def chunk_sizes(bands):
    quarter, small = bands // 4, bands // 8
    return [quarter, bands - 2 * quarter - small, quarter, small] if small else [bands]


def shards(spinors, kpt_mult, occupied, core_density, local_potential):
    bands, planes = spinors.shape[0], spinors.shape[2]
    total = bands * lax.axis_size("ka")
    size = lax.axis_size("brick")
    near_pairs = [(i, i ^ 1) for i in range(size) if i ^ 1 < size]
    far_pairs = [(i, j) for i in range(size) for j in [((i + 1) ^ 1) - 1] if 0 <= j < size]
    x = rows_view(spinors)
    core, local = rows_view(core_density), rows_view(local_potential)
    sizes = chunk_sizes(bands)
    starts = [sum(sizes[:k]) for k in range(len(sizes))]

    swap = lambda face: (lax.ppermute(face[0], "brick", near_pairs), lax.ppermute(face[1], "brick", far_pairs))
    faces = edges(x, planes, [(0, sizes[0])], (), VMEM_LIMIT)
    halos = [swap(faces[0])]
    density, others = front(x, kpt_mult, occupied, total, planes, sizes[1:], faces[0])
    faces += others
    halos += [swap(face) for face in faces[1:2]]
    density = group_sum(*density)
    gated = ()
    if len(sizes) > 2:
        gated = gate(*faces[2], halos[0] + (density[0],))
        halos.append(swap(gated))
    potential = potential_of(*density, core, local, gated)
    out, done = apply_bands(x, potential, *halos[0], planes, 0, None, ())
    if len(sizes) > 2:
        flat, done = ahead_of(x, potential, planes, starts[2], sizes[2] + sizes[3], (done,))
        halos.append(swap(gate(*faces[3], halos[1] + (done,))))
        out, done = apply_bands(x, potential, *halos[1], planes, starts[1], out, (done,))
        for k in (2, 3):
            out, done = finish(flat, *halos[k], planes, starts[k], starts[k] - starts[2], out)
    return planes_view(out.reshape(x.shape), planes)


def solution(mesh):
    placed = (P("ka", None, "brick", None), P("ka"), P("ka"), P("brick", None), P("brick", None))
    return jax.shard_map(
        shards, mesh=mesh, in_specs=placed, out_specs=P("ka", None, "brick", None), check_vma=False
    )
```

```python
import functools
import math

import jax
import jax.numpy as jnp
from jax import lax
from jax.experimental import pallas as pl
from jax.experimental.pallas import tpu as pltpu
from jax.sharding import PartitionSpec as P

NY = 192
LANES = 128
SUB = 8
TRIPLE = 3
HALF = 2 * NY - 2 * LANES - LANES // 2
PACK = 16
FLOOR_FRACTION = 0.05
VMEM_LIMIT = 63 * 1024 * 1024
UNROLL = 4
SMALL = pl.CostEstimate(flops=0, bytes_accessed=0, transcendentals=0)


def rows_view(x):
    lead, planes, cells = x.shape[:-2], x.shape[-2], x.shape[-1]
    tiles = cells // LANES
    n = len(lead)
    x = x.reshape(lead + (planes, tiles, LANES))
    x = x.transpose(tuple(range(n)) + (n + 1, n, n + 2))
    return x.reshape(lead + (tiles * planes, LANES))


def planes_view(x, planes):
    lead, rows = x.shape[:-2], x.shape[-2]
    tiles = rows // planes
    n = len(lead)
    x = x.reshape(lead + (tiles, planes, LANES))
    x = x.transpose(tuple(range(n)) + (n + 1, n, n + 2))
    return x.reshape(lead + (planes, tiles * LANES))


def even_brick():
    return lax.axis_index("brick") % 2 == 0


def spread_matrix(back):
    size = SUB * PACK
    row = lax.broadcasted_iota(jnp.int32, (size, size), 0)
    column = lax.broadcasted_iota(jnp.int32, (size, size), 1)
    if back:
        row, column = column, row
    return (column == (row % SUB) * PACK + row // SUB).astype(jnp.bfloat16)


def gathered(read, segment, i):
    return jnp.concatenate(
        [read(pl.ds(s * segment + i * PACK, PACK)) for s in range(SUB)], axis=0
    )


def product(matrix, values):
    return jnp.dot(matrix, values, preferred_element_type=jnp.float32)


def face_matrix(planes):
    out = PACK // planes * SUB
    row = lax.broadcasted_iota(jnp.int32, (2 * out, SUB * PACK), 0)
    column = lax.broadcasted_iota(jnp.int32, (2 * out, SUB * PACK), 1)
    upper = (row < out) == even_brick()
    inner = row % out
    wanted = (inner % SUB) * PACK + (inner // SUB) * planes + jnp.where(upper, planes - 1, 0)
    return (column == wanted).astype(jnp.bfloat16), out


def edges_body(planes, chunks, x_ref, *refs):
    faces, held, sems = refs[-2 - 2 * len(chunks) : -2], refs[-2], refs[-1]
    first = chunks[0][0]
    bands = [(start - first + b, k, b) for k, (start, count) in enumerate(chunks) for b in range(count)]
    rows = held.shape[2]
    segment = rows // SUB
    copies = [pltpu.make_async_copy(x_ref.at[first + i], held.at[i], sems.at[i]) for i, _, _ in bands]
    for copy in copies:
        copy.start()
    select, out = face_matrix(planes)
    for i, k, b in bands:
        copies[i].wait()
        near_ref, far_ref = faces[2 * k], faces[2 * k + 1]
        for part in range(segment // PACK):
            block = jnp.concatenate(
                [gathered(lambda at: held[i, c, at, :], segment, part) for c in range(4)], axis=1
            )
            picked = product(select, block).astype(jnp.bfloat16)
            at = pl.ds(part * out, out)
            for c in range(4):
                lanes = slice(c * LANES, (c + 1) * LANES)
                near_ref[b, c, at, :] = picked[:out, lanes]
                far_ref[b, c, at, :] = picked[out:, lanes]


def edges(x, planes, chunks, after, limit):
    rows = x.shape[2]
    total = sum(count for _, count in chunks)
    shapes = [
        jax.ShapeDtypeStruct((count, 4, rows // planes, LANES), jnp.bfloat16) for _, count in chunks for _ in range(2)
    ]
    faces = pl.pallas_call(
        functools.partial(edges_body, planes, chunks),
        in_specs=[pl.BlockSpec(memory_space=pltpu.HBM)] + [pl.BlockSpec(memory_space=pl.ANY)] * len(after),
        out_shape=shapes,
        scratch_shapes=[pltpu.VMEM((total, 4, rows, LANES), jnp.bfloat16), pltpu.SemaphoreType.DMA((total,))],
        compiler_params=pltpu.CompilerParams(vmem_limit_bytes=limit),
        cost_estimate=SMALL,
        name="edges",
    )(x, *after)
    return [tuple(faces[2 * k : 2 * k + 2]) for k in range(len(chunks))]


def gate(near, far, after):
    anywhere = pl.BlockSpec(memory_space=pl.ANY)
    return pl.pallas_call(
        lambda *refs: None,
        in_specs=[anywhere] * (2 + len(after)),
        out_specs=[anywhere, anywhere],
        out_shape=[jax.ShapeDtypeStruct(a.shape, a.dtype) for a in (near, far)],
        input_output_aliases={0: 0, 1: 1},
        compiler_params=pltpu.CompilerParams(vmem_limit_bytes=VMEM_LIMIT),
        name="gate",
    )(near, far, *after)


def front_body(planes, scale, counts, mult_ref, occ_ref, x_ref, *refs):
    bands = x_ref.shape[0]
    first = len(refs) - 2 * len(counts)
    mine_ref, other_ref, faces = refs[first - 2], refs[first - 1], refs[first:]
    lower_half = holds_lower_half()
    weights = [(mult_ref[b] * occ_ref[b]).astype(jnp.float32) * scale for b in range(bands)]
    for s in range(SUB):
        up = down = real = imag = None
        for b in range(bands):
            ur, ui, dr, di = (x_ref[b, c, s].astype(jnp.float32) for c in range(4))
            wur, wui = weights[b] * ur, weights[b] * ui
            wdr, wdi = weights[b] * dr, weights[b] * di
            terms = (
                wur * ur + wui * ui,
                wdr * dr + wdi * di,
                wur * dr + wui * di,
                wur * di - wui * dr,
            )
            if b == 0:
                up, down, real, imag = terms
            else:
                up, down, real, imag = up + terms[0], down + terms[1], real + terms[2], imag + terms[3]
        fields = (up + down, 2.0 * real, 2.0 * imag, up - down)
        for f in range(2):
            mine_ref[f, s] = jnp.where(lower_half, fields[f], fields[f + 2]).astype(jnp.bfloat16)
            other_ref[f, s] = jnp.where(lower_half, fields[f + 2], fields[f]).astype(jnp.bfloat16)
    if counts:
        select, out = face_matrix(planes)
    band = bands - sum(counts)
    for k, count in enumerate(counts):
        for b in range(count):
            block = jnp.concatenate(
                [x_ref[band, c].reshape(SUB * PACK, LANES) for c in range(4)], axis=1
            )
            picked = product(select, block).astype(jnp.bfloat16)
            for c in range(4):
                lanes = slice(c * LANES, (c + 1) * LANES)
                faces[2 * k][b, c] = picked[:out, lanes]
                faces[2 * k + 1][b, c] = picked[out:, lanes]
            band += 1


def front(x, mult, occ, total, planes, counts, after):
    bands, rows = x.shape[0], x.shape[2]
    segment = rows // SUB
    out = PACK // planes * SUB
    anywhere = pl.BlockSpec(memory_space=pl.ANY)
    results = pl.pallas_call(
        functools.partial(front_body, planes, 1.0 / (2.0 * total), counts),
        grid=(segment // PACK,),
        in_specs=[
            pl.BlockSpec(memory_space=pltpu.SMEM),
            pl.BlockSpec(memory_space=pltpu.SMEM),
            pl.BlockSpec((bands, 4, SUB, PACK, LANES), lambda i: (0, 0, 0, i, 0)),
        ]
        + [anywhere] * len(after),
        out_specs=[pl.BlockSpec((2, SUB, PACK, LANES), lambda i: (0, 0, i, 0))] * 2
        + [pl.BlockSpec((count, 4, out, LANES), lambda i: (0, 0, i, 0)) for count in counts for _ in range(2)],
        out_shape=[jax.ShapeDtypeStruct((2, SUB, segment, LANES), jnp.bfloat16)] * 2
        + [
            jax.ShapeDtypeStruct((count, 4, rows // planes, LANES), jnp.bfloat16)
            for count in counts
            for _ in range(2)
        ],
        compiler_params=pltpu.CompilerParams(vmem_limit_bytes=VMEM_LIMIT),
        cost_estimate=SMALL,
        name="front",
    )(mult, occ, x.reshape(bands, 4, SUB, segment, LANES), *after)
    halves = [half.reshape(2, rows, LANES) for half in results[:2]]
    return halves, [tuple(results[2 + 2 * k : 4 + 2 * k]) for k in range(len(counts))]


def add_body(a_ref, b_ref, out_ref):
    out_ref[...] = (a_ref[...].astype(jnp.float32) + b_ref[...].astype(jnp.float32)).astype(jnp.bfloat16)


def add(a, b):
    whole = pl.BlockSpec(memory_space=pltpu.VMEM)
    return pl.pallas_call(
        add_body,
        in_specs=[whole, whole],
        out_specs=whole,
        out_shape=jax.ShapeDtypeStruct(a.shape, a.dtype),
        compiler_params=pltpu.CompilerParams(vmem_limit_bytes=VMEM_LIMIT),
        cost_estimate=SMALL,
        name="add",
    )(a, b)


def holds_lower_half():
    return lax.axis_index("ka") % 2 == 0


def group_sum(mine, other):
    size = lax.axis_size("ka")
    assert size % 2 == 0
    partner = [(i, i ^ 1) for i in range(size)]

    def swaps(_, fields):
        total, given = fields
        total = add(total, lax.ppermute(given, "ka", partner))
        turning = total
        for _ in range(size // 2 - 1):
            turning = lax.ppermute(turning, "ka", [(i, (i + 2) % size) for i in range(size)])
            total = add(total, turning)
        return total, lax.ppermute(total, "ka", partner)

    trips = 1 + lax.div(lax.axis_index("ka"), size)
    return lax.fori_loop(0, trips, swaps, (mine, other))


def cube_root(x):
    root = jnp.exp(jnp.log(jnp.abs(x)) * (1.0 / 3.0))
    return jnp.where(x < 0.0, -root, root)


def potential_body(rows, mine_ref, other_ref, core_ref, local_ref, *refs):
    out_ref = refs[-1]
    segment = rows // SUB
    spread = spread_matrix(False)

    lower_half = holds_lower_half()

    def step(i, unused):
        block = jnp.concatenate(
            [gathered(lambda at: ref[f, at, :], segment, i) for ref in (mine_ref, other_ref) for f in range(2)], axis=1
        )
        fields = product(spread, block)
        m0, m1, o0, o1 = (fields[:, f * LANES : (f + 1) * LANES] for f in range(4))
        d0, d1 = jnp.where(lower_half, m0, o0), jnp.where(lower_half, m1, o1)
        d2, d3 = jnp.where(lower_half, o0, m0), jnp.where(lower_half, o1, m1)
        here = [pl.ds(i * PACK + r, SUB, stride=segment) for r in range(PACK)]
        core = jnp.concatenate([core_ref[at, :] for at in here], axis=0)
        local = jnp.concatenate([local_ref[at, :] for at in here], axis=0)
        electrons = d0 + core
        magnitude = jnp.sqrt(d1 * d1 + d2 * d2 + d3 * d3)
        upper = -cube_root((3.0 / math.pi) * (electrons + magnitude))
        lower = -cube_root((3.0 / math.pi) * (electrons - magnitude))
        factor = 0.5 * (upper - lower) / jnp.maximum(magnitude, FLOOR_FRACTION * electrons)
        v = 0.5 * (upper + lower) + local
        bz = factor * d3
        at = pl.ds(i * PACK, PACK)
        shape = (PACK, SUB, LANES)
        out_ref[0, at] = (v + bz + 3.0).reshape(shape)
        out_ref[1, at] = (factor * d1).reshape(shape)
        out_ref[2, at] = (factor * d2).reshape(shape)
        out_ref[3, at] = (v - bz + 3.0).reshape(shape)
        return unused

    lax.fori_loop(0, segment // PACK, step, 0, unroll=True)


def potential_of(mine, other, core, local, after):
    rows = mine.shape[1]
    whole = pl.BlockSpec(memory_space=pltpu.VMEM)
    return pl.pallas_call(
        functools.partial(potential_body, rows),
        in_specs=[whole] * 4 + [pl.BlockSpec(memory_space=pl.ANY)] * len(after),
        out_specs=whole,
        out_shape=jax.ShapeDtypeStruct((4, rows // SUB, SUB, LANES), jnp.float32),
        compiler_params=pltpu.CompilerParams(vmem_limit_bytes=VMEM_LIMIT),
        cost_estimate=SMALL,
        name="potential",
    )(mine, other, core, local, *after)


def hamiltonian(planes, x_ref, pot_ref, ends, flat, wide, turned):
    segment = wide.shape[1]
    stride = planes * TRIPLE
    steps = segment // stride
    spread = spread_matrix(False)

    def load(i, unused):
        block = jnp.concatenate([gathered(lambda at: x_ref[0, c, at, :], segment, i) for c in range(4)], axis=1)
        values = product(spread, block)
        for c in range(4):
            part = values[:, c * LANES : (c + 1) * LANES]
            wide[c, pl.ds(i * PACK, PACK)] = part.reshape(PACK, SUB, LANES)
            turned[c, pl.ds(stride + i * PACK, PACK)] = pltpu.roll(part, HALF, 1).reshape(PACK, SUB, LANES)
        return unused

    lax.fori_loop(0, segment // PACK, load, 0, unroll=True)
    for c in range(4):
        for q in range(stride):
            turned[c, q] = pltpu.roll(turned[c, segment + q], 1, 0)
            turned[c, segment + stride + q] = pltpu.roll(turned[c, stride + q], SUB - 1, 0)

    lane = lax.broadcasted_iota(jnp.int32, (SUB, LANES), 1)
    low = lane < HALF
    initial, final = lane == 0, lane == LANES - 1
    inner_initial, inner_final = lane == HALF, lane == HALF - 1

    def neighbours(c, plane, j):
        spot = [j * stride + tile * planes + plane for tile in range(TRIPLE)]
        v0, v1, v2 = (wide[c, at] for at in spot)
        r0, r1, r2 = (turned[c, at + stride] for at in spot)
        after0 = r0 + turned[c, spot[0] + 2 * stride]
        after1 = r1 + turned[c, spot[1] + 2 * stride]
        before1 = r1 + turned[c, spot[1]]
        before2 = r2 + turned[c, spot[2]]
        across = (
            jnp.where(low, before1, before2),
            jnp.where(low, before2, after0),
            jnp.where(low, after0, after1),
        )
        plus = (
            jnp.where(initial, v1, v0),
            jnp.where(inner_initial, r0, jnp.where(initial, v2, v1)),
            jnp.where(initial, r1, v2),
        )
        minus = (
            jnp.where(final, r1, v0),
            jnp.where(inner_final, r2, jnp.where(final, v0, v1)),
            jnp.where(final, v1, v2),
        )
        sums = []
        for tile in range(TRIPLE):
            total = across[tile] + (pltpu.roll(plus[tile], LANES - 1, 1) + pltpu.roll(minus[tile], 1, 1))
            if plane > 0:
                total = total + wide[c, spot[tile] - 1]
            elif ends is not None:
                total = total + ends[0, c, j * TRIPLE + tile]
            if plane < planes - 1:
                total = total + wide[c, spot[tile] + 1]
            elif ends is not None:
                total = total + ends[1, c, j * TRIPLE + tile]
            sums.append(total)
        return (v0, v1, v2), sums

    def step(j, unused):
        for plane in range(planes):
            (ur, nur), (ui, nui), (dr, ndr), (di, ndi) = (neighbours(c, plane, j) for c in range(4))
            for tile in range(TRIPLE):
                spot = j * stride + tile * planes + plane
                diag_up, bx, by, diag_down = (pot_ref[f, spot] for f in range(4))
                a, b, e, f = ur[tile], ui[tile], dr[tile], di[tile]
                flat[0, spot] = diag_up * a + bx * e + by * f - 0.5 * nur[tile]
                flat[1, spot] = diag_up * b + bx * f - by * e - 0.5 * nui[tile]
                flat[2, spot] = bx * a - by * b + diag_down * e - 0.5 * ndr[tile]
                flat[3, spot] = bx * b + by * a + diag_down * f - 0.5 * ndi[tile]
        return unused

    lax.fori_loop(0, steps, step, 0, unroll=UNROLL)


def store_rows(parts, i, out_ref):
    block = jnp.concatenate([part.astype(jnp.bfloat16) for part in parts], axis=1)
    values = product(spread_matrix(True), block).astype(jnp.bfloat16)
    for c in range(4):
        for s in range(SUB):
            out_ref[0, c, s, pl.ds(i * PACK, PACK), :] = values[s * PACK : (s + 1) * PACK, c * LANES : (c + 1) * LANES]


def apply_body(planes, x_ref, pot_ref, near_ref, far_ref, *refs):
    out_ref, token_ref, wide, turned, ends, flat = refs[-6:]
    near_slot = jnp.where(even_brick(), 1, 0)
    for c in range(4):
        ends[near_slot, c] = near_ref[0, c].astype(jnp.float32).reshape(ends.shape[2:])
        ends[1 - near_slot, c] = far_ref[0, c].astype(jnp.float32).reshape(ends.shape[2:])
    hamiltonian(planes, x_ref, pot_ref, ends, flat, wide, turned)
    for i in range(wide.shape[1] // PACK):
        store_rows([flat[c, pl.ds(i * PACK, PACK)].reshape(PACK * SUB, LANES) for c in range(4)], i, out_ref)


def ahead_body(planes, x_ref, pot_ref, *refs):
    flat_ref, token_ref, wide, turned = refs[-4:]
    hamiltonian(planes, x_ref, pot_ref, None, flat_ref.at[0], wide, turned)


def finish_body(planes, flat_ref, near_ref, far_ref, *refs):
    out_ref, token_ref = refs[-2:]
    even = even_brick()
    per = PACK // planes
    for i in range(flat_ref.shape[2] // PACK):
        outside = pl.ds(i * per * SUB, per * SUB)
        parts = []
        for c in range(4):
            near = near_ref[0, c, outside, :].astype(jnp.float32).reshape(per, SUB, LANES)
            far = far_ref[0, c, outside, :].astype(jnp.float32).reshape(per, SUB, LANES)
            below, above = jnp.where(even, far, near), jnp.where(even, near, far)
            pieces = []
            for q in range(PACK):
                piece = flat_ref[0, c, i * PACK + q]
                if q % planes == 0:
                    piece = piece - 0.5 * below[q // planes]
                if q % planes == planes - 1:
                    piece = piece - 0.5 * above[q // planes]
                pieces.append(piece)
            parts.append(jnp.concatenate(pieces, axis=0))
        store_rows(parts, i, out_ref)


def per_band(body, name, grid, inputs, in_specs, output, out_spec, carry, after, scratch, limit=VMEM_LIMIT):
    anywhere = pl.BlockSpec(memory_space=pl.ANY)
    carried = () if carry is None else (carry,)
    return pl.pallas_call(
        body,
        grid=grid,
        in_specs=in_specs + [anywhere] * (len(carried) + len(after)),
        out_specs=[out_spec, anywhere],
        out_shape=[
            jax.ShapeDtypeStruct(*output),
            jax.ShapeDtypeStruct((SUB, LANES), jnp.float32),
        ],
        input_output_aliases={len(inputs): 0} if carried else {},
        scratch_shapes=scratch,
        compiler_params=pltpu.CompilerParams(vmem_limit_bytes=limit),
        cost_estimate=SMALL,
        name=name,
    )(*inputs, *carried, *after)


def stencil_specs(rows, planes, start):
    segment = rows // SUB
    scratch = [
        pltpu.VMEM((4, segment, SUB, LANES), jnp.float32),
        pltpu.VMEM((4, segment + 2 * planes * TRIPLE, SUB, LANES), jnp.float32),
    ]
    in_specs = [
        pl.BlockSpec((1, 4, rows, LANES), lambda b: (start + b, 0, 0, 0)),
        pl.BlockSpec((4, segment, SUB, LANES), lambda b: (0, 0, 0, 0)),
    ]
    return in_specs, scratch


def apply_bands(x, potential, near, far, planes, start, carry, after):
    count, bands, rows = near.shape[0], x.shape[0], x.shape[2]
    segment, tiles = rows // SUB, rows // planes
    in_specs, scratch = stencil_specs(rows, planes, start)
    halo = pl.BlockSpec((1, 4, tiles, LANES), lambda b: (b, 0, 0, 0))
    scratch += [
        pltpu.VMEM((2, 4, tiles // SUB, SUB, LANES), jnp.float32),
        pltpu.VMEM((4, segment, SUB, LANES), jnp.float32),
    ]
    return per_band(
        functools.partial(apply_body, planes),
        "apply",
        (count,),
        (x, potential, near, far),
        in_specs + [halo, halo],
        ((bands, 4, SUB, segment, LANES), jnp.bfloat16),
        pl.BlockSpec((1, 4, SUB, segment, LANES), lambda b: (start + b, 0, 0, 0, 0)),
        carry,
        after,
        scratch,
    )


def ahead_of(x, potential, planes, start, count, after):
    segment = x.shape[2] // SUB
    in_specs, scratch = stencil_specs(x.shape[2], planes, start)
    return per_band(
        functools.partial(ahead_body, planes),
        "ahead",
        (count,),
        (x, potential),
        in_specs,
        ((count, 4, segment, SUB, LANES), jnp.float32),
        pl.BlockSpec((1, 4, segment, SUB, LANES), lambda b: (b, 0, 0, 0, 0)),
        None,
        after,
        scratch,
    )


def finish(flat, near, far, planes, start, skip, carry):
    count, segment = near.shape[0], flat.shape[2]
    halo = pl.BlockSpec((1, 4, segment // planes * SUB, LANES), lambda b: (b, 0, 0, 0))
    return per_band(
        functools.partial(finish_body, planes),
        "finish",
        (count,),
        (flat, near, far),
        [pl.BlockSpec((1, 4, segment, SUB, LANES), lambda b: (skip + b, 0, 0, 0, 0)), halo, halo],
        (carry.shape, carry.dtype),
        pl.BlockSpec((1, 4, SUB, segment, LANES), lambda b: (start + b, 0, 0, 0, 0)),
        carry,
        (),
        [],
        VMEM_LIMIT - 16 * 1024 * 1024,
    )


def chunk_sizes(bands):
    quarter, small = bands // 4, bands // 8
    return [quarter, bands - 2 * quarter - small, quarter, small] if small else [bands]


def shards(spinors, kpt_mult, occupied, core_density, local_potential):
    bands, planes = spinors.shape[0], spinors.shape[2]
    total = bands * lax.axis_size("ka")
    size = lax.axis_size("brick")
    near_pairs = [(i, i ^ 1) for i in range(size) if i ^ 1 < size]
    far_pairs = [(i, j) for i in range(size) for j in [((i + 1) ^ 1) - 1] if 0 <= j < size]
    x = rows_view(spinors)
    core, local = rows_view(core_density), rows_view(local_potential)
    sizes = chunk_sizes(bands)
    starts = [sum(sizes[:k]) for k in range(len(sizes))]

    swap = lambda face: (lax.ppermute(face[0], "brick", near_pairs), lax.ppermute(face[1], "brick", far_pairs))
    faces = edges(x, planes, [(0, sizes[0])], (), VMEM_LIMIT)
    halos = [swap(faces[0])]
    density, others = front(x, kpt_mult, occupied, total, planes, sizes[1:], faces[0])
    faces += others
    halos += [swap(face) for face in faces[1:2]]
    density = group_sum(*density)
    gated = ()
    if len(sizes) > 2:
        gated = gate(*faces[2], halos[0] + (density[0],))
        halos.append(swap(gated))
    potential = potential_of(*density, core, local, gated)
    out, done = apply_bands(x, potential, *halos[0], planes, 0, None, ())
    if len(sizes) > 2:
        flat, done = ahead_of(x, potential, planes, starts[2], sizes[2] + sizes[3], (done,))
        halos.append(swap(gate(*faces[3], halos[1] + (done,))))
        out, done = apply_bands(x, potential, *halos[1], planes, starts[1], out, (done,))
        for k in (2, 3):
            out, done = finish(flat, *halos[k], planes, starts[k], starts[k] - starts[2], out)
    return planes_view(out.reshape(x.shape), planes)


def solution(mesh):
    placed = (P("ka", None, "brick", None), P("ka"), P("ka"), P("brick", None), P("brick", None))
    return jax.shard_map(
        shards, mesh=mesh, in_specs=placed, out_specs=P("ka", None, "brick", None), check_vma=False
    )
```
